32 devices in a mesh: dp: 4 (over x, core), seq: 8 (over z, y).
Axes of the slice: x: 2, y: 2, z: 4, core: 2. Of those that a mesh axis runs over, the one named last changes fastest.
Arguments:
- embeddings: bfloat16 [4, 8, 512, 8192], P('dp', 'seq'), may hold values from -6 to 6
- layout: int32 [4, 8, 8], P('dp'), may hold values from 0 to 7, as said below
- lengths: int32 [4], P('dp'), may hold values from 1024 to 4096, as said below
- targets: int32 [4, 1024, 2048], P('dp', 'seq'), may hold values from 0 to 7
- projection: bfloat16 [8192, 768], P('dp'), may hold values from -0.0625 to 0.0625
- kernels: bfloat16 [2, 3, 768, 384], replicated, may hold values from -0.125 to 0.125
- mixers: bfloat16 [2, 384, 768], replicated, may hold values from -0.3125 to 0.3125
- readout: bfloat16 [768, 2048], replicated, may hold values from -0.21875 to 0.21875
Outputs:
- kernel_grads: float32 [2, 3, 768, 384], P(None, None, 'seq', 'dp')
- mixer_grads: float32 [2, 384, 768], P(None, 'seq', 'dp')
- readout_grad: float32 [768, 2048], P('seq', 'dp')
- trunk_grad: float32 [4, 2048, 768], P('dp', 'seq')
The draws below stay inside these ranges and needn't reach their ends.
Inputs may be any that keep to these rules, and one draw needn't show every extreme that they name: For every window w and shard j, layout[w, s, j] over all shards s lists every block number once. `lengths`: multiples of 128; in every draw one window has the full 4096 and another the least.
All inputs are finite; a program needn't handle non-finite values.
Results may differ from the reference program's by a relative error of at most 0.017.
Values may be sent and summed in bfloat16 or wider, within the bound.
No kernel may reach another device: no remote copies, remote signals or barrier semaphores. Data moves between devices by JAX's collectives and lax.ppermute only.
A program may use at most 128 MiB of HBM per device.

```python
import math
import jax
import jax.numpy as jnp
from jax import lax

EMB = 8192
CH = 768
INNER = 384
TRACKS = 2048
ROWS_DEV = 512
WINDOWS = 4
POSITIONS = 4096
BINS = 1024
BLOCK = 64
SPREAD_FINE = 256
SPREAD_COARSE = 128
N_SEQ = 8


def draw_layout(key, part):
    keys = jax.random.split(key, WINDOWS * N_SEQ)
    orders = jax.vmap(lambda single: jax.random.permutation(single, N_SEQ))(keys)
    orders = orders.reshape(WINDOWS, N_SEQ, N_SEQ)
    return jnp.transpose(orders, (0, 2, 1)).astype(jnp.int32)


def draw_lengths(key, part):
    first_key, second_key = jax.random.split(key)
    blocks = jax.random.randint(first_key, (WINDOWS,), POSITIONS // 512, POSITIONS // 128 + 1)
    chosen = jax.random.randint(second_key, (), 0, WINDOWS)
    windows_index = jnp.arange(WINDOWS)
    blocks = jnp.where(windows_index == chosen, POSITIONS // 128, blocks)
    blocks = jnp.where(windows_index == (chosen + 1) % WINDOWS, POSITIONS // 512, blocks)
    return (blocks * 128).astype(jnp.int32)


def set_ends(entries, own_key, least, largest):
    dims = entries.shape
    place = [jax.random.randint(jax.random.fold_in(own_key, axis), (), 0, dims[axis]) for axis in range(len(dims))]
    entries = entries.at[tuple(place)].set(least)
    longest = dims.index(max(dims))
    place[longest] = (place[longest] + 1) % dims[longest]
    return entries.at[tuple(place)].set(largest)


def shard_levels(own_key, shape, cuts, least, top_value):
    level = 1.0
    for axis_at, shards_of in cuts:
        draws = jax.random.uniform(jax.random.fold_in(jax.random.fold_in(own_key, 6), axis_at), (shards_of,), jnp.float32, least / len(cuts), top_value / len(cuts))
        level = level * jnp.repeat(jnp.exp(draws), shape[axis_at] // shards_of).reshape((-1,) + (1,) * (len(shape) - 1 - axis_at))
    return level


def gaussian(stream_key, extent, scale, reach, cuts=(), kind=jnp.bfloat16):
    level = shard_levels(stream_key, extent, cuts, -0.22, 0.18) if cuts else 1.0
    drawn = jax.random.normal(stream_key, extent, jnp.float32) * scale * level
    return jnp.minimum(jnp.maximum(drawn, -reach), reach).astype(kind)


def setup_inputs(seed: int = 0) -> dict:
    splits = jax.random.split(jax.random.key(seed), 9)
    return {
        "embeddings": gaussian(splits[0], (WINDOWS, N_SEQ, ROWS_DEV, EMB), 1.0, 6.0, ((0, 4), (1, 8))),
        "layout": draw_layout(jax.random.fold_in(splits[8], 71), 0),
        "lengths": draw_lengths(jax.random.fold_in(splits[8], 71), 0),
        "targets": set_ends(jax.random.randint(splits[3], (WINDOWS, BINS, TRACKS), 0, 8), jax.random.fold_in(splits[3], 1), 0, 7).astype(jnp.int32),
        "projection": gaussian(splits[4], (EMB, CH), EMB ** -0.5, 0.0625, ((0, 4),)),
        "kernels": gaussian(splits[5], (2, 3, CH, INNER), (3 * CH) ** -0.5, 0.125),
        "mixers": gaussian(splits[6], (2, INNER, CH), INNER ** -0.5, 0.3125),
        "readout": gaussian(splits[7], (CH, TRACKS), CH ** -0.5, 0.21875),
    }


def gelu_exact(values):
    return 0.5 * values * (1.0 + lax.erf(values * (1.0 / math.sqrt(2.0))))

def gelu_slope(values):
    cumulative = 0.5 * (1.0 + lax.erf(values * (1.0 / math.sqrt(2.0))))
    density = jnp.exp(-0.5 * values * values) * (1.0 / math.sqrt(2.0 * math.pi))
    return cumulative + values * density

def matmul(left_side, right_side):
    return jnp.dot(left_side, right_side, preferred_element_type=jnp.float32)

def times_transposed(left_side, right_side):
    return lax.dot_general(left_side, right_side, (((1,), (1,)), ((), ())), preferred_element_type=jnp.float32)

def transposed_times(left_side, right_side):
    return lax.dot_general(left_side, right_side, (((0,), (0,)), ((), ())), preferred_element_type=jnp.float32)

def padded_taps(values, spread):
    row_count = values.shape[0]
    padded = jnp.pad(values, ((spread, spread), (0, 0)))
    return (padded[0:row_count], padded[spread:spread + row_count], padded[2 * spread:2 * spread + row_count])

def block_rest(hidden, shifted, kernel, mixing):
    inner_sum = matmul(shifted[0], kernel[0]) + matmul(shifted[1], kernel[1]) + matmul(shifted[2], kernel[2])
    gated_out = gelu_exact(inner_sum).astype(jnp.bfloat16)
    output = hidden.astype(jnp.float32) + matmul(gated_out, mixing)
    pooled = (output.reshape(-1, 2, output.shape[1]).sum(axis=1) * 0.5).astype(jnp.bfloat16)
    return (pooled, inner_sum, gated_out)

def block_backward(upstream, shifted, inner_sum, gated_out, kernel, mixing):
    mixing_grad = transposed_times(gated_out, upstream)
    inner_grad = (times_transposed(upstream, mixing) * gelu_slope(inner_sum)).astype(jnp.bfloat16)
    kernel_grad = jnp.stack([transposed_times(shifted[tap_index], inner_grad) for tap_index in range(3)])
    return (kernel_grad, mixing_grad, inner_grad)

def window_gradients(window_rows, window_layout, window_length, window_targets, projection, kernels, mixers, readout):
    row_ids = jnp.arange(ROWS_DEV, dtype=jnp.int32)
    owner_shard = row_ids // BLOCK
    slot_ids = jnp.take(window_layout, owner_shard, axis=1)
    position = owner_shard[None, :] * ROWS_DEV + slot_ids * BLOCK + (row_ids % BLOCK)[None, :]
    position = position.reshape(N_SEQ * ROWS_DEV).astype(jnp.int32)
    inside = (position < window_length).astype(jnp.float32)
    projected = (matmul(window_rows.reshape(N_SEQ * ROWS_DEV, EMB), projection) * inside[:, None]).astype(jnp.bfloat16)
    hidden = jnp.zeros((POSITIONS, CH), jnp.bfloat16).at[position].set(projected)
    fine_active = gelu_exact(hidden.astype(jnp.float32)).astype(jnp.bfloat16)
    fine_shifted = padded_taps(fine_active, SPREAD_FINE)
    first_pooled, fine_inner, fine_gated = block_rest(hidden, fine_shifted, kernels[0], mixers[0])
    coarse_active = gelu_exact(first_pooled.astype(jnp.float32)).astype(jnp.bfloat16)
    coarse_shifted = padded_taps(coarse_active, SPREAD_COARSE)
    second, coarse_inner, coarse_gated = block_rest(first_pooled, coarse_shifted, kernels[1], mixers[1])
    logits = matmul(second, readout)
    bin_ids = jnp.arange(BINS, dtype=jnp.int32)
    valid_bins = (bin_ids * 4 < window_length).astype(jnp.float32)
    loss_scale = 2.0 / math.sqrt(WINDOWS * BINS)
    target_values = window_targets.astype(jnp.float32)
    logit_grad = (loss_scale * valid_bins[:, None] * (jax.nn.softplus(logits) - target_values) * jax.nn.sigmoid(logits)).astype(jnp.bfloat16)
    readout_grad = transposed_times(second, logit_grad)
    upper_grad = (times_transposed(logit_grad, readout) * 0.5).astype(jnp.bfloat16)
    upper_rows = jnp.repeat(upper_grad, 2, axis=0)
    coarse_kernel, coarse_mixing, coarse_grad = block_backward(upper_rows, coarse_shifted, coarse_inner, coarse_gated, kernels[1], mixers[1])
    half_count = coarse_grad.shape[0]
    grad_wide = jnp.pad(coarse_grad, ((SPREAD_COARSE, SPREAD_COARSE), (0, 0)))
    input_grad = times_transposed(grad_wide[2 * SPREAD_COARSE:2 * SPREAD_COARSE + half_count], kernels[1][0]) + times_transposed(coarse_grad, kernels[1][1]) + times_transposed(grad_wide[0:half_count], kernels[1][2])
    first_grad = upper_rows.astype(jnp.float32) + input_grad * gelu_slope(first_pooled.astype(jnp.float32))
    trunk_grad = first_grad * (math.sqrt(WINDOWS * BINS) * 0.5)
    lower_grad = (first_grad * 0.5).astype(jnp.bfloat16)
    lower_rows = jnp.repeat(lower_grad, 2, axis=0)
    fine_kernel, fine_mixing, fine_grad = block_backward(lower_rows, fine_shifted, fine_inner, fine_gated, kernels[0], mixers[0])
    return (jnp.stack([fine_kernel, coarse_kernel]), jnp.stack([fine_mixing, coarse_mixing]), readout_grad, trunk_grad)

def reference(embeddings, layout, lengths, targets, projection, kernels, mixers, readout):

    def one_window(inputs):
        return window_gradients(inputs[0], inputs[1], inputs[2], inputs[3], projection, kernels, mixers, readout)
    stacked = lax.map(one_window, (embeddings, layout, lengths, targets))
    return (lax.optimization_barrier(jnp.sum(stacked[0], axis=0)), lax.optimization_barrier(jnp.sum(stacked[1], axis=0)), lax.optimization_barrier(jnp.sum(stacked[2], axis=0)), stacked[3])
```

```python
import math

import jax
import jax.numpy as jnp
import ml_dtypes
import numpy as np
from jax import lax
from jax.experimental import pallas as pl
from jax.experimental.pallas import tpu as pltpu
from jax.sharding import PartitionSpec as P

SPREAD_FINE = 256
SPREAD_COARSE = 128
BF = jnp.bfloat16
F32 = jnp.float32
PIECES = 2

VMEM = pl.BlockSpec(memory_space=pltpu.VMEM)
SMEM = pl.BlockSpec(memory_space=pltpu.SMEM)


def params(mib):
    return pltpu.CompilerParams(vmem_limit_bytes=mib * 1024 * 1024)


def cost(flops, arrays):
    total = sum(int(np.prod(a.shape)) * a.dtype.itemsize for a in arrays)
    return pl.CostEstimate(flops=int(flops), bytes_accessed=int(total), transcendentals=0)


def gelu(v):
    return 0.5 * v * (1.0 + lax.erf(v * (1.0 / math.sqrt(2.0))))


def gelu_slope(v):
    cumulative = 0.5 * (1.0 + lax.erf(v * (1.0 / math.sqrt(2.0))))
    density = jnp.exp(-0.5 * v * v) * (1.0 / math.sqrt(2.0 * math.pi))
    return cumulative + v * density


def nn(a, b):
    return jnp.dot(a, b, preferred_element_type=F32)


def nt(a, b):
    return lax.dot_general(a, b, (((1,), (1,)), ((), ())), preferred_element_type=F32)


def tn(a, b):
    return lax.dot_general(a, b, (((0,), (0,)), ((), ())), preferred_element_type=F32)


def call(body, inputs, outs, flops, mib, smem=0, scratch=()):
    outs = [jax.ShapeDtypeStruct(s, d) for s, d in outs]
    return pl.pallas_call(
        body,
        out_shape=outs,
        in_specs=[SMEM] * smem + [VMEM] * (len(inputs) - smem),
        out_specs=[VMEM] * len(outs),
        scratch_shapes=list(scratch),
        compiler_params=params(mib),
        cost_estimate=cost(flops, list(inputs) + outs),
    )(*inputs)


def project(total, rows, weights, starts, final):
    count = len(weights)
    row_count = rows.shape[0]
    depth, channels = weights[0].shape
    block = min(512, depth)
    steps = depth // block

    def body(starts_ref, *refs):
        row_refs, weight_refs = refs[:count], refs[count : 2 * count]
        rest = refs[2 * count :]
        step = pl.program_id(0)
        part = nn(row_refs[0][...], weight_refs[0][...])
        for r, w in zip(row_refs[1:], weight_refs[1:]):
            part = part + nn(r[...], w[...])
        if total is None:
            out_ref = rest[0]

            @pl.when(step == 0)
            def _():
                out_ref[...] = part

            @pl.when(step > 0)
            def _():
                out_ref[...] += part
        else:
            old_ref, out_ref = rest
            if steps == 1:
                out_ref[...] = (old_ref[...] + part).astype(out_ref.dtype)
            else:

                @pl.when(step == 0)
                def _():
                    out_ref[...] = old_ref[...] + part

                @pl.when(step > 0)
                def _():
                    out_ref[...] += part

    def row_map(k):
        return lambda i, s: (0, s[k] + i)

    whole = pl.BlockSpec((row_count, channels), lambda i, s: (0, 0))
    in_specs = [pl.BlockSpec((row_count, block), row_map(k)) for k in range(count)]
    in_specs += [pl.BlockSpec((block, channels), lambda i, s: (i, 0)) for _ in range(count)]
    inputs = [rows] * count + list(weights)
    if total is not None:
        in_specs.append(whole)
        inputs.append(total)
    out = jax.ShapeDtypeStruct((row_count, channels), BF if final else F32)
    return pl.pallas_call(
        body,
        out_shape=out,
        grid_spec=pltpu.PrefetchScalarGridSpec(
            num_scalar_prefetch=1, grid=(steps,), in_specs=in_specs, out_specs=whole
        ),
        compiler_params=params(24),
        cost_estimate=cost(2 * row_count * depth * channels * count, list(weights) * 2 + [out]),
    )(jnp.stack(starts).astype(jnp.int32) // block, *inputs)


def place_body(target_ref, received_ref, hidden_ref, low_ref, high_ref):
    half = low_ref.shape[0]
    rows = received_ref[...]
    for h, out in enumerate((low_ref, high_ref)):
        order = lax.broadcasted_iota(jnp.int32, (half, rows.shape[0]), 0) + h * half
        pick = jnp.where(order == target_ref[...], 1.0, 0.0).astype(BF)
        placed = nn(pick, rows)
        hidden_ref[h * half : (h + 1) * half] = placed.astype(BF)
        out[...] = gelu(placed).astype(BF)


def fine_body(
    prev_ref, low_ref, high_ref, next_ref, hidden_ref, kernel_ref, mixer_ref,
    inner_ref, gated_ref, first_ref, alow_ref, ahigh_ref,
):
    half = low_ref.shape[0]
    slab = half // 4
    taps = (prev_ref, low_ref, high_ref, next_ref)
    for h, active in enumerate((alow_ref, ahigh_ref)):
        inner = (
            nn(taps[h + 1][...], kernel_ref[1])
            + nn(taps[h][...], kernel_ref[0])
            + nn(taps[h + 2][...], kernel_ref[2])
        )
        inner_ref[h * half : (h + 1) * half] = inner
        gated = gelu(inner).astype(BF)
        gated_ref[h * half : (h + 1) * half] = gated
        out = hidden_ref[h * half : (h + 1) * half].astype(F32) + nn(gated, mixer_ref[...])
        for s in range(2):
            a = out[2 * s * slab : (2 * s + 1) * slab]
            b = out[(2 * s + 1) * slab : (2 * s + 2) * slab]
            pooled = ((a + b) * 0.5).astype(BF)
            start = h * half // 2 + s * slab
            first_ref[start : start + slab] = pooled
            active[s * slab : (s + 1) * slab] = gelu(pooled.astype(F32)).astype(BF)


def coarse_body(
    scale, bins_per,
    ids_ref, prev_ref, low_ref, high_ref, next_ref, first_ref, kernel_ref, mixer_ref, readout_ref, targets_ref,
    gated_ref, second_ref, logit_ref, upper_ref, glow_ref, ghigh_ref,
):
    half = low_ref.shape[0]
    slab = half // 2
    taps = (prev_ref, low_ref, high_ref, next_ref)
    slopes = []
    for h in range(2):
        inner = (
            nn(taps[h + 1][...], kernel_ref[1])
            + nn(taps[h][...], kernel_ref[0])
            + nn(taps[h + 2][...], kernel_ref[2])
        )
        slopes.append(gelu_slope(inner))
        gated = gelu(inner).astype(BF)
        gated_ref[h * half : (h + 1) * half] = gated
        out = first_ref[h * half : (h + 1) * half].astype(F32) + nn(gated, mixer_ref[...])
        second_ref[h * slab : (h + 1) * slab] = ((out[:slab] + out[slab:]) * 0.5).astype(BF)
    bins = second_ref.shape[0]
    tracks = readout_ref.shape[1]
    width = min(512, tracks)
    bin_ids = ids_ref[0] * bins_per + lax.broadcasted_iota(jnp.int32, (bins, 1), 0)
    weight = jnp.where(bin_ids * 4 < ids_ref[1], scale, 0.0).astype(F32)
    second = second_ref[...]
    upper = jnp.zeros((bins, second.shape[1]), F32)
    for n in range(tracks // width):
        cols = slice(n * width, (n + 1) * width)
        readout = readout_ref[:, cols]
        logits = nn(second, readout)
        small = jnp.exp(-jnp.abs(logits))
        plus = jnp.maximum(logits, 0.0) + jnp.log1p(small)
        gate = jnp.where(logits >= 0.0, 1.0, small) / (1.0 + small)
        grad = (weight * (plus - targets_ref[:, cols].astype(F32)) * gate).astype(BF)
        logit_ref[:, cols] = grad
        upper = upper + nt(grad, readout)
    upper = (upper * 0.5).astype(BF)
    upper_ref[...] = upper
    back = nt(upper, mixer_ref[...])
    for h, out in enumerate((glow_ref, ghigh_ref)):
        piece = back[h * slab : (h + 1) * slab]
        for s in range(2):
            out[s * slab : (s + 1) * slab] = (piece * slopes[h][s * slab : (s + 1) * slab]).astype(BF)


def readout_body(ids_ref, second_ref, logit_ref, keep_ref, send_ref):
    width = keep_ref.shape[2]
    second = second_ref[...]
    for k in range(4):
        start = pl.multiple_of((ids_ref[0] ^ k) * width, width)
        out = send_ref if k & 1 else keep_ref
        out[k >> 1] = tn(second, logit_ref[:, pl.ds(start, width)]).astype(BF)


def store_blocks(ids_ref, pieces, keep_ref, send_ref):
    width = pieces[0].shape[1] // 4
    for d in range(4):
        block = jnp.concatenate([p[:, d * width : (d + 1) * width] for p in pieces], axis=1)
        far = (ids_ref[0] >> 1) ^ (d >> 1)

        @pl.when((ids_ref[0] & 1) == (d & 1))
        def _(block=block, far=far):
            keep_ref[far] = block

        @pl.when((ids_ref[0] & 1) != (d & 1))
        def _(block=block, far=far):
            send_ref[far] = block


def weight_pieces(taps, grads, gated, upstream, spread_ref, split_ref):
    pieces = []
    for t in range(3):
        pieces.append((tn(taps[t][...], grads[0]) + tn(taps[t + 1][...], grads[1])).astype(BF))
    mixed = 0.0
    for j in range(2):
        left = nn(gated, spread_ref[j]).astype(BF)
        right = nn(upstream, split_ref[j]).astype(BF)
        mixed = mixed + tn(left, right)
    pieces.append(mixed.astype(BF))
    return pieces


def coarse_grad_body(
    ids_ref, prev_ref, low_ref, high_ref, next_ref, glow_ref, ghigh_ref, gated_ref, upper_ref, spread_ref, split_ref,
    keep_ref, send_ref,
):
    slab = low_ref.shape[0] // 2
    upper = upper_ref[...]
    rows = jnp.concatenate([upper[:slab], upper[:slab], upper[slab:], upper[slab:]], axis=0)
    pieces = weight_pieces(
        (prev_ref, low_ref, high_ref, next_ref), (glow_ref[...], ghigh_ref[...]), gated_ref[...], rows,
        spread_ref, split_ref,
    )
    store_blocks(ids_ref, pieces, keep_ref, send_ref)


def fine_grad_body(
    scale,
    ids_ref, gprev_ref, glow_ref, ghigh_ref, gnext_ref, upper_ref, first_ref, kernel_ref, mixer_ref,
    prev_ref, low_ref, high_ref, next_ref, inner_ref, gated_ref, spread_ref, split_ref,
    trunk_ref, keep_ref, send_ref, lanes_ref,
):
    half = glow_ref.shape[0]
    slab = half // 2
    grads = (gprev_ref, glow_ref, ghigh_ref, gnext_ref)
    upper = upper_ref[...].astype(F32)
    inner_grads, rows = [], []
    for h in range(2):
        back = (
            nt(grads[h + 2][...], kernel_ref[0])
            + nt(grads[h + 1][...], kernel_ref[1])
            + nt(grads[h][...], kernel_ref[2])
        )
        slope = gelu_slope(first_ref[h * half : (h + 1) * half].astype(F32))
        base = upper[h * slab : (h + 1) * slab]
        total = jnp.concatenate([base, base], axis=0) + back * slope
        for t in range(lanes_ref.shape[0]):
            cols = slice(t * 128, (t + 1) * 128)
            for s in range(2):
                lanes_ref[t, pl.ds(s, slab, stride=2), :] = total[s * slab : (s + 1) * slab, cols] * scale
            trunk_ref[h * half : (h + 1) * half, cols] = lanes_ref[t]
        lower = (total * 0.5).astype(BF)
        inner = nt(lower, mixer_ref[...])
        spread_inner = jnp.concatenate([inner[:slab], inner[:slab], inner[slab:], inner[slab:]], axis=0)
        slope = gelu_slope(inner_ref[2 * h * half : 2 * (h + 1) * half])
        inner_grads.append((spread_inner * slope).astype(BF))
        rows += [lower[:slab], lower[:slab], lower[slab:], lower[slab:]]
    pieces = weight_pieces(
        (prev_ref, low_ref, high_ref, next_ref), inner_grads, gated_ref[...], jnp.concatenate(rows, axis=0),
        spread_ref, split_ref,
    )
    store_blocks(ids_ref, pieces, keep_ref, send_ref)


def swap(value, axis, bit):
    size = lax.axis_size(axis)
    return lax.ppermute(value, axis, [(i, i ^ bit) for i in range(size)])


def halo(low, high):
    size = lax.axis_size("seq")
    up = [(i, i + 1) for i in range(size - 1)]
    return (
        lax.ppermute(high, "seq", up),
        lax.ppermute(low, "seq", [(j, i) for i, j in up]),
    )


def scatter_sum(keep, send):
    came = swap(send, "dp", 1)
    away = (keep[1].astype(F32) + came[1].astype(F32)).astype(BF)
    here = keep[0].astype(F32) + came[0].astype(F32)
    total = (here + swap(away, "dp", 2).astype(F32)).astype(BF)
    groups = lax.axis_size("seq")
    rows, columns = total.shape
    parts = lax.all_to_all(
        total.reshape(groups, rows // groups, columns), "seq", split_axis=0, concat_axis=0, tiled=True
    )
    return parts.astype(F32).sum(axis=0)


def shards(embeddings, layout, lengths, targets, projection, kernels, mixers, readout):
    groups = lax.axis_size("seq")
    windows = lax.axis_size("dp")
    me = lax.axis_index("dp")
    device = lax.axis_index("seq")
    rows = embeddings[0, 0]
    row_count = rows.shape[0]
    depth, channels = projection.shape
    width = kernels.shape[3]
    tracks = readout.shape[1]
    half, quarter, eighth = row_count // 2, row_count // 4, row_count // 8
    length = lengths[0]

    side = device % 2
    share = depth // 2
    piece = share // PIECES
    from_core = swap(projection, "dp", 1)
    mine = lax.dynamic_slice_in_dim(projection, side * share, share, axis=0)
    far = [swap(lax.slice_in_dim(mine, i * piece, (i + 1) * piece), "dp", 2) for i in range(PIECES)]
    far_side = [swap(f, "seq", 1) for f in far]
    far_core = [swap(f, "dp", 1) for f in far]
    far_side_core = [swap(f, "dp", 1) for f in far_side]
    total = project(None, rows, [projection], [me * depth], False)
    total = project(total, rows, [from_core], [(me ^ 1) * depth], False)
    for i in range(PIECES):
        at = side * share + i * piece
        total = project(
            total, rows, [far[i], far_core[i]], [(me ^ 2) * depth + at, (me ^ 3) * depth + at], False
        )
    for i in range(PIECES):
        at = (1 - side) * share + i * piece
        total = project(
            total, rows, [far_side[i], far_side_core[i]],
            [(me ^ 2) * depth + at, (me ^ 3) * depth + at], i == PIECES - 1,
        )

    block = row_count // groups
    received = lax.all_to_all(
        total.reshape(groups, block, channels), "seq", split_axis=0, concat_axis=0, tiled=True
    ).reshape(row_count, channels)
    column = lax.dynamic_index_in_dim(layout[0], device, axis=1, keepdims=True)
    position = column * block + jnp.arange(block, dtype=jnp.int32)[None, :]
    slot = (position // half) * half + (position % 4) * eighth + (position % half) // 4
    target = jnp.where(device * row_count + position < length, slot, -1).reshape(1, row_count)

    hidden, low, high = call(
        place_body, (target, received),
        [((row_count, channels), BF), ((half, channels), BF), ((half, channels), BF)],
        2 * row_count * row_count * channels, 24,
    )
    prev, nxt = halo(low, high)
    inner, gated, first, alow, ahigh = call(
        fine_body, (prev, low, high, nxt, hidden, kernels[0], mixers[0]),
        [((row_count, width), F32), ((row_count, width), BF), ((half, channels), BF),
         ((quarter, channels), BF), ((quarter, channels), BF)],
        8 * row_count * width * channels, 24,
    )
    aprev, anext = halo(alow, ahigh)
    bins = quarter
    loss = 2.0 / math.sqrt(windows * groups * bins)
    ids = jnp.stack([device, length]).astype(jnp.int32)
    place = jnp.stack([me, device]).astype(jnp.int32)

    def coarse(*refs):
        coarse_body(loss, bins, *refs)

    cgated, second, logit_grad, upper, glow, ghigh = call(
        coarse, (ids, aprev, alow, ahigh, anext, first, kernels[1], mixers[1], readout, targets[0]),
        [((half, width), BF), ((bins, channels), BF), ((bins, tracks), BF), ((bins, channels), BF),
         ((quarter, width), BF), ((quarter, width), BF)],
        8 * half * width * channels + 4 * bins * tracks * channels, 32, smem=1,
    )
    gprev, gnext = halo(glow, ghigh)
    track_keep, track_send = call(
        readout_body, (place, second, logit_grad), [((2, channels, tracks // 4), BF)] * 2,
        2 * bins * tracks * channels, 24, smem=1,
    )
    readout_total = scatter_sum(track_keep, track_send)

    per = width // groups
    fold = np.zeros((2, width, channels), ml_dtypes.bfloat16)
    split = np.zeros((2, channels, width), ml_dtypes.bfloat16)
    for j in range(2):
        for a in range(width):
            fold[j, a, (a // per) * 2 * per + j * per + a % per] = 1
        piece_width = width // 4
        for b in range(width):
            split[j, (b // piece_width) * 2 * piece_width + j * piece_width + b % piece_width, b] = 1
    fold, split = jnp.asarray(fold), jnp.asarray(split)
    pair = [((2, channels, width), BF)] * 2
    coarse_keep, coarse_send = call(
        coarse_grad_body, (place, aprev, alow, ahigh, anext, glow, ghigh, cgated, upper, fold, split), pair,
        12 * half * width * channels, 32, smem=1,
    )
    coarse_total = scatter_sum(coarse_keep, coarse_send)

    def fine(*refs):
        fine_grad_body(math.sqrt(windows * groups * bins) * 0.5, *refs)

    trunk, fine_keep, fine_send = call(
        fine,
        (place, gprev, glow, ghigh, gnext, upper, first, kernels[1], mixers[0],
         prev, low, high, nxt, inner, gated, fold, split),
        [((half, channels), F32)] + pair,
        20 * row_count * width * channels, 40, smem=1,
        scratch=[pltpu.VMEM((channels // 128, quarter, 128), F32)],
    )
    fine_total = scatter_sum(fine_keep, fine_send)

    cut = width // windows
    kernel_rows, mixer_rows = [], []
    for value in (fine_total, coarse_total):
        kernel_rows.append(jnp.stack([value[:, t * cut : (t + 1) * cut] for t in range(3)]))
        tail = value[:, 3 * cut :]
        mixer_rows.append(jnp.concatenate([tail[:per], tail[per:]], axis=1))
    return (jnp.stack(kernel_rows), jnp.stack(mixer_rows), readout_total, trunk[None])


def solution(mesh):
    placed = (
        P("dp", "seq", None, None),
        P("dp", None, None),
        P("dp"),
        P("dp", "seq", None),
        P("dp", None),
        P(),
        P(),
        P(),
    )
    return jax.shard_map(
        shards,
        mesh=mesh,
        in_specs=placed,
        out_specs=(
            P(None, None, "seq", "dp"),
            P(None, "seq", "dp"),
            P("seq", "dp"),
            P("dp", "seq", None),
        ),
        check_vma=False,
    )
```

```python
import math

import jax
import jax.numpy as jnp
import ml_dtypes
import numpy as np
from jax import lax
from jax.experimental import pallas as pl
from jax.experimental.pallas import tpu as pltpu
from jax.sharding import PartitionSpec as P

SPREAD_FINE = 256
SPREAD_COARSE = 128
BF = jnp.bfloat16
F32 = jnp.float32
PIECES = 4

VMEM = pl.BlockSpec(memory_space=pltpu.VMEM)
SMEM = pl.BlockSpec(memory_space=pltpu.SMEM)
ANY = pl.BlockSpec(memory_space=pl.ANY)


def params(mib):
    return pltpu.CompilerParams(vmem_limit_bytes=mib * 1024 * 1024)


def cost(flops, arrays):
    total = sum(int(np.prod(a.shape)) * a.dtype.itemsize for a in arrays)
    return pl.CostEstimate(flops=int(flops), bytes_accessed=int(total), transcendentals=0)


def gelu(v):
    return 0.5 * v * (1.0 + lax.erf(v * (1.0 / math.sqrt(2.0))))


def gelu_slope(v):
    cumulative = 0.5 * (1.0 + lax.erf(v * (1.0 / math.sqrt(2.0))))
    density = jnp.exp(-0.5 * v * v) * (1.0 / math.sqrt(2.0 * math.pi))
    return cumulative + v * density


def nn(a, b):
    return jnp.dot(a, b, preferred_element_type=F32)


def nt(a, b):
    return lax.dot_general(a, b, (((1,), (1,)), ((), ())), preferred_element_type=F32)


def tn(a, b):
    return lax.dot_general(a, b, (((0,), (0,)), ((), ())), preferred_element_type=F32)


def call(body, inputs, outs, flops, mib, smem=0, scratch=(), after=0):
    outs = [jax.ShapeDtypeStruct(s, d) for s, d in outs]
    return pl.pallas_call(
        body,
        out_shape=outs,
        in_specs=[SMEM] * smem + [ANY] * after + [VMEM] * (len(inputs) - smem - after),
        out_specs=[VMEM] * len(outs),
        scratch_shapes=list(scratch),
        compiler_params=params(mib),
        cost_estimate=cost(flops, list(inputs) + outs),
    )(*inputs)


def project(total, rows, weights, starts, final):
    count = len(weights)
    row_count = rows.shape[0]
    depth, channels = weights[0].shape
    block = min(512, depth)
    steps = depth // block

    def body(starts_ref, *refs):
        row_refs, weight_refs = refs[:count], refs[count : 2 * count]
        rest = refs[2 * count :]
        step = pl.program_id(0)
        part = nn(row_refs[0][...], weight_refs[0][...])
        for r, w in zip(row_refs[1:], weight_refs[1:]):
            part = part + nn(r[...], w[...])
        if total is None:
            out_ref = rest[0]

            @pl.when(step == 0)
            def _():
                out_ref[...] = part

            @pl.when(step > 0)
            def _():
                out_ref[...] += part
        else:
            old_ref, out_ref = rest
            if steps == 1:
                out_ref[...] = (old_ref[...] + part).astype(out_ref.dtype)
            else:

                @pl.when(step == 0)
                def _():
                    out_ref[...] = old_ref[...] + part

                @pl.when(step > 0)
                def _():
                    out_ref[...] += part

    def row_map(k):
        return lambda i, s: (0, s[k] + i)

    whole = pl.BlockSpec((row_count, channels), lambda i, s: (0, 0))
    in_specs = [pl.BlockSpec((row_count, block), row_map(k)) for k in range(count)]
    in_specs += [pl.BlockSpec((block, channels), lambda i, s: (i, 0)) for _ in range(count)]
    inputs = [rows] * count + list(weights)
    if total is not None:
        in_specs.append(whole)
        inputs.append(total)
    out = jax.ShapeDtypeStruct((row_count, channels), BF if final else F32)
    return pl.pallas_call(
        body,
        out_shape=out,
        grid_spec=pltpu.PrefetchScalarGridSpec(
            num_scalar_prefetch=1, grid=(steps,), in_specs=in_specs, out_specs=whole
        ),
        compiler_params=params(56),
        cost_estimate=cost(2 * row_count * depth * channels * count, list(weights) * 2 + [out]),
    )(jnp.stack(starts).astype(jnp.int32) // block, *inputs)


def place_body(target_ref, received_ref, kernels_ref, hidden_ref, low_ref, high_ref, down_ref, up_ref):
    half = low_ref.shape[0]
    rows = received_ref[...]
    for h, out in enumerate((low_ref, high_ref)):
        order = lax.broadcasted_iota(jnp.int32, (half, rows.shape[0]), 0) + h * half
        pick = jnp.where(order == target_ref[...], 1.0, 0.0).astype(BF)
        placed = nn(pick, rows)
        hidden_ref[h * half : (h + 1) * half] = placed.astype(BF)
        out[...] = gelu(placed).astype(BF)
    down_ref[...] = nn(low_ref[...], kernels_ref[0, 2]).astype(BF)
    up_ref[...] = nn(high_ref[...], kernels_ref[0, 0]).astype(BF)


def local_body(low_ref, high_ref, kernels_ref, inner_ref):
    half = low_ref.shape[0]
    low, high = low_ref[...], high_ref[...]
    inner_ref[:half] = nn(low, kernels_ref[0, 1]) + nn(high, kernels_ref[0, 2])
    inner_ref[half:] = nn(low, kernels_ref[0, 0]) + nn(high, kernels_ref[0, 1])


def fine_body(
    prev_ref, next_ref, local_ref, hidden_ref, kernels_ref, mixers_ref,
    inner_ref, gated_ref, first_ref, alow_ref, ahigh_ref, down_ref, up_ref,
):
    half = prev_ref.shape[0]
    slab = half // 4
    for h, (came, active) in enumerate(((prev_ref, alow_ref), (next_ref, ahigh_ref))):
        inner = local_ref[h * half : (h + 1) * half] + came[...].astype(F32)
        inner_ref[h * half : (h + 1) * half] = inner
        gated = gelu(inner).astype(BF)
        gated_ref[h * half : (h + 1) * half] = gated
        out = hidden_ref[h * half : (h + 1) * half].astype(F32) + nn(gated, mixers_ref[0])
        for s in range(2):
            a = out[2 * s * slab : (2 * s + 1) * slab]
            b = out[(2 * s + 1) * slab : (2 * s + 2) * slab]
            pooled = ((a + b) * 0.5).astype(BF)
            start = h * half // 2 + s * slab
            first_ref[start : start + slab] = pooled
            active[s * slab : (s + 1) * slab] = gelu(pooled.astype(F32)).astype(BF)
    down_ref[...] = nn(alow_ref[...], kernels_ref[1, 2]).astype(BF)
    up_ref[...] = nn(ahigh_ref[...], kernels_ref[1, 0]).astype(BF)


def coarse_body(
    scale, bins_per,
    ids_ref, prev_ref, low_ref, high_ref, next_ref, first_ref, kernels_ref, mixers_ref, readout_ref, targets_ref,
    gated_ref, second_ref, logit_ref, upper_ref, glow_ref, ghigh_ref,
):
    half = low_ref.shape[0]
    slab = half // 2
    slopes = []
    for h, came in enumerate((prev_ref, next_ref)):
        inner = (
            nn(low_ref[...], kernels_ref[1, 1 - h]) + nn(high_ref[...], kernels_ref[1, 2 - h])
            + came[...].astype(F32)
        )
        slopes.append(gelu_slope(inner))
        gated = gelu(inner).astype(BF)
        gated_ref[h * half : (h + 1) * half] = gated
        out = first_ref[h * half : (h + 1) * half].astype(F32) + nn(gated, mixers_ref[1])
        second_ref[h * slab : (h + 1) * slab] = ((out[:slab] + out[slab:]) * 0.5).astype(BF)
    bins = second_ref.shape[0]
    tracks = readout_ref.shape[1]
    width = min(512, tracks)
    bin_ids = ids_ref[0] * bins_per + lax.broadcasted_iota(jnp.int32, (bins, 1), 0)
    weight = jnp.where(bin_ids * 4 < ids_ref[1], scale, 0.0).astype(F32)
    second = second_ref[...]
    upper = jnp.zeros((bins, second.shape[1]), F32)
    for n in range(tracks // width):
        cols = slice(n * width, (n + 1) * width)
        readout = readout_ref[:, cols]
        logits = nn(second, readout)
        small = jnp.exp(-jnp.abs(logits))
        plus = jnp.maximum(logits, 0.0) + jnp.log1p(small)
        gate = jnp.where(logits >= 0.0, 1.0, small) / (1.0 + small)
        grad = (weight * (plus - targets_ref[:, cols].astype(F32)) * gate).astype(BF)
        logit_ref[:, cols] = grad
        upper = upper + nt(grad, readout)
    upper = (upper * 0.5).astype(BF)
    upper_ref[...] = upper
    back = nt(upper, mixers_ref[1])
    for h, out in enumerate((glow_ref, ghigh_ref)):
        piece = back[h * slab : (h + 1) * slab]
        for s in range(2):
            out[s * slab : (s + 1) * slab] = (piece * slopes[h][s * slab : (s + 1) * slab]).astype(BF)


def readout_body(ids_ref, after_ref, before_ref, second_ref, logit_ref, keep_ref, send_ref):
    width = keep_ref.shape[2]
    second = second_ref[...]
    for k in range(4):
        start = pl.multiple_of((ids_ref[0] ^ k) * width, width)
        out = send_ref if k & 1 else keep_ref
        out[k >> 1] = tn(second, logit_ref[:, pl.ds(start, width)]).astype(BF)


def store_blocks(ids_ref, pieces, keep_ref, send_ref):
    width = pieces[0].shape[1] // 4
    for d in range(4):
        block = jnp.concatenate([p[:, d * width : (d + 1) * width] for p in pieces], axis=1)
        far = (ids_ref[0] >> 1) ^ (d >> 1)

        @pl.when((ids_ref[0] & 1) == (d & 1))
        def _(block=block, far=far):
            keep_ref[far] = block

        @pl.when((ids_ref[0] & 1) != (d & 1))
        def _(block=block, far=far):
            send_ref[far] = block


def mixer_piece(gated, upstream, spread_ref, split_ref):
    mixed = 0.0
    for j in range(2):
        left = nn(gated, spread_ref[j]).astype(BF)
        right = nn(upstream, split_ref[j]).astype(BF)
        mixed = mixed + tn(left, right)
    return mixed.astype(BF)


def coarse_grad_body(
    ids_ref, after_ref, before_ref, low_ref, high_ref, gprev_ref, glow_ref, ghigh_ref, gnext_ref, gated_ref, upper_ref,
    spread_ref, split_ref, keep_ref, send_ref,
):
    slab = low_ref.shape[0] // 2
    upper = upper_ref[...]
    rows = jnp.concatenate([upper[:slab], upper[:slab], upper[slab:], upper[slab:]], axis=0)
    grads = (gprev_ref, glow_ref, ghigh_ref, gnext_ref)
    pieces = []
    for t in range(3):
        pieces.append((tn(low_ref[...], grads[2 - t][...]) + tn(high_ref[...], grads[3 - t][...])).astype(BF))
    pieces.append(mixer_piece(gated_ref[...], rows, spread_ref, split_ref))
    store_blocks(ids_ref, pieces, keep_ref, send_ref)


def fine_grad_body(
    scale,
    ids_ref, after_ref, gprev_ref, glow_ref, ghigh_ref, gnext_ref, upper_ref, first_ref, kernels_ref, mixers_ref,
    prev_ref, low_ref, high_ref, next_ref, inner_ref, gated_ref, spread_ref, split_ref,
    trunk_ref, keep_ref, send_ref, lanes_ref,
):
    half = glow_ref.shape[0]
    slab = half // 2
    grads = (gprev_ref, glow_ref, ghigh_ref, gnext_ref)
    upper = upper_ref[...].astype(F32)
    inner_grads, rows = [], []
    for h in range(2):
        back = (
            nt(grads[h + 2][...], kernels_ref[1, 0])
            + nt(grads[h + 1][...], kernels_ref[1, 1])
            + nt(grads[h][...], kernels_ref[1, 2])
        )
        slope = gelu_slope(first_ref[h * half : (h + 1) * half].astype(F32))
        base = upper[h * slab : (h + 1) * slab]
        total = jnp.concatenate([base, base], axis=0) + back * slope
        for t in range(lanes_ref.shape[0]):
            cols = slice(t * 128, (t + 1) * 128)
            for s in range(2):
                lanes_ref[t, pl.ds(s, slab, stride=2), :] = total[s * slab : (s + 1) * slab, cols] * scale
            trunk_ref[h * half : (h + 1) * half, cols] = lanes_ref[t]
        lower = (total * 0.5).astype(BF)
        inner = nt(lower, mixers_ref[0])
        spread_inner = jnp.concatenate([inner[:slab], inner[:slab], inner[slab:], inner[slab:]], axis=0)
        slope = gelu_slope(inner_ref[2 * h * half : 2 * (h + 1) * half])
        inner_grads.append((spread_inner * slope).astype(BF))
        rows += [lower[:slab], lower[:slab], lower[slab:], lower[slab:]]
    taps = (prev_ref, low_ref, high_ref, next_ref)
    pieces = []
    for t in range(3):
        pieces.append((tn(taps[t][...], inner_grads[0]) + tn(taps[t + 1][...], inner_grads[1])).astype(BF))
    pieces.append(mixer_piece(gated_ref[...], jnp.concatenate(rows, axis=0), spread_ref, split_ref))
    store_blocks(ids_ref, pieces, keep_ref, send_ref)


def swap(value, axis, bit):
    size = lax.axis_size(axis)
    return lax.ppermute(value, axis, [(i, i ^ bit) for i in range(size)])


def halo(low, high):
    size = lax.axis_size("seq")
    up = [(i, i + 1) for i in range(size - 1)]
    return (
        lax.ppermute(high, "seq", up),
        lax.ppermute(low, "seq", [(j, i) for i, j in up]),
    )


def core_sum(keep, send):
    came = swap(send, "dp", 1)
    away = (keep[1].astype(F32) + came[1].astype(F32)).astype(BF)
    here = keep[0].astype(F32) + came[0].astype(F32)
    return here, away


def x_sum(here, away):
    return (here + swap(away, "dp", 2).astype(F32)).astype(BF)


def seq_sum(total):
    groups = lax.axis_size("seq")
    rows, columns = total.shape
    parts = lax.all_to_all(
        total.reshape(groups, rows // groups, columns), "seq", split_axis=0, concat_axis=0, tiled=True
    )
    return parts.astype(F32).sum(axis=0)


def side_first_sum(keep, send):
    groups = lax.axis_size("seq")
    side = lax.axis_index("seq") % 2
    came = swap(send, "dp", 1)
    blocks, rows, columns = keep.shape
    total = keep.astype(F32) + came.astype(F32)
    total = total.reshape(blocks, groups // 2, 2, rows // groups, columns)
    other = lax.dynamic_index_in_dim(total, 1 - side, axis=2, keepdims=False).astype(BF)
    own = lax.dynamic_index_in_dim(total, side, axis=2, keepdims=False)
    total = own + swap(other, "seq", 1).astype(F32)
    total = (total[0] + swap(total[1].astype(BF), "dp", 2).astype(F32)).astype(BF)
    lines = [list(range(start, groups, 2)) for start in range(2)]
    parts = lax.all_to_all(total, "seq", split_axis=0, concat_axis=0, axis_index_groups=lines, tiled=True)
    return parts.astype(F32).sum(axis=0)


def shards(embeddings, layout, lengths, targets, projection, kernels, mixers, readout):
    groups = lax.axis_size("seq")
    windows = lax.axis_size("dp")
    me = lax.axis_index("dp")
    device = lax.axis_index("seq")
    rows = embeddings[0, 0]
    row_count = rows.shape[0]
    depth, channels = projection.shape
    width = kernels.shape[3]
    tracks = readout.shape[1]
    half, quarter, eighth = row_count // 2, row_count // 4, row_count // 8
    length = lengths[0]

    side = device % 2
    share = depth // 2
    piece = share // PIECES
    from_core = swap(projection, "dp", 1)
    mine = lax.dynamic_slice_in_dim(projection, side * share, share, axis=0)
    far = [swap(lax.slice_in_dim(mine, i * piece, (i + 1) * piece), "dp", 2) for i in range(PIECES)]
    near, away = (me ^ 2) * depth, (me ^ 3) * depth
    total = project(None, rows, [projection], [me * depth], False)
    total = project(total, rows, [from_core], [(me ^ 1) * depth], False)
    weights, starts = [], []
    for i in range(PIECES):
        if weights:
            total = project(total, rows, weights, starts, False)
        held, total = lax.optimization_barrier((far[i], total))
        if i:
            weights, starts = [side_piece, swap(side_piece, "dp", 1)], [near + side_at, away + side_at]
        else:
            weights, starts = [], []
        at = side * share + i * piece
        weights += [held, swap(held, "dp", 1)]
        starts += [near + at, away + at]
        side_piece = swap(held, "seq", 1)
        side_at = (1 - side) * share + i * piece
    total = project(total, rows, weights, starts, False)
    total = project(
        total, rows, [side_piece, swap(side_piece, "dp", 1)], [near + side_at, away + side_at], True
    )

    block = row_count // groups
    received = lax.all_to_all(
        total.reshape(groups, block, channels), "seq", split_axis=0, concat_axis=0, tiled=True
    ).reshape(row_count, channels)
    column = lax.dynamic_index_in_dim(layout[0], device, axis=1, keepdims=True)
    position = column * block + jnp.arange(block, dtype=jnp.int32)[None, :]
    slot = (position // half) * half + (position % 4) * eighth + (position % half) // 4
    target = jnp.where(device * row_count + position < length, slot, -1).reshape(1, row_count)

    hidden, low, high, down, up = call(
        place_body, (target, received, kernels),
        [((row_count, channels), BF), ((half, channels), BF), ((half, channels), BF),
         ((half, width), BF), ((half, width), BF)],
        2 * row_count * row_count * channels, 24,
    )
    fprev, fnext = halo(down, up)
    local, = call(local_body, (low, high, kernels), [((row_count, width), F32)], 4 * row_count * width * channels, 24)
    fprev, fnext, low_later, high_later = lax.optimization_barrier((fprev, fnext, low, high))
    prev, nxt = halo(low_later, high_later)
    inner, gated, first, alow, ahigh, adown, aup = call(
        fine_body, (fprev, fnext, local, hidden, kernels, mixers),
        [((row_count, width), F32), ((row_count, width), BF), ((half, channels), BF),
         ((quarter, channels), BF), ((quarter, channels), BF), ((quarter, width), BF), ((quarter, width), BF)],
        3 * row_count * width * channels, 24,
    )
    aprev, anext = halo(adown, aup)
    bins = quarter
    loss = 2.0 / math.sqrt(windows * groups * bins)
    ids = jnp.stack([device, length]).astype(jnp.int32)
    place = jnp.stack([me, device]).astype(jnp.int32)

    def coarse(*refs):
        coarse_body(loss, bins, *refs)

    cgated, second, logit_grad, upper, glow, ghigh = call(
        coarse, (ids, aprev, alow, ahigh, anext, first, kernels, mixers, readout, targets[0]),
        [((half, width), BF), ((bins, channels), BF), ((bins, tracks), BF), ((bins, channels), BF),
         ((quarter, width), BF), ((quarter, width), BF)],
        8 * half * width * channels + 4 * bins * tracks * channels, 32, smem=1,
    )
    gprev, gnext = halo(glow, ghigh)
    track_keep, track_send = call(
        readout_body, (place, prev, nxt, second, logit_grad), [((2, channels, tracks // 4), BF)] * 2,
        2 * bins * tracks * channels, 24, smem=1, after=2,
    )
    track_here, track_away = core_sum(track_keep, track_send)

    per = width // groups
    fold = np.zeros((2, width, channels), ml_dtypes.bfloat16)
    split = np.zeros((2, channels, width), ml_dtypes.bfloat16)
    for j in range(2):
        for a in range(width):
            fold[j, a, (a // per) * 2 * per + j * per + a % per] = 1
        piece_width = width // 4
        for b in range(width):
            split[j, (b // piece_width) * 2 * piece_width + j * piece_width + b % piece_width, b] = 1
    fold, split = jnp.asarray(fold), jnp.asarray(split)
    pair = [((2, channels, width), BF)] * 2

    def fine(*refs):
        fine_grad_body(math.sqrt(windows * groups * bins) * 0.5, *refs)

    cut = channels // 2
    track_first = swap(track_away[:cut], "dp", 2)
    trunk, fine_keep, fine_send = call(
        fine,
        (place, track_away, gprev, glow, ghigh, gnext, upper, first, kernels, mixers,
         prev, low, high, nxt, inner, gated, fold, split),
        [((half, channels), F32)] + pair,
        20 * row_count * width * channels, 40, smem=1, after=1,
        scratch=[pltpu.VMEM((channels // 128, quarter, 128), F32)],
    )
    fine_send, track_first = lax.optimization_barrier((fine_send, track_first))
    track_last = swap(track_away[cut:], "dp", 2)
    track_total = (track_here + jnp.concatenate([track_first, track_last]).astype(F32)).astype(BF)
    readout_total = seq_sum(track_total)
    fine_here, fine_away = core_sum(fine_keep, fine_send)
    coarse_keep, coarse_send = call(
        coarse_grad_body,
        (place, fine_away, track_total, alow, ahigh, gprev, glow, ghigh, gnext, cgated, upper, fold, split), pair,
        12 * half * width * channels, 32, smem=1, after=2,
    )
    fine_total = seq_sum(x_sum(fine_here, fine_away))
    coarse_total = side_first_sum(coarse_keep, coarse_send)

    cut = width // windows
    kernel_rows, mixer_rows = [], []
    for value in (fine_total, coarse_total):
        kernel_rows.append(jnp.stack([value[:, t * cut : (t + 1) * cut] for t in range(3)]))
        tail = value[:, 3 * cut :]
        mixer_rows.append(jnp.concatenate([tail[:per], tail[per:]], axis=1))
    return (jnp.stack(kernel_rows), jnp.stack(mixer_rows), readout_total, trunk[None])


def solution(mesh):
    placed = (
        P("dp", "seq", None, None),
        P("dp", None, None),
        P("dp"),
        P("dp", "seq", None),
        P("dp", None),
        P(),
        P(),
        P(),
    )
    return jax.shard_map(
        shards,
        mesh=mesh,
        in_specs=placed,
        out_specs=(
            P(None, None, "seq", "dp"),
            P(None, "seq", "dp"),
            P("seq", "dp"),
            P("dp", "seq", None),
        ),
        check_vma=False,
    )
```

```python
import math

import jax
import jax.numpy as jnp
import ml_dtypes
import numpy as np
from jax import lax
from jax.experimental import pallas as pl
from jax.experimental.pallas import tpu as pltpu
from jax.sharding import PartitionSpec as P

SPREAD_FINE = 256
SPREAD_COARSE = 128
BF = jnp.bfloat16
F32 = jnp.float32
PIECES = 4

CHEAP = pl.CostEstimate(flops=1024, bytes_accessed=1024, transcendentals=0)
VMEM = pl.BlockSpec(memory_space=pltpu.VMEM)
SMEM = pl.BlockSpec(memory_space=pltpu.SMEM)
ANY = pl.BlockSpec(memory_space=pl.ANY)


def params(mib):
    return pltpu.CompilerParams(vmem_limit_bytes=mib * 1024 * 1024)


def gelu(v):
    return 0.5 * v * (1.0 + lax.erf(v * (1.0 / math.sqrt(2.0))))


def gelu_slope(v):
    cumulative = 0.5 * (1.0 + lax.erf(v * (1.0 / math.sqrt(2.0))))
    density = jnp.exp(-0.5 * v * v) * (1.0 / math.sqrt(2.0 * math.pi))
    return cumulative + v * density


def nn(a, b):
    return jnp.dot(a, b, preferred_element_type=F32)


def nt(a, b):
    return lax.dot_general(a, b, (((1,), (1,)), ((), ())), preferred_element_type=F32)


def tn(a, b):
    return lax.dot_general(a, b, (((0,), (0,)), ((), ())), preferred_element_type=F32)


def call(body, inputs, outs, mib, smem=0, scratch=(), after=0):
    outs = [jax.ShapeDtypeStruct(s, d) for s, d in outs]
    return pl.pallas_call(
        body,
        out_shape=outs,
        in_specs=[SMEM] * smem + [ANY] * after + [VMEM] * (len(inputs) - smem - after),
        out_specs=[VMEM] * len(outs),
        scratch_shapes=list(scratch),
        compiler_params=params(mib),
        cost_estimate=CHEAP,
    )(*inputs)


def project(total, rows, weights, starts, final):
    count = len(weights)
    row_count = rows.shape[0]
    depth, channels = weights[0].shape
    block = min(512, depth)
    steps = depth // block

    def body(starts_ref, *refs):
        row_refs, weight_refs = refs[:count], refs[count : 2 * count]
        rest = refs[2 * count :]
        step = pl.program_id(0)
        part = nn(row_refs[0][...], weight_refs[0][...])
        for r, w in zip(row_refs[1:], weight_refs[1:]):
            part = part + nn(r[...], w[...])
        if total is None:
            out_ref = rest[0]

            @pl.when(step == 0)
            def _():
                out_ref[...] = part

            @pl.when(step > 0)
            def _():
                out_ref[...] += part
        else:
            old_ref, out_ref = rest
            if steps == 1:
                out_ref[...] = (old_ref[...] + part).astype(out_ref.dtype)
            else:

                @pl.when(step == 0)
                def _():
                    out_ref[...] = old_ref[...] + part

                @pl.when(step > 0)
                def _():
                    out_ref[...] += part

    def row_map(k):
        return lambda i, s: (0, s[k] + i)

    whole = pl.BlockSpec((row_count, channels), lambda i, s: (0, 0))
    in_specs = [pl.BlockSpec((row_count, block), row_map(k)) for k in range(count)]
    in_specs += [pl.BlockSpec((block, channels), lambda i, s: (i, 0)) for _ in range(count)]
    inputs = [rows] * count + list(weights)
    if total is not None:
        in_specs.append(whole)
        inputs.append(total)
    out = jax.ShapeDtypeStruct((row_count, channels), BF if final else F32)
    return pl.pallas_call(
        body,
        out_shape=out,
        grid_spec=pltpu.PrefetchScalarGridSpec(
            num_scalar_prefetch=1, grid=(steps,), in_specs=in_specs, out_specs=whole
        ),
        compiler_params=params(56),
        cost_estimate=CHEAP,
    )(jnp.stack(starts).astype(jnp.int32) // block, *inputs)


def absorb(total, rows, weights, starts, final):
    count = len(weights)
    row_count = rows.shape[0]
    depth, channels = weights[0].shape

    def body(starts_ref, rows_ref, old_ref, *refs):
        weight_refs, (out_ref, held_ref, sems) = refs[:count], refs[count:]
        copies = []
        for k in range(count):
            start = pl.multiple_of(starts_ref[k], depth)
            copies.append(pltpu.make_async_copy(rows_ref.at[:, pl.ds(start, depth)], held_ref.at[k], sems.at[k]))
            copies[-1].start()
        for copy in copies:
            copy.wait()
        half = row_count // 2
        for h in range(2):
            part = slice(h * half, (h + 1) * half)
            sums = old_ref[part]
            for k in range(count):
                sums = sums + nn(held_ref[k, part], weight_refs[k][...])
            out_ref[part] = sums.astype(out_ref.dtype)

    return pl.pallas_call(
        body,
        out_shape=jax.ShapeDtypeStruct((row_count, channels), BF if final else F32),
        in_specs=[SMEM, ANY] + [VMEM] * (count + 1),
        out_specs=VMEM,
        scratch_shapes=[pltpu.VMEM((count, row_count, depth), BF), pltpu.SemaphoreType.DMA((count,))],
        compiler_params=params(24),
        cost_estimate=CHEAP,
    )(jnp.stack(starts).astype(jnp.int32), rows, total, *weights)


def place_body(target_ref, received_ref, kernels_ref, hidden_ref, low_ref, high_ref, down_ref, up_ref):
    half = low_ref.shape[0]
    rows = received_ref[...]
    for h, out in enumerate((low_ref, high_ref)):
        order = lax.broadcasted_iota(jnp.int32, (half, rows.shape[0]), 0) + h * half
        pick = jnp.where(order == target_ref[...], 1.0, 0.0).astype(BF)
        placed = nn(pick, rows)
        hidden_ref[h * half : (h + 1) * half] = placed.astype(BF)
        out[...] = gelu(placed).astype(BF)
    down_ref[...] = nn(low_ref[...], kernels_ref[0, 2]).astype(BF)
    up_ref[...] = nn(high_ref[...], kernels_ref[0, 0]).astype(BF)


def local_body(low_ref, high_ref, kernels_ref, inner_ref):
    half = low_ref.shape[0]
    low, high = low_ref[...], high_ref[...]
    inner_ref[:half] = nn(low, kernels_ref[0, 1]) + nn(high, kernels_ref[0, 2])
    inner_ref[half:] = nn(low, kernels_ref[0, 0]) + nn(high, kernels_ref[0, 1])


def fine_body(
    prev_ref, next_ref, local_ref, hidden_ref, kernels_ref, mixers_ref,
    inner_ref, gated_ref, first_ref, alow_ref, ahigh_ref, down_ref, up_ref,
):
    half = prev_ref.shape[0]
    slab = half // 4
    for h, (came, active) in enumerate(((prev_ref, alow_ref), (next_ref, ahigh_ref))):
        inner = local_ref[h * half : (h + 1) * half] + came[...].astype(F32)
        inner_ref[h * half : (h + 1) * half] = inner
        gated = gelu(inner).astype(BF)
        gated_ref[h * half : (h + 1) * half] = gated
        out = hidden_ref[h * half : (h + 1) * half].astype(F32) + nn(gated, mixers_ref[0])
        for s in range(2):
            a = out[2 * s * slab : (2 * s + 1) * slab]
            b = out[(2 * s + 1) * slab : (2 * s + 2) * slab]
            pooled = ((a + b) * 0.5).astype(BF)
            start = h * half // 2 + s * slab
            first_ref[start : start + slab] = pooled
            active[s * slab : (s + 1) * slab] = gelu(pooled.astype(F32)).astype(BF)
    down_ref[...] = nn(alow_ref[...], kernels_ref[1, 2]).astype(BF)
    up_ref[...] = nn(ahigh_ref[...], kernels_ref[1, 0]).astype(BF)


def coarse_body(
    scale, bins_per,
    ids_ref, prev_ref, low_ref, high_ref, next_ref, first_ref, kernels_ref, mixers_ref, readout_ref, targets_ref,
    gated_ref, second_ref, logit_ref, upper_ref, glow_ref, ghigh_ref,
):
    half = low_ref.shape[0]
    slab = half // 2
    slopes = []
    for h, came in enumerate((prev_ref, next_ref)):
        inner = (
            nn(low_ref[...], kernels_ref[1, 1 - h]) + nn(high_ref[...], kernels_ref[1, 2 - h])
            + came[...].astype(F32)
        )
        slopes.append(gelu_slope(inner))
        gated = gelu(inner).astype(BF)
        gated_ref[h * half : (h + 1) * half] = gated
        out = first_ref[h * half : (h + 1) * half].astype(F32) + nn(gated, mixers_ref[1])
        second_ref[h * slab : (h + 1) * slab] = ((out[:slab] + out[slab:]) * 0.5).astype(BF)
    bins = second_ref.shape[0]
    tracks = readout_ref.shape[1]
    width = min(512, tracks)
    bin_ids = ids_ref[0] * bins_per + lax.broadcasted_iota(jnp.int32, (bins, 1), 0)
    weight = jnp.where(bin_ids * 4 < ids_ref[1], scale, 0.0).astype(F32)
    second = second_ref[...]
    upper = jnp.zeros((bins, second.shape[1]), F32)
    for n in range(tracks // width):
        cols = slice(n * width, (n + 1) * width)
        readout = readout_ref[:, cols]
        logits = nn(second, readout)
        small = jnp.exp(-jnp.abs(logits))
        plus = jnp.maximum(logits, 0.0) + jnp.log1p(small)
        gate = jnp.where(logits >= 0.0, 1.0, small) / (1.0 + small)
        grad = (weight * (plus - targets_ref[:, cols].astype(F32)) * gate).astype(BF)
        logit_ref[:, cols] = grad
        upper = upper + nt(grad, readout)
    upper = (upper * 0.5).astype(BF)
    upper_ref[...] = upper
    back = nt(upper, mixers_ref[1])
    for h, out in enumerate((glow_ref, ghigh_ref)):
        piece = back[h * slab : (h + 1) * slab]
        for s in range(2):
            out[s * slab : (s + 1) * slab] = (piece * slopes[h][s * slab : (s + 1) * slab]).astype(BF)


def readout_body(ids_ref, second_ref, logit_ref, keep_ref, send_ref):
    width = keep_ref.shape[2]
    second = second_ref[...]
    for k in range(4):
        start = pl.multiple_of((ids_ref[0] ^ k) * width, width)
        out = send_ref if k & 1 else keep_ref
        out[k >> 1] = tn(second, logit_ref[:, pl.ds(start, width)]).astype(BF)


def store_blocks(ids_ref, pieces, keep_ref, send_ref):
    width = pieces[0].shape[1] // 4
    for d in range(4):
        block = jnp.concatenate([p[:, d * width : (d + 1) * width] for p in pieces], axis=1)
        far = (ids_ref[0] >> 1) ^ (d >> 1)

        @pl.when((ids_ref[0] & 1) == (d & 1))
        def _(block=block, far=far):
            keep_ref[far] = block

        @pl.when((ids_ref[0] & 1) != (d & 1))
        def _(block=block, far=far):
            send_ref[far] = block


def mixer_piece(gated, upstream, spread_ref, split_ref):
    mixed = 0.0
    for j in range(2):
        left = nn(gated, spread_ref[j]).astype(BF)
        right = nn(upstream, split_ref[j]).astype(BF)
        mixed = mixed + tn(left, right)
    return mixed.astype(BF)


def weight_body(
    slab, ids_ref, after_ref, low_ref, high_ref, gprev_ref, glow_ref, ghigh_ref, gnext_ref, gated_ref, up_ref,
    spread_ref, split_ref, keep_ref, send_ref,
):
    up = up_ref[...]
    rows = []
    for s in range(up.shape[0] // slab):
        rows += [up[s * slab : (s + 1) * slab]] * 2
    grads = (gprev_ref, glow_ref, ghigh_ref, gnext_ref)
    pieces = []
    for t in range(3):
        pieces.append((tn(low_ref[...], grads[2 - t][...]) + tn(high_ref[...], grads[3 - t][...])).astype(BF))
    pieces.append(mixer_piece(gated_ref[...], jnp.concatenate(rows, axis=0), spread_ref, split_ref))
    store_blocks(ids_ref, pieces, keep_ref, send_ref)


def fine_back_body(
    scale,
    after_ref, gprev_ref, glow_ref, ghigh_ref, gnext_ref, upper_ref, first_ref, kernels_ref, mixers_ref, inner_ref,
    trunk_ref, lower_ref, ilow_ref, ihigh_ref, lanes_ref,
):
    half = glow_ref.shape[0]
    slab = half // 2
    grads = (gprev_ref, glow_ref, ghigh_ref, gnext_ref)
    upper = upper_ref[...].astype(F32)
    for h, out in enumerate((ilow_ref, ihigh_ref)):
        back = (
            nt(grads[h + 2][...], kernels_ref[1, 0])
            + nt(grads[h + 1][...], kernels_ref[1, 1])
            + nt(grads[h][...], kernels_ref[1, 2])
        )
        slope = gelu_slope(first_ref[h * half : (h + 1) * half].astype(F32))
        base = upper[h * slab : (h + 1) * slab]
        total = jnp.concatenate([base, base], axis=0) + back * slope
        for t in range(lanes_ref.shape[0]):
            cols = slice(t * 128, (t + 1) * 128)
            for s in range(2):
                lanes_ref[t, pl.ds(s, slab, stride=2), :] = total[s * slab : (s + 1) * slab, cols] * scale
            trunk_ref[h * half : (h + 1) * half, cols] = lanes_ref[t]
        lower = (total * 0.5).astype(BF)
        lower_ref[h * half : (h + 1) * half] = lower
        inner = nt(lower, mixers_ref[0])
        spread_inner = jnp.concatenate([inner[:slab], inner[:slab], inner[slab:], inner[slab:]], axis=0)
        slope = gelu_slope(inner_ref[2 * h * half : 2 * (h + 1) * half])
        out[...] = (spread_inner * slope).astype(BF)


def swap(value, axis, bit):
    size = lax.axis_size(axis)
    return lax.ppermute(value, axis, [(i, i ^ bit) for i in range(size)])


def halo(low, high):
    size = lax.axis_size("seq")
    up = [(i, i + 1) for i in range(size - 1)]
    return (
        lax.ppermute(high, "seq", up),
        lax.ppermute(low, "seq", [(j, i) for i, j in up]),
    )


def core_sum(keep, send):
    came = swap(send, "dp", 1)
    away = (keep[1].astype(F32) + came[1].astype(F32)).astype(BF)
    here = keep[0].astype(F32) + came[0].astype(F32)
    return here, away


def seq_sum(total):
    groups = lax.axis_size("seq")
    rows, columns = total.shape
    parts = lax.all_to_all(
        total.reshape(groups, rows // groups, columns), "seq", split_axis=0, concat_axis=0, tiled=True
    )
    return parts.astype(F32).sum(axis=0)


def side_halves(total):
    groups = lax.axis_size("seq")
    side = lax.axis_index("seq") % 2
    blocks, rows, columns = total.shape
    total = total.reshape(blocks, groups // 2, 2, rows // groups, columns)
    return (
        lax.dynamic_index_in_dim(total, 1 - side, axis=2, keepdims=False).astype(BF),
        lax.dynamic_index_in_dim(total, side, axis=2, keepdims=False),
    )


def crossed_sums(here, away, keep, send):
    groups = lax.axis_size("seq")
    other, own = side_halves(keep.astype(F32) + swap(send, "dp", 1).astype(F32))
    x_came, side_came = swap(away, "dp", 2), swap(other, "seq", 1)
    left_other, left_own = side_halves((here + x_came.astype(F32))[None])
    right = own + side_came.astype(F32)
    side_came, x_came = swap(left_other[0], "seq", 1), swap(right[1].astype(BF), "dp", 2)
    left = left_own[0] + side_came.astype(F32)
    right = right[0] + x_came.astype(F32)
    both = jnp.concatenate([left, right], axis=2).astype(BF)
    lines = [list(range(start, groups, 2)) for start in range(2)]
    parts = lax.all_to_all(both, "seq", split_axis=0, concat_axis=0, axis_index_groups=lines, tiled=True)
    total = parts.astype(F32).sum(axis=0)
    return total[:, : left.shape[2]], total[:, left.shape[2] :]


def shards(embeddings, layout, lengths, targets, projection, kernels, mixers, readout):
    groups = lax.axis_size("seq")
    windows = lax.axis_size("dp")
    me = lax.axis_index("dp")
    device = lax.axis_index("seq")
    rows = embeddings[0, 0]
    row_count = rows.shape[0]
    depth, channels = projection.shape
    width = kernels.shape[3]
    tracks = readout.shape[1]
    half, quarter, eighth = row_count // 2, row_count // 4, row_count // 8
    length = lengths[0]

    side = device % 2
    share = depth // 2
    piece = share // PIECES
    from_core = swap(projection, "dp", 1)
    mine = lax.dynamic_slice_in_dim(projection, side * share, share, axis=0)
    far = [swap(lax.slice_in_dim(mine, i * piece, (i + 1) * piece), "dp", 2) for i in range(PIECES)]
    near, away = (me ^ 2) * depth, (me ^ 3) * depth
    total = project(None, rows, [projection, from_core], [me * depth, (me ^ 1) * depth], False)
    far_weights, far_starts, side_weights, side_starts = [], [], [], []
    for i in range(PIECES):
        held = far[i]
        if i == 0:
            held, total = lax.optimization_barrier((held, total))
        if i == 2:
            total = absorb(
                total, rows, far_weights + side_weights[:2], far_starts + side_starts[:2], False
            )
            held, total = lax.optimization_barrier((held, total))
            far_weights, far_starts = side_weights[2:], side_starts[2:]
            side_weights, side_starts = [], []
        crossed = swap(held, "seq", 1)
        at, side_at = side * share + i * piece, (1 - side) * share + i * piece
        far_weights += [held, swap(held, "dp", 1)]
        far_starts += [near + at, away + at]
        side_weights += [crossed, swap(crossed, "dp", 1)]
        side_starts += [near + side_at, away + side_at]
    total = absorb(total, rows, far_weights, far_starts, False)
    total = absorb(total, rows, side_weights, side_starts, True)

    block = row_count // groups
    received = lax.all_to_all(
        total.reshape(groups, block, channels), "seq", split_axis=0, concat_axis=0, tiled=True
    ).reshape(row_count, channels)
    column = lax.dynamic_index_in_dim(layout[0], device, axis=1, keepdims=True)
    position = column * block + jnp.arange(block, dtype=jnp.int32)[None, :]
    slot = (position // half) * half + (position % 4) * eighth + (position % half) // 4
    target = jnp.where(device * row_count + position < length, slot, -1).reshape(1, row_count)

    hidden, low, high, down, up = call(
        place_body, (target, received, kernels),
        [((row_count, channels), BF), ((half, channels), BF), ((half, channels), BF),
         ((half, width), BF), ((half, width), BF)],
        24,
    )
    fprev, fnext = halo(down, up)
    local, = call(local_body, (low, high, kernels), [((row_count, width), F32)], 24)
    inner, gated, first, alow, ahigh, adown, aup = call(
        fine_body, (fprev, fnext, local, hidden, kernels, mixers),
        [((row_count, width), F32), ((row_count, width), BF), ((half, channels), BF),
         ((quarter, channels), BF), ((quarter, channels), BF), ((quarter, width), BF), ((quarter, width), BF)],
        24,
    )
    aprev, anext = halo(adown, aup)
    bins = quarter
    loss = 2.0 / math.sqrt(windows * groups * bins)
    ids = jnp.stack([device, length]).astype(jnp.int32)
    place = jnp.stack([me, device]).astype(jnp.int32)

    def coarse(*refs):
        coarse_body(loss, bins, *refs)

    cgated, second, logit_grad, upper, glow, ghigh = call(
        coarse, (ids, aprev, alow, ahigh, anext, first, kernels, mixers, readout, targets[0]),
        [((half, width), BF), ((bins, channels), BF), ((bins, tracks), BF), ((bins, channels), BF),
         ((quarter, width), BF), ((quarter, width), BF)],
        32, smem=1,
    )
    gprev, gnext = halo(glow, ghigh)
    track_keep, track_send = call(
        readout_body, (place, second, logit_grad), [((2, channels, tracks // 4), BF)] * 2,
        24, smem=1,
    )
    track_here, track_away = core_sum(track_keep, track_send)

    per = width // groups
    fold = np.zeros((2, width, channels), ml_dtypes.bfloat16)
    split = np.zeros((2, channels, width), ml_dtypes.bfloat16)
    for j in range(2):
        for a in range(width):
            fold[j, a, (a // per) * 2 * per + j * per + a % per] = 1
        piece_width = width // 4
        for b in range(width):
            split[j, (b // piece_width) * 2 * piece_width + j * piece_width + b % piece_width, b] = 1
    fold, split = jnp.asarray(fold), jnp.asarray(split)
    pair = [((2, channels, width), BF)] * 2

    def fine_back(*refs):
        fine_back_body(math.sqrt(windows * groups * bins) * 0.5, *refs)

    def weights(*refs):
        weight_body(eighth, *refs)

    track_x = swap(track_away, "dp", 2)
    trunk, lower, ilow, ihigh = call(
        fine_back, (track_away, gprev, glow, ghigh, gnext, upper, first, kernels, mixers, inner),
        [((half, channels), F32), ((half, channels), BF), ((half, width), BF), ((half, width), BF)],
        32, after=1,
        scratch=[pltpu.VMEM((channels // 128, quarter, 128), F32)],
    )
    iprev, inext = halo(ilow, ihigh)
    coarse_keep, coarse_send = call(
        weights, (place, ilow, alow, ahigh, gprev, glow, ghigh, gnext, cgated, upper, fold, split), pair,
        32, smem=1, after=1,
    )
    iprev, inext, coarse_send = lax.optimization_barrier((iprev, inext, coarse_send))
    fine_keep, fine_send = call(
        weights, (place, ilow, low, high, iprev, ilow, ihigh, inext, gated, lower, fold, split), pair,
        32, smem=1, after=1,
    )
    fine_send, track_x = lax.optimization_barrier((fine_send, track_x))
    readout_total = seq_sum((track_here + track_x.astype(F32)).astype(BF))
    fine_total, coarse_total = crossed_sums(*core_sum(fine_keep, fine_send), coarse_keep, coarse_send)

    cut = width // windows
    kernel_rows, mixer_rows = [], []
    for value in (fine_total, coarse_total):
        kernel_rows.append(jnp.stack([value[:, t * cut : (t + 1) * cut] for t in range(3)]))
        tail = value[:, 3 * cut :]
        mixer_rows.append(jnp.concatenate([tail[:per], tail[per:]], axis=1))
    return (jnp.stack(kernel_rows), jnp.stack(mixer_rows), readout_total, trunk[None])


def solution(mesh):
    placed = (
        P("dp", "seq", None, None),
        P("dp", None, None),
        P("dp"),
        P("dp", "seq", None),
        P("dp", None),
        P(),
        P(),
        P(),
    )
    return jax.shard_map(
        shards,
        mesh=mesh,
        in_specs=placed,
        out_specs=(
            P(None, None, "seq", "dp"),
            P(None, "seq", "dp"),
            P("seq", "dp"),
            P("dp", "seq", None),
        ),
        check_vma=False,
    )
```

```python
import math

import jax
import jax.numpy as jnp
import ml_dtypes
import numpy as np
from jax import lax
from jax.experimental import pallas as pl
from jax.experimental.pallas import tpu as pltpu
from jax.sharding import PartitionSpec as P

SPREAD_FINE = 256
SPREAD_COARSE = 128
BF = jnp.bfloat16
F32 = jnp.float32

CHEAP = pl.CostEstimate(flops=1024, bytes_accessed=1024, transcendentals=0)
VMEM = pl.BlockSpec(memory_space=pltpu.VMEM)
SMEM = pl.BlockSpec(memory_space=pltpu.SMEM)
HBM = pl.BlockSpec(memory_space=pltpu.HBM)
ANY = pl.BlockSpec(memory_space=pl.ANY)


def params(mib):
    return pltpu.CompilerParams(vmem_limit_bytes=mib * 1024 * 1024)


def gelu(v):
    return 0.5 * v * (1.0 + lax.erf(v * (1.0 / math.sqrt(2.0))))


def gelu_slope(v):
    cumulative = 0.5 * (1.0 + lax.erf(v * (1.0 / math.sqrt(2.0))))
    density = jnp.exp(-0.5 * v * v) * (1.0 / math.sqrt(2.0 * math.pi))
    return cumulative + v * density


def nn(a, b):
    return jnp.dot(a, b, preferred_element_type=F32)


def nt(a, b):
    return lax.dot_general(a, b, (((1,), (1,)), ((), ())), preferred_element_type=F32)


def tn(a, b):
    return lax.dot_general(a, b, (((0,), (0,)), ((), ())), preferred_element_type=F32)


def call(body, inputs, outs, mib, smem=0, scratch=(), after=0):
    outs = [jax.ShapeDtypeStruct(s, d) for s, d in outs]
    return pl.pallas_call(
        body,
        out_shape=outs,
        in_specs=[SMEM] * smem + [ANY] * after + [VMEM] * (len(inputs) - smem - after),
        out_specs=[VMEM] * len(outs),
        scratch_shapes=list(scratch),
        compiler_params=params(mib),
        cost_estimate=CHEAP,
    )(*inputs)


def absorb(total, column, rows, weights, starts, final, after=()):
    count = len(weights)
    row_count = rows.shape[0]
    depth, columns = weights[0].shape
    block = min(512, depth)
    blocks = [(k, at) for k in range(count) for at in range(0, depth, block)]
    first = total is None
    fixed = 2 if first else 3

    def body(*refs):
        starts_ref, rows_ref, old_ref = refs[0], refs[1], refs[2]
        weight_refs = refs[fixed : fixed + count]
        out_ref, held_ref, sems, *more = refs[fixed + count + len(after) :]
        copies = []
        for n, (k, at) in enumerate(blocks):
            start = pl.multiple_of(starts_ref[k] + at, block)
            batch = [pltpu.make_async_copy(rows_ref.at[:, pl.ds(start, block)], held_ref.at[n], sems.at[0, n])]
            if first:
                batch.append(
                    pltpu.make_async_copy(weight_refs[k].at[pl.ds(at, block)], more[0].at[n], sems.at[1, n])
                )
            for copy in batch:
                copy.start()
            copies.append(batch)
        half = row_count // 2
        for h in range(2):
            part = slice(h * half, (h + 1) * half)
            sums = 0.0 if first else old_ref[part, column : column + columns]
            for n, (k, at) in enumerate(blocks):
                if h == 0:
                    for copy in copies[n]:
                        copy.wait()
                piece = more[0][n] if first else weight_refs[k][at : at + block]
                sums = sums + nn(held_ref[n, part], piece)
            out_ref[part] = sums.astype(out_ref.dtype)

    scratch = [
        pltpu.VMEM((len(blocks), row_count, block), BF),
        pltpu.SemaphoreType.DMA((2, len(blocks))),
    ]
    if first:
        scratch.append(pltpu.VMEM((len(blocks), block, columns), BF))
    return pl.pallas_call(
        body,
        out_shape=jax.ShapeDtypeStruct((row_count, columns), BF if final else F32),
        in_specs=[SMEM, HBM] + ([] if first else [VMEM]) + [HBM if first else VMEM] * count + [ANY] * len(after),
        out_specs=VMEM,
        scratch_shapes=scratch,
        compiler_params=params(49),
        cost_estimate=CHEAP,
    )(jnp.stack(starts).astype(jnp.int32), rows, *([] if first else [total]), *weights, *after)


def place_body(target_ref, left_ref, right_ref, kernels_ref, hidden_ref, low_ref, high_ref, down_ref, up_ref):
    half = low_ref.shape[0]
    row_count, columns = left_ref.shape
    for h, out in enumerate((low_ref, high_ref)):
        order = lax.broadcasted_iota(jnp.int32, (half, row_count), 0) + h * half
        pick = jnp.where(order == target_ref[...], 1.0, 0.0).astype(BF)
        for n, rows_ref in enumerate((left_ref, right_ref)):
            placed = nn(pick, rows_ref[...])
            cols = slice(n * columns, (n + 1) * columns)
            hidden_ref[h * half : (h + 1) * half, cols] = placed.astype(BF)
            out[:, cols] = gelu(placed).astype(BF)
    down_ref[...] = nn(low_ref[...], kernels_ref[0, 2]).astype(BF)
    up_ref[...] = nn(high_ref[...], kernels_ref[0, 0]).astype(BF)


def local_body(low_ref, high_ref, kernels_ref, inner_ref):
    half = low_ref.shape[0]
    low, high = low_ref[...], high_ref[...]
    inner_ref[:half] = nn(low, kernels_ref[0, 1]) + nn(high, kernels_ref[0, 2])
    inner_ref[half:] = nn(low, kernels_ref[0, 0]) + nn(high, kernels_ref[0, 1])


def fine_body(
    prev_ref, next_ref, local_ref, hidden_ref, kernels_ref, mixers_ref,
    inner_ref, gated_ref, first_ref, alow_ref, ahigh_ref, down_ref, up_ref,
):
    half = prev_ref.shape[0]
    slab = half // 4
    for h, (came, active) in enumerate(((prev_ref, alow_ref), (next_ref, ahigh_ref))):
        inner = local_ref[h * half : (h + 1) * half] + came[...].astype(F32)
        inner_ref[h * half : (h + 1) * half] = inner
        gated = gelu(inner).astype(BF)
        gated_ref[h * half : (h + 1) * half] = gated
        out = hidden_ref[h * half : (h + 1) * half].astype(F32) + nn(gated, mixers_ref[0])
        for s in range(2):
            a = out[2 * s * slab : (2 * s + 1) * slab]
            b = out[(2 * s + 1) * slab : (2 * s + 2) * slab]
            pooled = ((a + b) * 0.5).astype(BF)
            start = h * half // 2 + s * slab
            first_ref[start : start + slab] = pooled
            active[s * slab : (s + 1) * slab] = gelu(pooled.astype(F32)).astype(BF)
    down_ref[...] = nn(alow_ref[...], kernels_ref[1, 2]).astype(BF)
    up_ref[...] = nn(ahigh_ref[...], kernels_ref[1, 0]).astype(BF)


def coarse_body(
    scale, bins_per,
    ids_ref, prev_ref, low_ref, high_ref, next_ref, first_ref, kernels_ref, mixers_ref, readout_ref, targets_ref,
    gated_ref, second_ref, logit_ref, upper_ref, glow_ref, ghigh_ref,
):
    half = low_ref.shape[0]
    slab = half // 2
    slopes = []
    for h, came in enumerate((prev_ref, next_ref)):
        inner = (
            nn(low_ref[...], kernels_ref[1, 1 - h]) + nn(high_ref[...], kernels_ref[1, 2 - h])
            + came[...].astype(F32)
        )
        slopes.append(gelu_slope(inner))
        gated = gelu(inner).astype(BF)
        gated_ref[h * half : (h + 1) * half] = gated
        out = first_ref[h * half : (h + 1) * half].astype(F32) + nn(gated, mixers_ref[1])
        second_ref[h * slab : (h + 1) * slab] = ((out[:slab] + out[slab:]) * 0.5).astype(BF)
    bins = second_ref.shape[0]
    tracks = readout_ref.shape[1]
    width = min(512, tracks)
    bin_ids = ids_ref[0] * bins_per + lax.broadcasted_iota(jnp.int32, (bins, 1), 0)
    weight = jnp.where(bin_ids * 4 < ids_ref[1], scale, 0.0).astype(F32)
    second = second_ref[...]
    upper = jnp.zeros((bins, second.shape[1]), F32)
    for n in range(tracks // width):
        cols = slice(n * width, (n + 1) * width)
        readout = readout_ref[:, cols]
        logits = nn(second, readout)
        small = jnp.exp(-jnp.abs(logits))
        plus = jnp.maximum(logits, 0.0) + jnp.log1p(small)
        gate = jnp.where(logits >= 0.0, 1.0, small) / (1.0 + small)
        grad = (weight * (plus - targets_ref[:, cols].astype(F32)) * gate).astype(BF)
        logit_ref[:, cols] = grad
        upper = upper + nt(grad, readout)
    upper = (upper * 0.5).astype(BF)
    upper_ref[...] = upper
    back = nt(upper, mixers_ref[1])
    for h, out in enumerate((glow_ref, ghigh_ref)):
        piece = back[h * slab : (h + 1) * slab]
        for s in range(2):
            out[s * slab : (s + 1) * slab] = (piece * slopes[h][s * slab : (s + 1) * slab]).astype(BF)


def readout_body(ids_ref, second_ref, logit_ref, keep_ref, send_ref):
    width = keep_ref.shape[2]
    second = second_ref[...]
    for k in range(4):
        start = pl.multiple_of((ids_ref[0] ^ k) * width, width)
        out = send_ref if k & 1 else keep_ref
        out[k >> 1] = tn(second, logit_ref[:, pl.ds(start, width)]).astype(BF)


def store_blocks(ids_ref, pieces, keep_ref, send_ref):
    width = pieces[0].shape[1] // 4
    for d in range(4):
        block = jnp.concatenate([p[:, d * width : (d + 1) * width] for p in pieces], axis=1)
        far = (ids_ref[0] >> 1) ^ (d >> 1)

        @pl.when((ids_ref[0] & 1) == (d & 1))
        def _(block=block, far=far):
            keep_ref[far] = block

        @pl.when((ids_ref[0] & 1) != (d & 1))
        def _(block=block, far=far):
            send_ref[far] = block


def mixer_piece(slab, gated, up, spread_ref, split_ref):
    mixed = 0.0
    for j in range(2):
        left = nn(gated, spread_ref[j]).astype(BF)
        right = nn(up, split_ref[j]).astype(BF)
        rows = []
        for s in range(up.shape[0] // slab):
            rows += [right[s * slab : (s + 1) * slab]] * 2
        mixed = mixed + tn(left, jnp.concatenate(rows, axis=0))
    return mixed.astype(BF)


def weight_body(
    slab, ids_ref, after_ref, low_ref, high_ref, gprev_ref, glow_ref, ghigh_ref, gnext_ref, gated_ref, up_ref,
    spread_ref, split_ref, keep_ref, send_ref,
):
    grads = (gprev_ref, glow_ref, ghigh_ref, gnext_ref)
    pieces = []
    for t in range(3):
        pieces.append((tn(low_ref[...], grads[2 - t][...]) + tn(high_ref[...], grads[3 - t][...])).astype(BF))
    pieces.append(mixer_piece(slab, gated_ref[...], up_ref[...], spread_ref, split_ref))
    store_blocks(ids_ref, pieces, keep_ref, send_ref)


def fine_back_body(
    scale,
    after_ref, gprev_ref, glow_ref, ghigh_ref, gnext_ref, upper_ref, first_ref, kernels_ref, mixers_ref, inner_ref,
    trunk_ref, lower_ref, ilow_ref, ihigh_ref, lanes_ref,
):
    half = glow_ref.shape[0]
    slab = half // 2
    grads = (gprev_ref, glow_ref, ghigh_ref, gnext_ref)
    upper = upper_ref[...].astype(F32)
    for h, out in enumerate((ilow_ref, ihigh_ref)):
        back = (
            nt(grads[h + 2][...], kernels_ref[1, 0])
            + nt(grads[h + 1][...], kernels_ref[1, 1])
            + nt(grads[h][...], kernels_ref[1, 2])
        )
        slope = gelu_slope(first_ref[h * half : (h + 1) * half].astype(F32))
        base = upper[h * slab : (h + 1) * slab]
        total = jnp.concatenate([base, base], axis=0) + back * slope
        for t in range(lanes_ref.shape[0]):
            cols = slice(t * 128, (t + 1) * 128)
            for s in range(2):
                lanes_ref[t, pl.ds(s, slab, stride=2), :] = total[s * slab : (s + 1) * slab, cols] * scale
            trunk_ref[h * half : (h + 1) * half, cols] = lanes_ref[t]
        lower = (total * 0.5).astype(BF)
        lower_ref[h * half : (h + 1) * half] = lower
        inner = nt(lower, mixers_ref[0])
        spread_inner = jnp.concatenate([inner[:slab], inner[:slab], inner[slab:], inner[slab:]], axis=0)
        slope = gelu_slope(inner_ref[2 * h * half : 2 * (h + 1) * half])
        out[...] = (spread_inner * slope).astype(BF)


def swap(value, axis, bit):
    size = lax.axis_size(axis)
    return lax.ppermute(value, axis, [(i, i ^ bit) for i in range(size)])


def halo(low, high):
    size = lax.axis_size("seq")
    up = [(i, i + 1) for i in range(size - 1)]
    return (
        lax.ppermute(high, "seq", up),
        lax.ppermute(low, "seq", [(j, i) for i, j in up]),
    )


def core_sum(keep, send):
    came = swap(send, "dp", 1)
    away = (keep[1].astype(F32) + came[1].astype(F32)).astype(BF)
    here = keep[0].astype(F32) + came[0].astype(F32)
    return here, away


def seq_sum(total):
    groups = lax.axis_size("seq")
    rows, columns = total.shape
    parts = lax.all_to_all(
        total.reshape(groups, rows // groups, columns), "seq", split_axis=0, concat_axis=0, tiled=True
    )
    return parts.astype(F32).sum(axis=0)


def side_rows(value, side):
    groups = lax.axis_size("seq")
    *blocks, rows, columns = value.shape
    value = value.reshape(*blocks, groups // 2, 2, rows // groups, columns)
    return lax.dynamic_index_in_dim(value, side, axis=len(blocks) + 1, keepdims=False).astype(F32)


def crossed_sums(left_keep, left_send, right_keep, right_send):
    groups = lax.axis_size("seq")
    side = lax.axis_index("seq") % 2
    right_came = swap(right_send, "dp", 1)
    left_came = swap(left_send, "dp", 1)
    x_came = swap((left_keep[1].astype(F32) + left_came[1].astype(F32)).astype(BF), "dp", 2)
    other = side_rows(right_keep, 1 - side) + side_rows(right_came, 1 - side)
    side_came = swap(other.astype(BF), "seq", 1)

    def left_half(at):
        return side_rows(left_keep[0], at) + side_rows(left_came[0], at) + side_rows(x_came, at)

    def right_half(at):
        return side_rows(right_keep[at], side) + side_rows(right_came[at], side) + side_came[at].astype(F32)

    left = swap(left_half(1 - side).astype(BF), "seq", 1)
    right = swap(right_half(1).astype(BF), "dp", 2)
    left = left_half(side) + left.astype(F32)
    right = right_half(0) + right.astype(F32)
    both = jnp.concatenate([left, right], axis=2).astype(BF)
    lines = [list(range(start, groups, 2)) for start in range(2)]
    parts = lax.all_to_all(both, "seq", split_axis=0, concat_axis=0, axis_index_groups=lines, tiled=True)
    total = parts.astype(F32).sum(axis=0)
    return total[:, : left.shape[2]], total[:, left.shape[2] :]


def shards(embeddings, layout, lengths, targets, projection, kernels, mixers, readout):
    groups = lax.axis_size("seq")
    windows = lax.axis_size("dp")
    me = lax.axis_index("dp")
    device = lax.axis_index("seq")
    rows = embeddings[0, 0]
    row_count = rows.shape[0]
    depth, channels = projection.shape
    width = kernels.shape[3]
    tracks = readout.shape[1]
    half, quarter, eighth = row_count // 2, row_count // 4, row_count // 8
    length = lengths[0]

    side = device % 2
    share = depth // 2
    piece = share // 2
    columns = channels // 2
    block = row_count // groups
    from_core = swap(projection, "dp", 1)
    mine = lax.dynamic_slice_in_dim(projection, side * share, share, axis=0)
    far = [
        [swap(mine[i * piece : (i + 1) * piece, n * columns : (n + 1) * columns], "dp", 2) for i in range(2)]
        for n in range(2)
    ]
    near, away = (me ^ 2) * depth, (me ^ 3) * depth
    total = absorb(None, 0, rows, [projection, from_core], [me * depth, (me ^ 1) * depth], False)
    received = []
    for n in range(2):
        far_weights, far_starts, side_weights, side_starts = [], [], [], []
        for i in range(2):
            held = far[n][i]
            if n == 0 and i == 0:
                held, total = lax.optimization_barrier((held, total))
            crossed = swap(held, "seq", 1)
            at, side_at = side * share + i * piece, (1 - side) * share + i * piece
            far_weights += [held, swap(held, "dp", 1)]
            far_starts += [near + at, away + at]
            side_weights += [crossed, swap(crossed, "dp", 1)]
            side_starts += [near + side_at, away + side_at]
        sums = absorb(total, n * columns, rows, far_weights, far_starts, False)
        sums = absorb(sums, 0, rows, side_weights, side_starts, True, received)
        received.append(
            lax.all_to_all(
                sums.reshape(groups, block, columns), "seq", split_axis=0, concat_axis=0, tiled=True
            ).reshape(row_count, columns)
        )

    column = lax.dynamic_index_in_dim(layout[0], device, axis=1, keepdims=True)
    position = column * block + jnp.arange(block, dtype=jnp.int32)[None, :]
    slot = (position // half) * half + (position % 4) * eighth + (position % half) // 4
    target = jnp.where(device * row_count + position < length, slot, -1).reshape(1, row_count)

    hidden, low, high, down, up = call(
        place_body, (target, *received, kernels),
        [((row_count, channels), BF), ((half, channels), BF), ((half, channels), BF),
         ((half, width), BF), ((half, width), BF)],
        24,
    )
    fprev, fnext = halo(down, up)
    local, = call(local_body, (low, high, kernels), [((row_count, width), F32)], 24)
    inner, gated, first, alow, ahigh, adown, aup = call(
        fine_body, (fprev, fnext, local, hidden, kernels, mixers),
        [((row_count, width), F32), ((row_count, width), BF), ((half, channels), BF),
         ((quarter, channels), BF), ((quarter, channels), BF), ((quarter, width), BF), ((quarter, width), BF)],
        24,
    )
    aprev, anext = halo(adown, aup)
    bins = quarter
    loss = 2.0 / math.sqrt(windows * groups * bins)
    ids = jnp.stack([device, length]).astype(jnp.int32)
    place = jnp.stack([me, device]).astype(jnp.int32)

    def coarse(*refs):
        coarse_body(loss, bins, *refs)

    cgated, second, logit_grad, upper, glow, ghigh = call(
        coarse, (ids, aprev, alow, ahigh, anext, first, kernels, mixers, readout, targets[0]),
        [((half, width), BF), ((bins, channels), BF), ((bins, tracks), BF), ((bins, channels), BF),
         ((quarter, width), BF), ((quarter, width), BF)],
        32, smem=1,
    )
    gprev, gnext = halo(glow, ghigh)
    track_keep, track_send = call(
        readout_body, (place, second, logit_grad), [((2, channels, tracks // 4), BF)] * 2,
        24, smem=1,
    )
    track_here, track_away = core_sum(track_keep, track_send)

    per = width // groups
    fold = np.zeros((2, width, channels), ml_dtypes.bfloat16)
    split = np.zeros((2, channels, width), ml_dtypes.bfloat16)
    for j in range(2):
        for a in range(width):
            fold[j, a, (a // per) * 2 * per + j * per + a % per] = 1
        piece_width = width // 4
        for b in range(width):
            split[j, (b // piece_width) * 2 * piece_width + j * piece_width + b % piece_width, b] = 1
    fold, split = jnp.asarray(fold), jnp.asarray(split)
    pair = [((2, channels, width), BF)] * 2

    def fine_back(*refs):
        fine_back_body(math.sqrt(windows * groups * bins) * 0.5, *refs)

    def weights(*refs):
        weight_body(eighth, *refs)

    track_x = swap(track_away, "dp", 2)
    trunk, lower, ilow, ihigh = call(
        fine_back, (track_away, gprev, glow, ghigh, gnext, upper, first, kernels, mixers, inner),
        [((half, channels), F32), ((half, channels), BF), ((half, width), BF), ((half, width), BF)],
        32, after=1,
        scratch=[pltpu.VMEM((channels // 128, quarter, 128), F32)],
    )
    iprev, inext = halo(ilow, ihigh)
    coarse_keep, coarse_send = call(
        weights, (place, ilow, alow, ahigh, gprev, glow, ghigh, gnext, cgated, upper, fold, split), pair,
        32, smem=1, after=1,
    )
    iprev, inext, coarse_send = lax.optimization_barrier((iprev, inext, coarse_send))
    fine_keep, fine_send = call(
        weights, (place, ilow, low, high, iprev, ilow, ihigh, inext, gated, lower, fold, split), pair,
        32, smem=1, after=1,
    )
    fine_send, track_x = lax.optimization_barrier((fine_send, track_x))
    readout_total = seq_sum((track_here + track_x.astype(F32)).astype(BF))
    fine_total, coarse_total = crossed_sums(fine_keep, fine_send, coarse_keep, coarse_send)

    cut = width // windows
    kernel_rows, mixer_rows = [], []
    for value in (fine_total, coarse_total):
        kernel_rows.append(jnp.stack([value[:, t * cut : (t + 1) * cut] for t in range(3)]))
        tail = value[:, 3 * cut :]
        mixer_rows.append(jnp.concatenate([tail[:per], tail[per:]], axis=1))
    return (jnp.stack(kernel_rows), jnp.stack(mixer_rows), readout_total, trunk[None])


def solution(mesh):
    placed = (
        P("dp", "seq", None, None),
        P("dp", None, None),
        P("dp"),
        P("dp", "seq", None),
        P("dp", None),
        P(),
        P(),
        P(),
    )
    return jax.shard_map(
        shards,
        mesh=mesh,
        in_specs=placed,
        out_specs=(
            P(None, None, "seq", "dp"),
            P(None, "seq", "dp"),
            P("seq", "dp"),
            P("dp", "seq", None),
        ),
        check_vma=False,
    )
```

```python
import math

import jax
import jax.numpy as jnp
import ml_dtypes
import numpy as np
from jax import lax
from jax.experimental import pallas as pl
from jax.experimental.pallas import tpu as pltpu
from jax.sharding import PartitionSpec as P

SPREAD_FINE = 256
SPREAD_COARSE = 128
BF = jnp.bfloat16
F32 = jnp.float32

CHEAP = pl.CostEstimate(flops=1024, bytes_accessed=1024, transcendentals=0)
VMEM = pl.BlockSpec(memory_space=pltpu.VMEM)
SMEM = pl.BlockSpec(memory_space=pltpu.SMEM)
HBM = pl.BlockSpec(memory_space=pltpu.HBM)
ANY = pl.BlockSpec(memory_space=pl.ANY)


def params(mib):
    return pltpu.CompilerParams(vmem_limit_bytes=mib * 1024 * 1024)


def gelu(v):
    return 0.5 * v * (1.0 + lax.erf(v * (1.0 / math.sqrt(2.0))))


def gelu_slope(v):
    cumulative = 0.5 * (1.0 + lax.erf(v * (1.0 / math.sqrt(2.0))))
    density = jnp.exp(-0.5 * v * v) * (1.0 / math.sqrt(2.0 * math.pi))
    return cumulative + v * density


def nn(a, b):
    return jnp.dot(a, b, preferred_element_type=F32)


def nt(a, b):
    return lax.dot_general(a, b, (((1,), (1,)), ((), ())), preferred_element_type=F32)


def tn(a, b):
    return lax.dot_general(a, b, (((0,), (0,)), ((), ())), preferred_element_type=F32)


def call(body, inputs, outs, mib, smem=0, scratch=(), after=0):
    outs = [jax.ShapeDtypeStruct(s, d) for s, d in outs]
    return pl.pallas_call(
        body,
        out_shape=outs,
        in_specs=[SMEM] * smem + [ANY] * after + [VMEM] * (len(inputs) - smem - after),
        out_specs=[VMEM] * len(outs),
        scratch_shapes=list(scratch),
        compiler_params=params(mib),
        cost_estimate=CHEAP,
    )(*inputs)


def absorb(total, column, rows, weights, starts, final, after=()):
    count = len(weights)
    row_count = rows.shape[0]
    depth, columns = weights[0].shape
    block = min(512, depth)
    blocks = [(k, at) for k in range(count) for at in range(0, depth, block)]
    first = total is None
    fixed = 2 if first else 3

    def body(*refs):
        starts_ref, rows_ref, old_ref = refs[0], refs[1], refs[2]
        weight_refs = refs[fixed : fixed + count]
        out_ref, held_ref, sems, *more = refs[fixed + count + len(after) :]
        copies = []
        for n, (k, at) in enumerate(blocks):
            start = pl.multiple_of(starts_ref[k] + at, block)
            batch = [pltpu.make_async_copy(rows_ref.at[:, pl.ds(start, block)], held_ref.at[n], sems.at[0, n])]
            if first:
                batch.append(
                    pltpu.make_async_copy(weight_refs[k].at[pl.ds(at, block)], more[0].at[n], sems.at[1, n])
                )
            for copy in batch:
                copy.start()
            copies.append(batch)
        half = row_count // 2
        for h in range(2):
            part = slice(h * half, (h + 1) * half)
            sums = 0.0 if first else old_ref[part, column : column + columns]
            for n, (k, at) in enumerate(blocks):
                if h == 0:
                    for copy in copies[n]:
                        copy.wait()
                piece = more[0][n] if first else weight_refs[k][at : at + block]
                sums = sums + nn(held_ref[n, part], piece)
            out_ref[part] = sums.astype(out_ref.dtype)

    scratch = [
        pltpu.VMEM((len(blocks), row_count, block), BF),
        pltpu.SemaphoreType.DMA((2, len(blocks))),
    ]
    if first:
        scratch.append(pltpu.VMEM((len(blocks), block, columns), BF))
    return pl.pallas_call(
        body,
        out_shape=jax.ShapeDtypeStruct((row_count, columns), BF if final else F32),
        in_specs=[SMEM, HBM] + ([] if first else [VMEM]) + [HBM if first else VMEM] * count + [ANY] * len(after),
        out_specs=VMEM,
        scratch_shapes=scratch,
        compiler_params=params(20 if first else 14),
        cost_estimate=CHEAP,
    )(jnp.stack(starts).astype(jnp.int32), rows, *([] if first else [total]), *weights, *after)


def place_body(target_ref, left_ref, right_ref, kernels_ref, hidden_ref, low_ref, high_ref, down_ref, up_ref):
    half = low_ref.shape[0]
    row_count, columns = left_ref.shape
    for h, out in enumerate((low_ref, high_ref)):
        order = lax.broadcasted_iota(jnp.int32, (half, row_count), 0) + h * half
        pick = jnp.where(order == target_ref[...], 1.0, 0.0).astype(BF)
        for n, rows_ref in enumerate((left_ref, right_ref)):
            placed = nn(pick, rows_ref[...])
            cols = slice(n * columns, (n + 1) * columns)
            hidden_ref[h * half : (h + 1) * half, cols] = placed.astype(BF)
            out[:, cols] = gelu(placed).astype(BF)
    down_ref[...] = nn(low_ref[...], kernels_ref[0, 2]).astype(BF)
    up_ref[...] = nn(high_ref[...], kernels_ref[0, 0]).astype(BF)


def local_body(low_ref, high_ref, kernels_ref, inner_ref):
    half = low_ref.shape[0]
    low, high = low_ref[...], high_ref[...]
    inner_ref[:half] = nn(low, kernels_ref[0, 1]) + nn(high, kernels_ref[0, 2])
    inner_ref[half:] = nn(low, kernels_ref[0, 0]) + nn(high, kernels_ref[0, 1])


def fine_body(
    prev_ref, next_ref, local_ref, hidden_ref, kernels_ref, mixers_ref,
    inner_ref, gated_ref, first_ref, alow_ref, ahigh_ref, down_ref, up_ref,
):
    half = prev_ref.shape[0]
    slab = half // 4
    for h, (came, active) in enumerate(((prev_ref, alow_ref), (next_ref, ahigh_ref))):
        inner = local_ref[h * half : (h + 1) * half] + came[...].astype(F32)
        inner_ref[h * half : (h + 1) * half] = inner
        gated = gelu(inner).astype(BF)
        gated_ref[h * half : (h + 1) * half] = gated
        out = hidden_ref[h * half : (h + 1) * half].astype(F32) + nn(gated, mixers_ref[0])
        for s in range(2):
            a = out[2 * s * slab : (2 * s + 1) * slab]
            b = out[(2 * s + 1) * slab : (2 * s + 2) * slab]
            pooled = ((a + b) * 0.5).astype(BF)
            start = h * half // 2 + s * slab
            first_ref[start : start + slab] = pooled
            active[s * slab : (s + 1) * slab] = gelu(pooled.astype(F32)).astype(BF)
    down_ref[...] = nn(alow_ref[...], kernels_ref[1, 2]).astype(BF)
    up_ref[...] = nn(ahigh_ref[...], kernels_ref[1, 0]).astype(BF)


def coarse_body(
    scale, bins_per,
    ids_ref, prev_ref, low_ref, high_ref, next_ref, first_ref, kernels_ref, mixers_ref, readout_ref, targets_ref,
    gated_ref, second_ref, logit_ref, upper_ref, glow_ref, ghigh_ref,
):
    half = low_ref.shape[0]
    slab = half // 2
    slopes = []
    for h, came in enumerate((prev_ref, next_ref)):
        inner = (
            nn(low_ref[...], kernels_ref[1, 1 - h]) + nn(high_ref[...], kernels_ref[1, 2 - h])
            + came[...].astype(F32)
        )
        slopes.append(gelu_slope(inner))
        gated = gelu(inner).astype(BF)
        gated_ref[h * half : (h + 1) * half] = gated
        out = first_ref[h * half : (h + 1) * half].astype(F32) + nn(gated, mixers_ref[1])
        second_ref[h * slab : (h + 1) * slab] = ((out[:slab] + out[slab:]) * 0.5).astype(BF)
    bins = second_ref.shape[0]
    tracks = readout_ref.shape[1]
    width = min(512, tracks)
    bin_ids = ids_ref[0] * bins_per + lax.broadcasted_iota(jnp.int32, (bins, 1), 0)
    weight = jnp.where(bin_ids * 4 < ids_ref[1], scale, 0.0).astype(F32)
    second = second_ref[...]
    upper = jnp.zeros((bins, second.shape[1]), F32)
    for n in range(tracks // width):
        cols = slice(n * width, (n + 1) * width)
        readout = readout_ref[:, cols]
        logits = nn(second, readout)
        small = jnp.exp(-jnp.abs(logits))
        plus = jnp.maximum(logits, 0.0) + jnp.log1p(small)
        gate = jnp.where(logits >= 0.0, 1.0, small) / (1.0 + small)
        grad = (weight * (plus - targets_ref[:, cols].astype(F32)) * gate).astype(BF)
        logit_ref[:, cols] = grad
        upper = upper + nt(grad, readout)
    upper = (upper * 0.5).astype(BF)
    upper_ref[...] = upper
    back = nt(upper, mixers_ref[1])
    for h, out in enumerate((glow_ref, ghigh_ref)):
        piece = back[h * slab : (h + 1) * slab]
        for s in range(2):
            out[s * slab : (s + 1) * slab] = (piece * slopes[h][s * slab : (s + 1) * slab]).astype(BF)


def readout_body(ids_ref, second_ref, logit_ref, keep_ref, send_ref):
    width = keep_ref.shape[2]
    second = second_ref[...]
    for k in range(4):
        start = pl.multiple_of((ids_ref[0] ^ k) * width, width)
        out = send_ref if k & 1 else keep_ref
        out[k >> 1] = tn(second, logit_ref[:, pl.ds(start, width)]).astype(BF)


def store_blocks(ids_ref, pieces, keep_ref, send_ref):
    width = pieces[0].shape[1] // 4
    for d in range(4):
        block = jnp.concatenate([p[:, d * width : (d + 1) * width] for p in pieces], axis=1)
        far = (ids_ref[0] >> 1) ^ (d >> 1)

        @pl.when((ids_ref[0] & 1) == (d & 1))
        def _(block=block, far=far):
            keep_ref[far] = block

        @pl.when((ids_ref[0] & 1) != (d & 1))
        def _(block=block, far=far):
            send_ref[far] = block


def mixer_piece(slab, gated, up, spread_ref, split_ref):
    mixed = 0.0
    for j in range(2):
        left = nn(gated, spread_ref[j]).astype(BF)
        right = nn(up, split_ref[j]).astype(BF)
        rows = []
        for s in range(up.shape[0] // slab):
            rows += [right[s * slab : (s + 1) * slab]] * 2
        mixed = mixed + tn(left, jnp.concatenate(rows, axis=0))
    return mixed.astype(BF)


def weight_body(
    slab, ids_ref, after_ref, low_ref, high_ref, gprev_ref, glow_ref, ghigh_ref, gnext_ref, gated_ref, up_ref,
    spread_ref, split_ref, keep_ref, send_ref,
):
    grads = (gprev_ref, glow_ref, ghigh_ref, gnext_ref)
    pieces = []
    for t in range(3):
        pieces.append((tn(low_ref[...], grads[2 - t][...]) + tn(high_ref[...], grads[3 - t][...])).astype(BF))
    pieces.append(mixer_piece(slab, gated_ref[...], up_ref[...], spread_ref, split_ref))
    store_blocks(ids_ref, pieces, keep_ref, send_ref)


def fine_back_body(
    scale,
    after_ref, gprev_ref, glow_ref, ghigh_ref, gnext_ref, upper_ref, first_ref, kernels_ref, mixers_ref, inner_ref,
    trunk_ref, lower_ref, ilow_ref, ihigh_ref, lanes_ref,
):
    half = glow_ref.shape[0]
    slab = half // 2
    grads = (gprev_ref, glow_ref, ghigh_ref, gnext_ref)
    upper = upper_ref[...].astype(F32)
    for h, out in enumerate((ilow_ref, ihigh_ref)):
        back = (
            nt(grads[h + 2][...], kernels_ref[1, 0])
            + nt(grads[h + 1][...], kernels_ref[1, 1])
            + nt(grads[h][...], kernels_ref[1, 2])
        )
        slope = gelu_slope(first_ref[h * half : (h + 1) * half].astype(F32))
        base = upper[h * slab : (h + 1) * slab]
        total = jnp.concatenate([base, base], axis=0) + back * slope
        for t in range(lanes_ref.shape[0]):
            cols = slice(t * 128, (t + 1) * 128)
            for s in range(2):
                lanes_ref[t, pl.ds(s, slab, stride=2), :] = total[s * slab : (s + 1) * slab, cols] * scale
            trunk_ref[h * half : (h + 1) * half, cols] = lanes_ref[t]
        lower = (total * 0.5).astype(BF)
        lower_ref[h * half : (h + 1) * half] = lower
        inner = nt(lower, mixers_ref[0])
        spread_inner = jnp.concatenate([inner[:slab], inner[:slab], inner[slab:], inner[slab:]], axis=0)
        slope = gelu_slope(inner_ref[2 * h * half : 2 * (h + 1) * half])
        out[...] = (spread_inner * slope).astype(BF)


def output_body(parts_ref, kernels_ref, mixers_ref):
    total = parts_ref[0].astype(F32)
    for g in range(1, parts_ref.shape[0]):
        total = total + parts_ref[g].astype(F32)
    cut, per = kernels_ref.shape[3], mixers_ref.shape[1]
    for n in range(2):
        start = 4 * n * cut
        for t in range(3):
            kernels_ref[n, t] = total[:, start + t * cut : start + (t + 1) * cut]
        tail = total[:, start + 3 * cut : start + 4 * cut]
        mixers_ref[n] = jnp.concatenate([tail[:per], tail[per:]], axis=1)


def swap(value, axis, bit):
    size = lax.axis_size(axis)
    return lax.ppermute(value, axis, [(i, i ^ bit) for i in range(size)])


def halo(low, high):
    size = lax.axis_size("seq")
    up = [(i, i + 1) for i in range(size - 1)]
    return (
        lax.ppermute(high, "seq", up),
        lax.ppermute(low, "seq", [(j, i) for i, j in up]),
    )


def core_sum(keep, send):
    came = swap(send, "dp", 1)
    away = (keep[1].astype(F32) + came[1].astype(F32)).astype(BF)
    here = keep[0].astype(F32) + came[0].astype(F32)
    return here, away


def seq_parts(total):
    groups = lax.axis_size("seq")
    rows, columns = total.shape
    return lax.all_to_all(
        total.reshape(groups, rows // groups, columns), "seq", split_axis=0, concat_axis=0, tiled=True
    )


def side_rows(value, side):
    groups = lax.axis_size("seq")
    *blocks, rows, columns = value.shape
    value = value.reshape(*blocks, groups // 2, 2, rows // groups, columns)
    return lax.dynamic_index_in_dim(value, side, axis=len(blocks) + 1, keepdims=False).astype(F32)


def crossed_sums(left_keep, left_send, right_keep, right_send, first, first_came):
    groups = lax.axis_size("seq")
    side = lax.axis_index("seq") % 2
    right_came = swap(right_send, "dp", 1)
    left_came = swap(left_send, "dp", 1)
    left_away = (left_keep[1].astype(F32) + left_came[1].astype(F32)).astype(BF)
    left_away, first_came = lax.optimization_barrier((left_away, first_came))
    x_came = swap(left_away, "dp", 2)
    other = side_rows(right_keep, 1 - side) + side_rows(right_came, 1 - side)
    side_came = swap(other.astype(BF), "seq", 1)

    def left_half(at):
        return side_rows(left_keep[0], at) + side_rows(left_came[0], at) + side_rows(x_came, at)

    def right_half(at):
        return side_rows(right_keep[at], side) + side_rows(right_came[at], side) + side_came[at].astype(F32)

    left = swap(left_half(1 - side).astype(BF), "seq", 1)
    right = swap(right_half(1).astype(BF), "dp", 2)
    left = left_half(side) + left.astype(F32)
    right = right_half(0) + right.astype(F32)
    both = jnp.concatenate([left, right], axis=2).astype(BF)
    first = seq_parts((first + first_came.astype(F32)).astype(BF))
    both, first = lax.optimization_barrier((both, first))
    lines = [list(range(start, groups, 2)) for start in range(2)]
    parts = lax.all_to_all(both, "seq", split_axis=0, concat_axis=0, axis_index_groups=lines, tiled=True)
    return parts, first.astype(F32).sum(axis=0)


def shards(embeddings, layout, lengths, targets, projection, kernels, mixers, readout):
    groups = lax.axis_size("seq")
    windows = lax.axis_size("dp")
    me = lax.axis_index("dp")
    device = lax.axis_index("seq")
    rows = embeddings[0, 0]
    row_count = rows.shape[0]
    depth, channels = projection.shape
    width = kernels.shape[3]
    tracks = readout.shape[1]
    half, quarter, eighth = row_count // 2, row_count // 4, row_count // 8
    length = lengths[0]

    side = device % 2
    share = depth // 2
    piece = share // 2
    columns = channels // 2
    block = row_count // groups
    from_core = swap(projection, "dp", 1)
    mine = lax.dynamic_slice_in_dim(projection, side * share, share, axis=0)
    far = [
        [swap(mine[i * piece : (i + 1) * piece, n * columns : (n + 1) * columns], "dp", 2) for i in range(2)]
        for n in range(2)
    ]
    near, away = (me ^ 2) * depth, (me ^ 3) * depth
    total = absorb(None, 0, rows, [projection, from_core], [me * depth, (me ^ 1) * depth], False)
    weights, starts = [], []
    for n in range(2):
        for i in range(2):
            held = far[n][i]
            if n == 0 and i == 0:
                held, total = lax.optimization_barrier((held, total))
            crossed = swap(held, "seq", 1)
            at, side_at = side * share + i * piece, (1 - side) * share + i * piece
            weights.append([held, swap(held, "dp", 1), crossed, swap(crossed, "dp", 1)])
            starts.append([near + at, away + at, near + side_at, away + side_at])

    def send(sums):
        return lax.all_to_all(
            sums.reshape(groups, block, columns), "seq", split_axis=0, concat_axis=0, tiled=True
        ).reshape(row_count, columns)

    left = send(absorb(total, 0, rows, weights[0] + weights[1], starts[0] + starts[1], True, [weights[2][2]]))
    right = absorb(
        total, columns, rows, weights[2] + weights[3][:2], starts[2] + starts[3][:2], False
    )
    right = send(absorb(right, 0, rows, weights[3][2:], starts[3][2:], True, [left]))

    column = lax.dynamic_index_in_dim(layout[0], device, axis=1, keepdims=True)
    position = column * block + jnp.arange(block, dtype=jnp.int32)[None, :]
    slot = (position // half) * half + (position % 4) * eighth + (position % half) // 4
    target = jnp.where(device * row_count + position < length, slot, -1).reshape(1, row_count)

    hidden, low, high, down, up = call(
        place_body, (target, left, right, kernels),
        [((row_count, channels), BF), ((half, channels), BF), ((half, channels), BF),
         ((half, width), BF), ((half, width), BF)],
        24,
    )
    fprev, fnext = halo(down, up)
    local, = call(local_body, (low, high, kernels), [((row_count, width), F32)], 24)
    inner, gated, first, alow, ahigh, adown, aup = call(
        fine_body, (fprev, fnext, local, hidden, kernels, mixers),
        [((row_count, width), F32), ((row_count, width), BF), ((half, channels), BF),
         ((quarter, channels), BF), ((quarter, channels), BF), ((quarter, width), BF), ((quarter, width), BF)],
        24,
    )
    aprev, anext = halo(adown, aup)
    bins = quarter
    loss = 2.0 / math.sqrt(windows * groups * bins)
    ids = jnp.stack([device, length]).astype(jnp.int32)
    place = jnp.stack([me, device]).astype(jnp.int32)

    def coarse(*refs):
        coarse_body(loss, bins, *refs)

    cgated, second, logit_grad, upper, glow, ghigh = call(
        coarse, (ids, aprev, alow, ahigh, anext, first, kernels, mixers, readout, targets[0]),
        [((half, width), BF), ((bins, channels), BF), ((bins, tracks), BF), ((bins, channels), BF),
         ((quarter, width), BF), ((quarter, width), BF)],
        32, smem=1,
    )
    gprev, gnext = halo(glow, ghigh)
    track_keep, track_send = call(
        readout_body, (place, second, logit_grad), [((2, channels, tracks // 4), BF)] * 2,
        24, smem=1,
    )
    track_here, track_away = core_sum(track_keep, track_send)
    track_away, gprev, gnext = lax.optimization_barrier((track_away, gprev, gnext))

    per = width // groups
    fold = np.zeros((2, width, channels), ml_dtypes.bfloat16)
    split = np.zeros((2, channels, width), ml_dtypes.bfloat16)
    for j in range(2):
        for a in range(width):
            fold[j, a, (a // per) * 2 * per + j * per + a % per] = 1
        piece_width = width // 4
        for b in range(width):
            split[j, (b // piece_width) * 2 * piece_width + j * piece_width + b % piece_width, b] = 1
    fold, split = jnp.asarray(fold), jnp.asarray(split)
    pair = [((2, channels, width), BF)] * 2

    def fine_back(*refs):
        fine_back_body(math.sqrt(windows * groups * bins) * 0.5, *refs)

    def weights(*refs):
        weight_body(eighth, *refs)

    track_x = swap(track_away, "dp", 2)
    trunk, lower, ilow, ihigh = call(
        fine_back, (track_away, gprev, glow, ghigh, gnext, upper, first, kernels, mixers, inner),
        [((half, channels), F32), ((half, channels), BF), ((half, width), BF), ((half, width), BF)],
        32, after=1,
        scratch=[pltpu.VMEM((channels // 128, quarter, 128), F32)],
    )
    iprev, inext = halo(ilow, ihigh)
    coarse_keep, coarse_send = call(
        weights, (place, ilow, alow, ahigh, gprev, glow, ghigh, gnext, cgated, upper, fold, split), pair,
        32, smem=1, after=1,
    )
    iprev, inext, coarse_send = lax.optimization_barrier((iprev, inext, coarse_send))
    fine_keep, fine_send = call(
        weights, (place, ilow, low, high, iprev, ilow, ihigh, inext, gated, lower, fold, split), pair,
        32, smem=1, after=1,
    )
    fine_send, track_x = lax.optimization_barrier((fine_send, track_x))
    both, readout_total = crossed_sums(fine_keep, fine_send, coarse_keep, coarse_send, track_here, track_x)
    cut = width // windows
    kernel_total, mixer_total = call(
        output_body, (both,),
        [((2, 3, channels // groups, cut), F32), ((2, per, 2 * cut), F32)], 16,
    )
    return (kernel_total, mixer_total, readout_total, trunk[None])


def solution(mesh):
    placed = (
        P("dp", "seq", None, None),
        P("dp", None, None),
        P("dp"),
        P("dp", "seq", None),
        P("dp", None),
        P(),
        P(),
        P(),
    )
    return jax.shard_map(
        shards,
        mesh=mesh,
        in_specs=placed,
        out_specs=(
            P(None, None, "seq", "dp"),
            P(None, "seq", "dp"),
            P("seq", "dp"),
            P("dp", "seq", None),
        ),
        check_vma=False,
    )
```

```python
import math

import jax
import jax.numpy as jnp
import ml_dtypes
import numpy as np
from jax import lax
from jax.experimental import pallas as pl
from jax.experimental.pallas import tpu as pltpu
from jax.sharding import PartitionSpec as P

SPREAD_FINE = 256
SPREAD_COARSE = 128
BF = jnp.bfloat16
F32 = jnp.float32

CHEAP = pl.CostEstimate(flops=1024, bytes_accessed=1024, transcendentals=0)
VMEM = pl.BlockSpec(memory_space=pltpu.VMEM)
SMEM = pl.BlockSpec(memory_space=pltpu.SMEM)
HBM = pl.BlockSpec(memory_space=pltpu.HBM)
ANY = pl.BlockSpec(memory_space=pl.ANY)


def params(mib):
    return pltpu.CompilerParams(vmem_limit_bytes=mib * 1024 * 1024)


def gelu(v):
    return 0.5 * v * (1.0 + lax.erf(v * (1.0 / math.sqrt(2.0))))


def gelu_slope(v):
    cumulative = 0.5 * (1.0 + lax.erf(v * (1.0 / math.sqrt(2.0))))
    density = jnp.exp(-0.5 * v * v) * (1.0 / math.sqrt(2.0 * math.pi))
    return cumulative + v * density


def nn(a, b):
    return jnp.dot(a, b, preferred_element_type=F32)


def nt(a, b):
    return lax.dot_general(a, b, (((1,), (1,)), ((), ())), preferred_element_type=F32)


def tn(a, b):
    return lax.dot_general(a, b, (((0,), (0,)), ((), ())), preferred_element_type=F32)


def call(body, inputs, outs, mib, smem=0, scratch=(), after=0):
    outs = [jax.ShapeDtypeStruct(s, d) for s, d in outs]
    return pl.pallas_call(
        body,
        out_shape=outs,
        in_specs=[SMEM] * smem + [ANY] * after + [VMEM] * (len(inputs) - smem - after),
        out_specs=[VMEM] * len(outs),
        scratch_shapes=list(scratch),
        compiler_params=params(mib),
        cost_estimate=CHEAP,
    )(*inputs)


def product(rows, weights, starts, later, block):
    count, spare = len(weights), len(later)
    row_count = rows.shape[0]
    depth, columns = weights[0].shape
    blocks = [(k, at) for k in range(count) for at in range(0, depth, block)]

    def body(starts_ref, rows_ref, *refs):
        weight_refs, out_ref, later_refs = refs[:count], refs[count], refs[count + 1 : count + 1 + spare]
        held_ref, piece_ref, sems, later_sems = refs[count + 1 + spare :]
        copies = []
        for n, (k, at) in enumerate(blocks):
            start = pl.multiple_of(starts_ref[k] + at, block)
            copies.append((
                pltpu.make_async_copy(rows_ref.at[:, pl.ds(start, block)], held_ref.at[n], sems.at[0, n]),
                pltpu.make_async_copy(weight_refs[k].at[pl.ds(at, block)], piece_ref.at[n], sems.at[1, n]),
            ))
            for copy in copies[-1]:
                copy.start()
        rest = []
        for n in range(spare):
            start = pl.multiple_of(starts_ref[count + n], block)
            rest.append(
                pltpu.make_async_copy(rows_ref.at[:, pl.ds(start, block)], later_refs[n], later_sems.at[n])
            )
            rest[-1].start()
        half = row_count // 2
        for h in range(2):
            part = slice(h * half, (h + 1) * half)
            sums = 0.0
            for n in range(len(blocks)):
                if h == 0:
                    for copy in copies[n]:
                        copy.wait()
                sums = sums + nn(held_ref[n, part], piece_ref[n])
            out_ref[part] = sums
        for copy in rest:
            copy.wait()

    out = [jax.ShapeDtypeStruct((row_count, columns), F32)]
    out += [jax.ShapeDtypeStruct((row_count, block), BF)] * spare
    return pl.pallas_call(
        body,
        out_shape=out,
        in_specs=[SMEM] + [HBM] * (count + 1),
        out_specs=[VMEM] * (1 + spare),
        scratch_shapes=[
            pltpu.VMEM((len(blocks), row_count, block), BF),
            pltpu.VMEM((len(blocks), block, columns), BF),
            pltpu.SemaphoreType.DMA((2, len(blocks))),
            pltpu.SemaphoreType.DMA((spare,)),
        ],
        compiler_params=params(49),
        cost_estimate=CHEAP,
    )(jnp.stack(starts + later).astype(jnp.int32), rows, *weights)


def absorb(total, column, blocks, weights, final):
    count = len(weights)
    row_count = total.shape[0]
    columns = weights[0].shape[1]

    def body(old_ref, *refs):
        out_ref = refs[2 * count]
        half = row_count // 2
        for h in range(2):
            part = slice(h * half, (h + 1) * half)
            sums = old_ref[part, column : column + columns]
            for k in range(count):
                sums = sums + nn(refs[k][part], refs[count + k][...])
            out_ref[part] = sums.astype(out_ref.dtype)

    return call(
        body, (total, *blocks, *weights), [((row_count, columns), BF if final else F32)], 20
    )[0]


def place_body(target_ref, left_ref, right_ref, kernels_ref, hidden_ref, low_ref, high_ref, down_ref, up_ref):
    half = low_ref.shape[0]
    row_count, columns = left_ref.shape
    for h, out in enumerate((low_ref, high_ref)):
        order = lax.broadcasted_iota(jnp.int32, (half, row_count), 0) + h * half
        pick = jnp.where(order == target_ref[...], 1.0, 0.0).astype(BF)
        for n, rows_ref in enumerate((left_ref, right_ref)):
            placed = nn(pick, rows_ref[...])
            cols = slice(n * columns, (n + 1) * columns)
            hidden_ref[h * half : (h + 1) * half, cols] = placed.astype(BF)
            out[:, cols] = gelu(placed).astype(BF)
    down_ref[...] = nn(low_ref[...], kernels_ref[0, 2]).astype(BF)
    up_ref[...] = nn(high_ref[...], kernels_ref[0, 0]).astype(BF)


def local_body(low_ref, high_ref, kernels_ref, inner_ref):
    half = low_ref.shape[0]
    low, high = low_ref[...], high_ref[...]
    inner_ref[:half] = nn(low, kernels_ref[0, 1]) + nn(high, kernels_ref[0, 2])
    inner_ref[half:] = nn(low, kernels_ref[0, 0]) + nn(high, kernels_ref[0, 1])


def fine_body(
    prev_ref, next_ref, local_ref, hidden_ref, kernels_ref, mixers_ref,
    inner_ref, gated_ref, first_ref, alow_ref, ahigh_ref, down_ref, up_ref,
):
    half = prev_ref.shape[0]
    slab = half // 4
    for h, (came, active) in enumerate(((prev_ref, alow_ref), (next_ref, ahigh_ref))):
        inner = local_ref[h * half : (h + 1) * half] + came[...].astype(F32)
        inner_ref[h * half : (h + 1) * half] = inner
        gated = gelu(inner).astype(BF)
        gated_ref[h * half : (h + 1) * half] = gated
        out = hidden_ref[h * half : (h + 1) * half].astype(F32) + nn(gated, mixers_ref[0])
        for s in range(2):
            a = out[2 * s * slab : (2 * s + 1) * slab]
            b = out[(2 * s + 1) * slab : (2 * s + 2) * slab]
            pooled = ((a + b) * 0.5).astype(BF)
            start = h * half // 2 + s * slab
            first_ref[start : start + slab] = pooled
            active[s * slab : (s + 1) * slab] = gelu(pooled.astype(F32)).astype(BF)
    down_ref[...] = nn(alow_ref[...], kernels_ref[1, 2]).astype(BF)
    up_ref[...] = nn(ahigh_ref[...], kernels_ref[1, 0]).astype(BF)


def coarse_body(
    scale, bins_per,
    ids_ref, prev_ref, low_ref, high_ref, next_ref, first_ref, kernels_ref, mixers_ref, readout_ref, targets_ref,
    gated_ref, second_ref, logit_ref, upper_ref, glow_ref, ghigh_ref,
):
    half = low_ref.shape[0]
    slab = half // 2
    slopes = []
    for h, came in enumerate((prev_ref, next_ref)):
        inner = (
            nn(low_ref[...], kernels_ref[1, 1 - h]) + nn(high_ref[...], kernels_ref[1, 2 - h])
            + came[...].astype(F32)
        )
        slopes.append(gelu_slope(inner))
        gated = gelu(inner).astype(BF)
        gated_ref[h * half : (h + 1) * half] = gated
        out = first_ref[h * half : (h + 1) * half].astype(F32) + nn(gated, mixers_ref[1])
        second_ref[h * slab : (h + 1) * slab] = ((out[:slab] + out[slab:]) * 0.5).astype(BF)
    bins = second_ref.shape[0]
    tracks = readout_ref.shape[1]
    width = min(512, tracks)
    bin_ids = ids_ref[0] * bins_per + lax.broadcasted_iota(jnp.int32, (bins, 1), 0)
    weight = jnp.where(bin_ids * 4 < ids_ref[1], scale, 0.0).astype(F32)
    second = second_ref[...]
    upper = jnp.zeros((bins, second.shape[1]), F32)
    for n in range(tracks // width):
        cols = slice(n * width, (n + 1) * width)
        readout = readout_ref[:, cols]
        logits = nn(second, readout)
        small = jnp.exp(-jnp.abs(logits))
        plus = jnp.maximum(logits, 0.0) + jnp.log1p(small)
        gate = jnp.where(logits >= 0.0, 1.0, small) / (1.0 + small)
        grad = (weight * (plus - targets_ref[:, cols].astype(F32)) * gate).astype(BF)
        logit_ref[:, cols] = grad
        upper = upper + nt(grad, readout)
    upper = (upper * 0.5).astype(BF)
    upper_ref[...] = upper
    back = nt(upper, mixers_ref[1])
    for h, out in enumerate((glow_ref, ghigh_ref)):
        piece = back[h * slab : (h + 1) * slab]
        for s in range(2):
            out[s * slab : (s + 1) * slab] = (piece * slopes[h][s * slab : (s + 1) * slab]).astype(BF)


def readout_body(ids_ref, second_ref, logit_ref, keep_ref, send_ref):
    width = keep_ref.shape[2]
    second = second_ref[...]
    for k in range(4):
        start = pl.multiple_of((ids_ref[0] ^ k) * width, width)
        out = send_ref if k & 1 else keep_ref
        out[k >> 1] = tn(second, logit_ref[:, pl.ds(start, width)]).astype(BF)


def store_blocks(ids_ref, pieces, keep_ref, send_ref):
    width = pieces[0].shape[1] // 4
    for d in range(4):
        block = jnp.concatenate([p[:, d * width : (d + 1) * width] for p in pieces], axis=1)
        far = (ids_ref[0] >> 1) ^ (d >> 1)

        @pl.when((ids_ref[0] & 1) == (d & 1))
        def _(block=block, far=far):
            keep_ref[far] = block

        @pl.when((ids_ref[0] & 1) != (d & 1))
        def _(block=block, far=far):
            send_ref[far] = block


def mixer_piece(slab, gated, up, spread_ref, split_ref):
    mixed = 0.0
    for j in range(2):
        left = nn(gated, spread_ref[j]).astype(BF)
        right = nn(up, split_ref[j]).astype(BF)
        rows = []
        for s in range(up.shape[0] // slab):
            rows += [right[s * slab : (s + 1) * slab]] * 2
        mixed = mixed + tn(left, jnp.concatenate(rows, axis=0))
    return mixed.astype(BF)


def weight_body(
    slab, ids_ref, after_ref, low_ref, high_ref, gprev_ref, glow_ref, ghigh_ref, gnext_ref, gated_ref, up_ref,
    spread_ref, split_ref, keep_ref, send_ref,
):
    grads = (gprev_ref, glow_ref, ghigh_ref, gnext_ref)
    pieces = []
    for t in range(3):
        pieces.append((tn(low_ref[...], grads[2 - t][...]) + tn(high_ref[...], grads[3 - t][...])).astype(BF))
    pieces.append(mixer_piece(slab, gated_ref[...], up_ref[...], spread_ref, split_ref))
    store_blocks(ids_ref, pieces, keep_ref, send_ref)


def fine_back_body(
    scale,
    after_ref, gprev_ref, glow_ref, ghigh_ref, gnext_ref, upper_ref, first_ref, kernels_ref, mixers_ref, inner_ref,
    trunk_ref, lower_ref, ilow_ref, ihigh_ref, lanes_ref,
):
    half = glow_ref.shape[0]
    slab = half // 2
    grads = (gprev_ref, glow_ref, ghigh_ref, gnext_ref)
    upper = upper_ref[...].astype(F32)
    for h, out in enumerate((ilow_ref, ihigh_ref)):
        back = (
            nt(grads[h + 2][...], kernels_ref[1, 0])
            + nt(grads[h + 1][...], kernels_ref[1, 1])
            + nt(grads[h][...], kernels_ref[1, 2])
        )
        slope = gelu_slope(first_ref[h * half : (h + 1) * half].astype(F32))
        base = upper[h * slab : (h + 1) * slab]
        total = jnp.concatenate([base, base], axis=0) + back * slope
        for t in range(lanes_ref.shape[0]):
            cols = slice(t * 128, (t + 1) * 128)
            for s in range(2):
                lanes_ref[t, pl.ds(s, slab, stride=2), :] = total[s * slab : (s + 1) * slab, cols] * scale
            trunk_ref[h * half : (h + 1) * half, cols] = lanes_ref[t]
        lower = (total * 0.5).astype(BF)
        lower_ref[h * half : (h + 1) * half] = lower
        inner = nt(lower, mixers_ref[0])
        spread_inner = jnp.concatenate([inner[:slab], inner[:slab], inner[slab:], inner[slab:]], axis=0)
        slope = gelu_slope(inner_ref[2 * h * half : 2 * (h + 1) * half])
        out[...] = (spread_inner * slope).astype(BF)


def output_body(parts_ref, kernels_ref, mixers_ref):
    total = parts_ref[0].astype(F32)
    for g in range(1, parts_ref.shape[0]):
        total = total + parts_ref[g].astype(F32)
    cut, per = kernels_ref.shape[3], mixers_ref.shape[1]
    for n in range(2):
        start = 4 * n * cut
        for t in range(3):
            kernels_ref[n, t] = total[:, start + t * cut : start + (t + 1) * cut]
        tail = total[:, start + 3 * cut : start + 4 * cut]
        mixers_ref[n] = jnp.concatenate([tail[:per], tail[per:]], axis=1)


def swap(value, axis, bit):
    size = lax.axis_size(axis)
    return lax.ppermute(value, axis, [(i, i ^ bit) for i in range(size)])


def halo(low, high):
    size = lax.axis_size("seq")
    up = [(i, i + 1) for i in range(size - 1)]
    return (
        lax.ppermute(high, "seq", up),
        lax.ppermute(low, "seq", [(j, i) for i, j in up]),
    )


def core_sum(keep, send):
    came = swap(send, "dp", 1)
    away = (keep[1].astype(F32) + came[1].astype(F32)).astype(BF)
    here = keep[0].astype(F32) + came[0].astype(F32)
    return here, away


def seq_parts(total):
    groups = lax.axis_size("seq")
    rows, columns = total.shape
    return lax.all_to_all(
        total.reshape(groups, rows // groups, columns), "seq", split_axis=0, concat_axis=0, tiled=True
    )


def side_rows(value, side):
    groups = lax.axis_size("seq")
    *blocks, rows, columns = value.shape
    value = value.reshape(*blocks, groups // 2, 2, rows // groups, columns)
    return lax.dynamic_index_in_dim(value, side, axis=len(blocks) + 1, keepdims=False).astype(F32)


def crossed_sums(left_keep, left_send, right_keep, right_send, first, first_came):
    groups = lax.axis_size("seq")
    side = lax.axis_index("seq") % 2
    right_came = swap(right_send, "dp", 1)
    left_came = swap(left_send, "dp", 1)
    left_away = (left_keep[1].astype(F32) + left_came[1].astype(F32)).astype(BF)
    left_away, first_came = lax.optimization_barrier((left_away, first_came))
    x_came = swap(left_away, "dp", 2)
    other = side_rows(right_keep, 1 - side) + side_rows(right_came, 1 - side)
    side_came = swap(other.astype(BF), "seq", 1)

    def left_half(at):
        return side_rows(left_keep[0], at) + side_rows(left_came[0], at) + side_rows(x_came, at)

    def right_half(at):
        return side_rows(right_keep[at], side) + side_rows(right_came[at], side) + side_came[at].astype(F32)

    left = swap(left_half(1 - side).astype(BF), "seq", 1)
    right = swap(right_half(1).astype(BF), "dp", 2)
    left = left_half(side) + left.astype(F32)
    right = right_half(0) + right.astype(F32)
    both = jnp.concatenate([left, right], axis=2).astype(BF)
    first = seq_parts((first + first_came.astype(F32)).astype(BF))
    both, first = lax.optimization_barrier((both, first))
    lines = [list(range(start, groups, 2)) for start in range(2)]
    parts = lax.all_to_all(both, "seq", split_axis=0, concat_axis=0, axis_index_groups=lines, tiled=True)
    return parts, first.astype(F32).sum(axis=0)


def shards(embeddings, layout, lengths, targets, projection, kernels, mixers, readout):
    groups = lax.axis_size("seq")
    windows = lax.axis_size("dp")
    me = lax.axis_index("dp")
    device = lax.axis_index("seq")
    rows = embeddings[0, 0]
    row_count = rows.shape[0]
    depth, channels = projection.shape
    width = kernels.shape[3]
    tracks = readout.shape[1]
    half, quarter, eighth = row_count // 2, row_count // 4, row_count // 8
    length = lengths[0]

    side = device % 2
    share = depth // 2
    piece = share // 2
    columns = channels // 2
    block = row_count // groups
    from_core = swap(projection, "dp", 1)
    mine = lax.dynamic_slice_in_dim(projection, side * share, share, axis=0)
    far = [
        [swap(mine[i * piece : (i + 1) * piece, n * columns : (n + 1) * columns], "dp", 2) for i in range(2)]
        for n in range(2)
    ]
    near, away = (me ^ 2) * depth, (me ^ 3) * depth
    later = []
    for i in range(2):
        at, side_at = side * share + i * piece, (1 - side) * share + i * piece
        later += [near + at, away + at, near + side_at, away + side_at]
    total, *blocks = product(rows, [projection, from_core], [me * depth, (me ^ 1) * depth], later, piece)
    weights = []
    for n in range(2):
        for i in range(2):
            held = far[n][i]
            if n == 0 and i == 0:
                held, total = lax.optimization_barrier((held, total))
            crossed = swap(held, "seq", 1)
            weights.append([held, swap(held, "dp", 1), crossed, swap(crossed, "dp", 1)])

    def send(sums):
        return lax.all_to_all(
            sums.reshape(groups, block, columns), "seq", split_axis=0, concat_axis=0, tiled=True
        ).reshape(row_count, columns)

    left = send(absorb(total, 0, blocks, weights[0] + weights[1], True))
    right = absorb(total, columns, blocks[:6], weights[2] + weights[3][:2], False)
    left, last = lax.optimization_barrier((left, weights[3][2]))
    right = send(absorb(right, 0, blocks[6:], [last, weights[3][3]], True))

    column = lax.dynamic_index_in_dim(layout[0], device, axis=1, keepdims=True)
    position = column * block + jnp.arange(block, dtype=jnp.int32)[None, :]
    slot = (position // half) * half + (position % 4) * eighth + (position % half) // 4
    target = jnp.where(device * row_count + position < length, slot, -1).reshape(1, row_count)

    hidden, low, high, down, up = call(
        place_body, (target, left, right, kernels),
        [((row_count, channels), BF), ((half, channels), BF), ((half, channels), BF),
         ((half, width), BF), ((half, width), BF)],
        24,
    )
    fprev, fnext = halo(down, up)
    local, = call(local_body, (low, high, kernels), [((row_count, width), F32)], 24)
    inner, gated, first, alow, ahigh, adown, aup = call(
        fine_body, (fprev, fnext, local, hidden, kernels, mixers),
        [((row_count, width), F32), ((row_count, width), BF), ((half, channels), BF),
         ((quarter, channels), BF), ((quarter, channels), BF), ((quarter, width), BF), ((quarter, width), BF)],
        24,
    )
    aprev, anext = halo(adown, aup)
    bins = quarter
    loss = 2.0 / math.sqrt(windows * groups * bins)
    ids = jnp.stack([device, length]).astype(jnp.int32)
    place = jnp.stack([me, device]).astype(jnp.int32)

    def coarse(*refs):
        coarse_body(loss, bins, *refs)

    cgated, second, logit_grad, upper, glow, ghigh = call(
        coarse, (ids, aprev, alow, ahigh, anext, first, kernels, mixers, readout, targets[0]),
        [((half, width), BF), ((bins, channels), BF), ((bins, tracks), BF), ((bins, channels), BF),
         ((quarter, width), BF), ((quarter, width), BF)],
        32, smem=1,
    )
    gprev, gnext = halo(glow, ghigh)
    track_keep, track_send = call(
        readout_body, (place, second, logit_grad), [((2, channels, tracks // 4), BF)] * 2,
        24, smem=1,
    )
    track_here, track_away = core_sum(track_keep, track_send)
    track_away, gprev, gnext = lax.optimization_barrier((track_away, gprev, gnext))

    per = width // groups
    fold = np.zeros((2, width, channels), ml_dtypes.bfloat16)
    split = np.zeros((2, channels, width), ml_dtypes.bfloat16)
    for j in range(2):
        for a in range(width):
            fold[j, a, (a // per) * 2 * per + j * per + a % per] = 1
        piece_width = width // 4
        for b in range(width):
            split[j, (b // piece_width) * 2 * piece_width + j * piece_width + b % piece_width, b] = 1
    fold, split = jnp.asarray(fold), jnp.asarray(split)
    pair = [((2, channels, width), BF)] * 2

    def fine_back(*refs):
        fine_back_body(math.sqrt(windows * groups * bins) * 0.5, *refs)

    def weights(*refs):
        weight_body(eighth, *refs)

    track_x = swap(track_away, "dp", 2)
    trunk, lower, ilow, ihigh = call(
        fine_back, (track_away, gprev, glow, ghigh, gnext, upper, first, kernels, mixers, inner),
        [((half, channels), F32), ((half, channels), BF), ((half, width), BF), ((half, width), BF)],
        32, after=1,
        scratch=[pltpu.VMEM((channels // 128, quarter, 128), F32)],
    )
    iprev, inext = halo(ilow, ihigh)
    coarse_keep, coarse_send = call(
        weights, (place, ilow, alow, ahigh, gprev, glow, ghigh, gnext, cgated, upper, fold, split), pair,
        32, smem=1, after=1,
    )
    iprev, inext, coarse_send = lax.optimization_barrier((iprev, inext, coarse_send))
    fine_keep, fine_send = call(
        weights, (place, ilow, low, high, iprev, ilow, ihigh, inext, gated, lower, fold, split), pair,
        32, smem=1, after=1,
    )
    fine_send, track_x = lax.optimization_barrier((fine_send, track_x))
    both, readout_total = crossed_sums(fine_keep, fine_send, coarse_keep, coarse_send, track_here, track_x)
    cut = width // windows
    kernel_total, mixer_total = call(
        output_body, (both,),
        [((2, 3, channels // groups, cut), F32), ((2, per, 2 * cut), F32)], 16,
    )
    return (kernel_total, mixer_total, readout_total, trunk[None])


def solution(mesh):
    placed = (
        P("dp", "seq", None, None),
        P("dp", None, None),
        P("dp"),
        P("dp", "seq", None),
        P("dp", None),
        P(),
        P(),
        P(),
    )
    return jax.shard_map(
        shards,
        mesh=mesh,
        in_specs=placed,
        out_specs=(
            P(None, None, "seq", "dp"),
            P(None, "seq", "dp"),
            P("seq", "dp"),
            P("dp", "seq", None),
        ),
        check_vma=False,
    )
```

```python
import math

import jax
import jax.numpy as jnp
import ml_dtypes
import numpy as np
from jax import lax
from jax.experimental import pallas as pl
from jax.experimental.pallas import tpu as pltpu
from jax.sharding import PartitionSpec as P

SPREAD_FINE = 256
SPREAD_COARSE = 128
BF = jnp.bfloat16
F32 = jnp.float32

CHEAP = pl.CostEstimate(flops=1024, bytes_accessed=1024, transcendentals=0)
VMEM = pl.BlockSpec(memory_space=pltpu.VMEM)
SMEM = pl.BlockSpec(memory_space=pltpu.SMEM)
HBM = pl.BlockSpec(memory_space=pltpu.HBM)
ANY = pl.BlockSpec(memory_space=pl.ANY)


def params(mib):
    return pltpu.CompilerParams(vmem_limit_bytes=mib * 1024 * 1024)


def gelu(v):
    return 0.5 * v * (1.0 + lax.erf(v * (1.0 / math.sqrt(2.0))))


def gelu_slope(v):
    cumulative = 0.5 * (1.0 + lax.erf(v * (1.0 / math.sqrt(2.0))))
    density = jnp.exp(-0.5 * v * v) * (1.0 / math.sqrt(2.0 * math.pi))
    return cumulative + v * density


def nn(a, b):
    return jnp.dot(a, b, preferred_element_type=F32)


def nt(a, b):
    return lax.dot_general(a, b, (((1,), (1,)), ((), ())), preferred_element_type=F32)


def tn(a, b):
    return lax.dot_general(a, b, (((0,), (0,)), ((), ())), preferred_element_type=F32)


def call(body, inputs, outs, mib, smem=0, scratch=(), after=0):
    outs = [jax.ShapeDtypeStruct(s, d) for s, d in outs]
    return pl.pallas_call(
        body,
        out_shape=outs,
        in_specs=[SMEM] * smem + [ANY] * after + [VMEM] * (len(inputs) - smem - after),
        out_specs=[VMEM] * len(outs),
        scratch_shapes=list(scratch),
        compiler_params=params(mib),
        cost_estimate=CHEAP,
    )(*inputs)


def product(rows, weights, starts, later, block):
    count, spare = len(weights), len(later)
    row_count = rows.shape[0]
    depth, columns = weights[0].shape
    blocks = [(k, at) for k in range(count) for at in range(0, depth, block)]

    def body(starts_ref, rows_ref, *refs):
        weight_refs, out_ref, later_refs = refs[:count], refs[count], refs[count + 1 : count + 1 + spare]
        held_ref, piece_ref, sems, later_sems = refs[count + 1 + spare :]
        copies = []
        for n, (k, at) in enumerate(blocks):
            start = pl.multiple_of(starts_ref[k] + at, block)
            copies.append((
                pltpu.make_async_copy(rows_ref.at[:, pl.ds(start, block)], held_ref.at[n], sems.at[0, n]),
                pltpu.make_async_copy(weight_refs[k].at[pl.ds(at, block)], piece_ref.at[n], sems.at[1, n]),
            ))
            for copy in copies[-1]:
                copy.start()
        rest = []
        for n in range(spare):
            start = pl.multiple_of(starts_ref[count + n], block)
            rest.append(
                pltpu.make_async_copy(rows_ref.at[:, pl.ds(start, block)], later_refs[n], later_sems.at[n])
            )
            rest[-1].start()
        half = row_count // 2
        for h in range(2):
            part = slice(h * half, (h + 1) * half)
            sums = 0.0
            for n in range(len(blocks)):
                if h == 0:
                    for copy in copies[n]:
                        copy.wait()
                sums = sums + nn(held_ref[n, part], piece_ref[n])
            out_ref[part] = sums
        for copy in rest:
            copy.wait()

    out = [jax.ShapeDtypeStruct((row_count, columns), F32)]
    out += [jax.ShapeDtypeStruct((row_count, block), BF)] * spare
    return pl.pallas_call(
        body,
        out_shape=out,
        in_specs=[SMEM] + [HBM] * (count + 1),
        out_specs=[VMEM] * (1 + spare),
        scratch_shapes=[
            pltpu.VMEM((len(blocks), row_count, block), BF),
            pltpu.VMEM((len(blocks), block, columns), BF),
            pltpu.SemaphoreType.DMA((2, len(blocks))),
            pltpu.SemaphoreType.DMA((spare,)),
        ],
        compiler_params=params(49),
        cost_estimate=CHEAP,
    )(jnp.stack(starts + later).astype(jnp.int32), rows, *weights)


def absorb(total, column, blocks, weights, final):
    count = len(weights)
    row_count = total.shape[0]
    columns = weights[0].shape[1]

    def body(old_ref, *refs):
        out_ref = refs[2 * count]
        half = row_count // 2
        for h in range(2):
            part = slice(h * half, (h + 1) * half)
            sums = old_ref[part, column : column + columns]
            for k in range(count):
                sums = sums + nn(refs[k][part], refs[count + k][...])
            out_ref[part] = sums.astype(out_ref.dtype)

    return call(
        body, (total, *blocks, *weights), [((row_count, columns), BF if final else F32)], 60
    )[0]


def place_body(target_ref, left_ref, right_ref, kernels_ref, hidden_ref, low_ref, high_ref, down_ref, up_ref):
    half = low_ref.shape[0]
    row_count, columns = left_ref.shape
    for h, out in enumerate((low_ref, high_ref)):
        order = lax.broadcasted_iota(jnp.int32, (half, row_count), 0) + h * half
        pick = jnp.where(order == target_ref[...], 1.0, 0.0).astype(BF)
        for n, rows_ref in enumerate((left_ref, right_ref)):
            placed = nn(pick, rows_ref[...])
            cols = slice(n * columns, (n + 1) * columns)
            hidden_ref[h * half : (h + 1) * half, cols] = placed.astype(BF)
            out[:, cols] = gelu(placed).astype(BF)
    down_ref[...] = nn(low_ref[...], kernels_ref[0, 2]).astype(BF)
    up_ref[...] = nn(high_ref[...], kernels_ref[0, 0]).astype(BF)


def local_body(low_ref, high_ref, kernels_ref, inner_ref):
    half = low_ref.shape[0]
    low, high = low_ref[...], high_ref[...]
    inner_ref[:half] = nn(low, kernels_ref[0, 1]) + nn(high, kernels_ref[0, 2])
    inner_ref[half:] = nn(low, kernels_ref[0, 0]) + nn(high, kernels_ref[0, 1])


def fine_body(
    prev_ref, next_ref, local_ref, hidden_ref, kernels_ref, mixers_ref,
    inner_ref, gated_ref, first_ref, alow_ref, ahigh_ref, down_ref, up_ref,
):
    half = prev_ref.shape[0]
    slab = half // 4
    for h, (came, active) in enumerate(((prev_ref, alow_ref), (next_ref, ahigh_ref))):
        inner = local_ref[h * half : (h + 1) * half] + came[...].astype(F32)
        inner_ref[h * half : (h + 1) * half] = inner
        gated = gelu(inner).astype(BF)
        gated_ref[h * half : (h + 1) * half] = gated
        out = hidden_ref[h * half : (h + 1) * half].astype(F32) + nn(gated, mixers_ref[0])
        for s in range(2):
            a = out[2 * s * slab : (2 * s + 1) * slab]
            b = out[(2 * s + 1) * slab : (2 * s + 2) * slab]
            pooled = ((a + b) * 0.5).astype(BF)
            start = h * half // 2 + s * slab
            first_ref[start : start + slab] = pooled
            active[s * slab : (s + 1) * slab] = gelu(pooled.astype(F32)).astype(BF)
    down_ref[...] = nn(alow_ref[...], kernels_ref[1, 2]).astype(BF)
    up_ref[...] = nn(ahigh_ref[...], kernels_ref[1, 0]).astype(BF)


def coarse_body(
    scale, bins_per,
    ids_ref, prev_ref, low_ref, high_ref, next_ref, first_ref, kernels_ref, mixers_ref, readout_ref, targets_ref,
    gated_ref, second_ref, logit_ref, upper_ref, glow_ref, ghigh_ref,
):
    half = low_ref.shape[0]
    slab = half // 2
    slopes = []
    for h, came in enumerate((prev_ref, next_ref)):
        inner = (
            nn(low_ref[...], kernels_ref[1, 1 - h]) + nn(high_ref[...], kernels_ref[1, 2 - h])
            + came[...].astype(F32)
        )
        slopes.append(gelu_slope(inner))
        gated = gelu(inner).astype(BF)
        gated_ref[h * half : (h + 1) * half] = gated
        out = first_ref[h * half : (h + 1) * half].astype(F32) + nn(gated, mixers_ref[1])
        second_ref[h * slab : (h + 1) * slab] = ((out[:slab] + out[slab:]) * 0.5).astype(BF)
    bins = second_ref.shape[0]
    tracks = readout_ref.shape[1]
    width = min(512, tracks)
    bin_ids = ids_ref[0] * bins_per + lax.broadcasted_iota(jnp.int32, (bins, 1), 0)
    weight = jnp.where(bin_ids * 4 < ids_ref[1], scale, 0.0).astype(F32)
    second = second_ref[...]
    upper = jnp.zeros((bins, second.shape[1]), F32)
    for n in range(tracks // width):
        cols = slice(n * width, (n + 1) * width)
        readout = readout_ref[:, cols]
        logits = nn(second, readout)
        small = jnp.exp(-jnp.abs(logits))
        plus = jnp.maximum(logits, 0.0) + jnp.log1p(small)
        gate = jnp.where(logits >= 0.0, 1.0, small) / (1.0 + small)
        grad = (weight * (plus - targets_ref[:, cols].astype(F32)) * gate).astype(BF)
        logit_ref[:, cols] = grad
        upper = upper + nt(grad, readout)
    upper = (upper * 0.5).astype(BF)
    upper_ref[...] = upper
    back = nt(upper, mixers_ref[1])
    for h, out in enumerate((glow_ref, ghigh_ref)):
        piece = back[h * slab : (h + 1) * slab]
        for s in range(2):
            out[s * slab : (s + 1) * slab] = (piece * slopes[h][s * slab : (s + 1) * slab]).astype(BF)


def readout_body(ids_ref, second_ref, logit_ref, keep_ref, send_ref):
    width = keep_ref.shape[2]
    second = second_ref[...]
    for k in range(4):
        start = pl.multiple_of((ids_ref[0] ^ k) * width, width)
        out = send_ref if k & 1 else keep_ref
        out[k >> 1] = tn(second, logit_ref[:, pl.ds(start, width)]).astype(BF)


def store_blocks(ids_ref, pieces, keep_ref, send_ref):
    width = pieces[0].shape[1] // 4
    for d in range(4):
        block = jnp.concatenate([p[:, d * width : (d + 1) * width] for p in pieces], axis=1)
        far = (ids_ref[0] >> 1) ^ (d >> 1)

        @pl.when((ids_ref[0] & 1) == (d & 1))
        def _(block=block, far=far):
            keep_ref[far] = block

        @pl.when((ids_ref[0] & 1) != (d & 1))
        def _(block=block, far=far):
            send_ref[far] = block


def mixer_piece(slab, gated, up, spread_ref, split_ref):
    mixed = 0.0
    for j in range(2):
        left = nn(gated, spread_ref[j]).astype(BF)
        right = nn(up, split_ref[j]).astype(BF)
        rows = []
        for s in range(up.shape[0] // slab):
            rows += [right[s * slab : (s + 1) * slab]] * 2
        mixed = mixed + tn(left, jnp.concatenate(rows, axis=0))
    return mixed.astype(BF)


def weight_body(
    slab, ids_ref, after_ref, low_ref, high_ref, gprev_ref, glow_ref, ghigh_ref, gnext_ref, gated_ref, up_ref,
    spread_ref, split_ref, keep_ref, send_ref,
):
    grads = (gprev_ref, glow_ref, ghigh_ref, gnext_ref)
    pieces = []
    for t in range(3):
        pieces.append((tn(low_ref[...], grads[2 - t][...]) + tn(high_ref[...], grads[3 - t][...])).astype(BF))
    pieces.append(mixer_piece(slab, gated_ref[...], up_ref[...], spread_ref, split_ref))
    store_blocks(ids_ref, pieces, keep_ref, send_ref)


def fine_back_body(
    scale,
    after_ref, gprev_ref, glow_ref, ghigh_ref, gnext_ref, upper_ref, first_ref, kernels_ref, mixers_ref, inner_ref,
    trunk_ref, lower_ref, ilow_ref, ihigh_ref, lanes_ref,
):
    half = glow_ref.shape[0]
    slab = half // 2
    grads = (gprev_ref, glow_ref, ghigh_ref, gnext_ref)
    upper = upper_ref[...].astype(F32)
    for h, out in enumerate((ilow_ref, ihigh_ref)):
        back = (
            nt(grads[h + 2][...], kernels_ref[1, 0])
            + nt(grads[h + 1][...], kernels_ref[1, 1])
            + nt(grads[h][...], kernels_ref[1, 2])
        )
        slope = gelu_slope(first_ref[h * half : (h + 1) * half].astype(F32))
        base = upper[h * slab : (h + 1) * slab]
        total = jnp.concatenate([base, base], axis=0) + back * slope
        for t in range(lanes_ref.shape[0]):
            cols = slice(t * 128, (t + 1) * 128)
            for s in range(2):
                lanes_ref[t, pl.ds(s, slab, stride=2), :] = total[s * slab : (s + 1) * slab, cols] * scale
            trunk_ref[h * half : (h + 1) * half, cols] = lanes_ref[t]
        lower = (total * 0.5).astype(BF)
        lower_ref[h * half : (h + 1) * half] = lower
        inner = nt(lower, mixers_ref[0])
        spread_inner = jnp.concatenate([inner[:slab], inner[:slab], inner[slab:], inner[slab:]], axis=0)
        slope = gelu_slope(inner_ref[2 * h * half : 2 * (h + 1) * half])
        out[...] = (spread_inner * slope).astype(BF)


def output_body(parts_ref, kernels_ref, mixers_ref):
    total = parts_ref[0].astype(F32)
    for g in range(1, parts_ref.shape[0]):
        total = total + parts_ref[g].astype(F32)
    cut, per = kernels_ref.shape[3], mixers_ref.shape[1]
    for n in range(2):
        start = 4 * n * cut
        for t in range(3):
            kernels_ref[n, t] = total[:, start + t * cut : start + (t + 1) * cut]
        tail = total[:, start + 3 * cut : start + 4 * cut]
        mixers_ref[n] = jnp.concatenate([tail[:per], tail[per:]], axis=1)


def swap(value, axis, bit):
    size = lax.axis_size(axis)
    return lax.ppermute(value, axis, [(i, i ^ bit) for i in range(size)])


def halo(low, high):
    size = lax.axis_size("seq")
    up = [(i, i + 1) for i in range(size - 1)]
    return (
        lax.ppermute(high, "seq", up),
        lax.ppermute(low, "seq", [(j, i) for i, j in up]),
    )


def core_sum(keep, send):
    came = swap(send, "dp", 1)
    away = (keep[1].astype(F32) + came[1].astype(F32)).astype(BF)
    here = keep[0].astype(F32) + came[0].astype(F32)
    return here, away


def seq_parts(total):
    groups = lax.axis_size("seq")
    rows, columns = total.shape
    return lax.all_to_all(
        total.reshape(groups, rows // groups, columns), "seq", split_axis=0, concat_axis=0, tiled=True
    )


def far_body(keep_ref, came_ref, away_ref, here_ref):
    away_ref[...] = (keep_ref[1].astype(F32) + came_ref[1].astype(F32)).astype(BF)
    here_ref[...] = keep_ref[0].astype(F32) + came_ref[0].astype(F32)


def side_body(ids_ref, held_ref, came_ref, other_ref, own_ref):
    side = ids_ref[1] & 1
    lead = (slice(None),) * (len(held_ref.shape) - 3)

    def total(at):
        place = (*lead, at)
        return held_ref[place].astype(F32) + came_ref[place].astype(F32)

    other_ref[...] = total(1 - side).astype(BF)
    own_ref[...] = total(side)


def both_body(left_ref, left_came_ref, right_ref, right_came_ref, both_ref):
    columns = left_ref.shape[2]
    both_ref[:, :, :columns] = (left_ref[...] + left_came_ref[...].astype(F32)).astype(BF)
    both_ref[:, :, columns:] = (right_ref[...] + right_came_ref[...].astype(F32)).astype(BF)


def crossed_sums(place, left_keep, left_send, right_keep, right_send, first, first_came):
    groups = lax.axis_size("seq")
    blocks, rows, columns = left_keep.shape
    pairs = (groups // 2, 2, rows // groups, columns)
    half = (groups // 2, rows // groups, columns)
    right_came = swap(right_send, "dp", 1)
    left_came = swap(left_send, "dp", 1)
    other, own = call(
        side_body, (place, right_keep.reshape(blocks, *pairs), right_came.reshape(blocks, *pairs)),
        [((blocks, *half), BF), ((blocks, *half), F32)], 20, smem=1,
    )
    side_came = swap(other, "seq", 1)
    away, here = call(far_body, (left_keep, left_came), [((rows, columns), BF), ((rows, columns), F32)], 20)
    away, first_came = lax.optimization_barrier((away, first_came))
    x_came = swap(away, "dp", 2)
    other, left = call(
        side_body, (place, here.reshape(pairs), x_came.reshape(pairs)), [(half, BF), (half, F32)], 20, smem=1
    )
    left_came = swap(other, "seq", 1)
    away, right = call(far_body, (own, side_came), [(half, BF), (half, F32)], 20)
    right_came = swap(away, "dp", 2)
    both, = call(
        both_body, (left, left_came, right, right_came), [((groups // 2, rows // groups, 2 * columns), BF)], 20
    )
    first = seq_parts((first + first_came.astype(F32)).astype(BF))
    both, first = lax.optimization_barrier((both, first))
    lines = [list(range(start, groups, 2)) for start in range(2)]
    parts = lax.all_to_all(both, "seq", split_axis=0, concat_axis=0, axis_index_groups=lines, tiled=True)
    return parts, first.astype(F32).sum(axis=0)


def shards(embeddings, layout, lengths, targets, projection, kernels, mixers, readout):
    groups = lax.axis_size("seq")
    windows = lax.axis_size("dp")
    me = lax.axis_index("dp")
    device = lax.axis_index("seq")
    rows = embeddings[0, 0]
    row_count = rows.shape[0]
    depth, channels = projection.shape
    width = kernels.shape[3]
    tracks = readout.shape[1]
    half, quarter, eighth = row_count // 2, row_count // 4, row_count // 8
    length = lengths[0]

    side = device % 2
    share = depth // 2
    piece = share // 2
    columns = channels // 2
    block = row_count // groups
    from_core = swap(projection, "dp", 1)
    mine = lax.dynamic_slice_in_dim(projection, side * share, share, axis=0)
    far = [
        [swap(mine[i * piece : (i + 1) * piece, n * columns : (n + 1) * columns], "dp", 2) for i in range(2)]
        for n in range(2)
    ]
    near, away = (me ^ 2) * depth, (me ^ 3) * depth
    later = []
    for i in range(2):
        at, side_at = side * share + i * piece, (1 - side) * share + i * piece
        later += [near + at, away + at, near + side_at, away + side_at]
    total, *blocks = product(rows, [projection, from_core], [me * depth, (me ^ 1) * depth], later, piece)
    weights = []
    for n in range(2):
        for i in range(2):
            held = far[n][i]
            if n == 0 and i == 0:
                held, total = lax.optimization_barrier((held, total))
            crossed = swap(held, "seq", 1)
            weights.append([held, swap(held, "dp", 1), crossed, swap(crossed, "dp", 1)])

    def send(sums):
        return lax.all_to_all(
            sums.reshape(groups, block, columns), "seq", split_axis=0, concat_axis=0, tiled=True
        ).reshape(row_count, columns)

    left = send(absorb(total, 0, blocks, weights[0] + weights[1], True))
    right = absorb(total, columns, blocks[:6], weights[2] + weights[3][:2], False)
    left, last = lax.optimization_barrier((left, weights[3][2]))
    right = send(absorb(right, 0, blocks[6:], [last, weights[3][3]], True))

    column = lax.dynamic_index_in_dim(layout[0], device, axis=1, keepdims=True)
    position = column * block + jnp.arange(block, dtype=jnp.int32)[None, :]
    slot = (position // half) * half + (position % 4) * eighth + (position % half) // 4
    target = jnp.where(device * row_count + position < length, slot, -1).reshape(1, row_count)

    hidden, low, high, down, up = call(
        place_body, (target, left, right, kernels),
        [((row_count, channels), BF), ((half, channels), BF), ((half, channels), BF),
         ((half, width), BF), ((half, width), BF)],
        24,
    )
    fprev, fnext = halo(down, up)
    local, = call(local_body, (low, high, kernels), [((row_count, width), F32)], 24)
    inner, gated, first, alow, ahigh, adown, aup = call(
        fine_body, (fprev, fnext, local, hidden, kernels, mixers),
        [((row_count, width), F32), ((row_count, width), BF), ((half, channels), BF),
         ((quarter, channels), BF), ((quarter, channels), BF), ((quarter, width), BF), ((quarter, width), BF)],
        24,
    )
    aprev, anext = halo(adown, aup)
    bins = quarter
    loss = 2.0 / math.sqrt(windows * groups * bins)
    ids = jnp.stack([device, length]).astype(jnp.int32)
    place = jnp.stack([me, device]).astype(jnp.int32)

    def coarse(*refs):
        coarse_body(loss, bins, *refs)

    cgated, second, logit_grad, upper, glow, ghigh = call(
        coarse, (ids, aprev, alow, ahigh, anext, first, kernels, mixers, readout, targets[0]),
        [((half, width), BF), ((bins, channels), BF), ((bins, tracks), BF), ((bins, channels), BF),
         ((quarter, width), BF), ((quarter, width), BF)],
        32, smem=1,
    )
    gprev, gnext = halo(glow, ghigh)
    track_keep, track_send = call(
        readout_body, (place, second, logit_grad), [((2, channels, tracks // 4), BF)] * 2,
        24, smem=1,
    )
    track_here, track_away = core_sum(track_keep, track_send)
    track_away, gprev, gnext = lax.optimization_barrier((track_away, gprev, gnext))

    per = width // groups
    fold = np.zeros((2, width, channels), ml_dtypes.bfloat16)
    split = np.zeros((2, channels, width), ml_dtypes.bfloat16)
    for j in range(2):
        for a in range(width):
            fold[j, a, (a // per) * 2 * per + j * per + a % per] = 1
        piece_width = width // 4
        for b in range(width):
            split[j, (b // piece_width) * 2 * piece_width + j * piece_width + b % piece_width, b] = 1
    fold, split = jnp.asarray(fold), jnp.asarray(split)
    pair = [((2, channels, width), BF)] * 2

    def fine_back(*refs):
        fine_back_body(math.sqrt(windows * groups * bins) * 0.5, *refs)

    def weights(*refs):
        weight_body(eighth, *refs)

    track_x = swap(track_away, "dp", 2)
    trunk, lower, ilow, ihigh = call(
        fine_back, (track_away, gprev, glow, ghigh, gnext, upper, first, kernels, mixers, inner),
        [((half, channels), F32), ((half, channels), BF), ((half, width), BF), ((half, width), BF)],
        32, after=1,
        scratch=[pltpu.VMEM((channels // 128, quarter, 128), F32)],
    )
    iprev, inext = halo(ilow, ihigh)
    coarse_keep, coarse_send = call(
        weights, (place, ilow, alow, ahigh, gprev, glow, ghigh, gnext, cgated, upper, fold, split), pair,
        32, smem=1, after=1,
    )
    iprev, inext, coarse_send = lax.optimization_barrier((iprev, inext, coarse_send))
    fine_keep, fine_send = call(
        weights, (place, ilow, low, high, iprev, ilow, ihigh, inext, gated, lower, fold, split), pair,
        32, smem=1, after=1,
    )
    fine_send, track_x = lax.optimization_barrier((fine_send, track_x))
    both, readout_total = crossed_sums(
        place, fine_keep, fine_send, coarse_keep, coarse_send, track_here, track_x
    )
    cut = width // windows
    kernel_total, mixer_total = call(
        output_body, (both,),
        [((2, 3, channels // groups, cut), F32), ((2, per, 2 * cut), F32)], 16,
    )
    return (kernel_total, mixer_total, readout_total, trunk[None])


def solution(mesh):
    placed = (
        P("dp", "seq", None, None),
        P("dp", None, None),
        P("dp"),
        P("dp", "seq", None),
        P("dp", None),
        P(),
        P(),
        P(),
    )
    return jax.shard_map(
        shards,
        mesh=mesh,
        in_specs=placed,
        out_specs=(
            P(None, None, "seq", "dp"),
            P(None, "seq", "dp"),
            P("seq", "dp"),
            P("dp", "seq", None),
        ),
        check_vma=False,
    )
```

```python
import math

import jax
import jax.numpy as jnp
import ml_dtypes
import numpy as np
from jax import lax
from jax.experimental import pallas as pl
from jax.experimental.pallas import tpu as pltpu
from jax.sharding import PartitionSpec as P

SPREAD_FINE = 256
SPREAD_COARSE = 128
BF = jnp.bfloat16
F32 = jnp.float32

CHEAP = pl.CostEstimate(flops=1024, bytes_accessed=1024, transcendentals=0)
VMEM = pl.BlockSpec(memory_space=pltpu.VMEM)
SMEM = pl.BlockSpec(memory_space=pltpu.SMEM)
HBM = pl.BlockSpec(memory_space=pltpu.HBM)
ANY = pl.BlockSpec(memory_space=pl.ANY)


def params(mib):
    return pltpu.CompilerParams(vmem_limit_bytes=mib * 1024 * 1024)


def gelu(v):
    return 0.5 * v * (1.0 + lax.erf(v * (1.0 / math.sqrt(2.0))))


def gelu_slope(v):
    cumulative = 0.5 * (1.0 + lax.erf(v * (1.0 / math.sqrt(2.0))))
    density = jnp.exp(-0.5 * v * v) * (1.0 / math.sqrt(2.0 * math.pi))
    return cumulative + v * density


def nn(a, b):
    return jnp.dot(a, b, preferred_element_type=F32)


def nt(a, b):
    return lax.dot_general(a, b, (((1,), (1,)), ((), ())), preferred_element_type=F32)


def tn(a, b):
    return lax.dot_general(a, b, (((0,), (0,)), ((), ())), preferred_element_type=F32)


def call(body, inputs, outs, mib, smem=0, scratch=(), after=0):
    outs = [jax.ShapeDtypeStruct(s, d) for s, d in outs]
    return pl.pallas_call(
        body,
        out_shape=outs,
        in_specs=[SMEM] * smem + [ANY] * after + [VMEM] * (len(inputs) - smem - after),
        out_specs=[VMEM] * len(outs),
        scratch_shapes=list(scratch),
        compiler_params=params(mib),
        cost_estimate=CHEAP,
    )(*inputs)


def product(rows, weights, starts, later, block):
    count, spare = len(weights), len(later)
    row_count = rows.shape[0]
    depth, columns = weights[0].shape
    blocks = [(k, at) for k in range(count) for at in range(0, depth, block)]

    def body(starts_ref, rows_ref, *refs):
        weight_refs, out_ref, later_refs = refs[:count], refs[count], refs[count + 1 : count + 1 + spare]
        held_ref, piece_ref, sems, later_sems = refs[count + 1 + spare :]
        copies = []
        for n, (k, at) in enumerate(blocks):
            start = pl.multiple_of(starts_ref[k] + at, block)
            copies.append((
                pltpu.make_async_copy(rows_ref.at[:, pl.ds(start, block)], held_ref.at[n], sems.at[0, n]),
                pltpu.make_async_copy(weight_refs[k].at[pl.ds(at, block)], piece_ref.at[n], sems.at[1, n]),
            ))
            for copy in copies[-1]:
                copy.start()
        rest = []
        for n in range(spare):
            start = pl.multiple_of(starts_ref[count + n], block)
            rest.append(
                pltpu.make_async_copy(rows_ref.at[:, pl.ds(start, block)], later_refs[n], later_sems.at[n])
            )
            rest[-1].start()
        half = row_count // 2
        for h in range(2):
            part = slice(h * half, (h + 1) * half)
            sums = 0.0
            for n in range(len(blocks)):
                if h == 0:
                    for copy in copies[n]:
                        copy.wait()
                sums = sums + nn(held_ref[n, part], piece_ref[n])
            out_ref[part] = sums
        for copy in rest:
            copy.wait()

    out = [jax.ShapeDtypeStruct((row_count, columns), F32)]
    out += [jax.ShapeDtypeStruct((row_count, block), BF)] * spare
    return pl.pallas_call(
        body,
        out_shape=out,
        in_specs=[SMEM] + [HBM] * (count + 1),
        out_specs=[VMEM] * (1 + spare),
        scratch_shapes=[
            pltpu.VMEM((len(blocks), row_count, block), BF),
            pltpu.VMEM((len(blocks), block, columns), BF),
            pltpu.SemaphoreType.DMA((2, len(blocks))),
            pltpu.SemaphoreType.DMA((spare,)),
        ],
        compiler_params=params(49),
        cost_estimate=CHEAP,
    )(jnp.stack(starts + later).astype(jnp.int32), rows, *weights)


def absorb(total, column, blocks, weights, final, mib):
    count = len(weights)
    row_count = total.shape[0]
    columns = weights[0].shape[1]

    def body(old_ref, *refs):
        out_ref = refs[2 * count]
        half = row_count // 2
        for h in range(2):
            part = slice(h * half, (h + 1) * half)
            sums = old_ref[part, column : column + columns]
            for k in range(count):
                sums = sums + nn(refs[k][part], refs[count + k][...])
            out_ref[part] = sums.astype(out_ref.dtype)

    return call(
        body, (total, *blocks, *weights), [((row_count, columns), BF if final else F32)], mib
    )[0]


def place_body(target_ref, left_ref, right_ref, kernels_ref, hidden_ref, low_ref, high_ref, down_ref, up_ref):
    half = low_ref.shape[0]
    row_count, columns = left_ref.shape
    for h, out in enumerate((low_ref, high_ref)):
        order = lax.broadcasted_iota(jnp.int32, (half, row_count), 0) + h * half
        pick = jnp.where(order == target_ref[...], 1.0, 0.0).astype(BF)
        for n, rows_ref in enumerate((left_ref, right_ref)):
            placed = nn(pick, rows_ref[...])
            cols = slice(n * columns, (n + 1) * columns)
            hidden_ref[h * half : (h + 1) * half, cols] = placed.astype(BF)
            out[:, cols] = gelu(placed).astype(BF)
    down_ref[...] = nn(low_ref[...], kernels_ref[0, 2]).astype(BF)
    up_ref[...] = nn(high_ref[...], kernels_ref[0, 0]).astype(BF)


def local_body(low_ref, high_ref, kernels_ref, inner_ref):
    half = low_ref.shape[0]
    low, high = low_ref[...], high_ref[...]
    inner_ref[:half] = nn(low, kernels_ref[0, 1]) + nn(high, kernels_ref[0, 2])
    inner_ref[half:] = nn(low, kernels_ref[0, 0]) + nn(high, kernels_ref[0, 1])


def fine_body(
    prev_ref, next_ref, local_ref, hidden_ref, kernels_ref, mixers_ref,
    inner_ref, gated_ref, first_ref, alow_ref, ahigh_ref, down_ref, up_ref,
):
    half = prev_ref.shape[0]
    slab = half // 4
    for h, (came, active) in enumerate(((prev_ref, alow_ref), (next_ref, ahigh_ref))):
        inner = local_ref[h * half : (h + 1) * half] + came[...].astype(F32)
        inner_ref[h * half : (h + 1) * half] = inner
        gated = gelu(inner).astype(BF)
        gated_ref[h * half : (h + 1) * half] = gated
        out = hidden_ref[h * half : (h + 1) * half].astype(F32) + nn(gated, mixers_ref[0])
        for s in range(2):
            a = out[2 * s * slab : (2 * s + 1) * slab]
            b = out[(2 * s + 1) * slab : (2 * s + 2) * slab]
            pooled = ((a + b) * 0.5).astype(BF)
            start = h * half // 2 + s * slab
            first_ref[start : start + slab] = pooled
            active[s * slab : (s + 1) * slab] = gelu(pooled.astype(F32)).astype(BF)
    down_ref[...] = nn(alow_ref[...], kernels_ref[1, 2]).astype(BF)
    up_ref[...] = nn(ahigh_ref[...], kernels_ref[1, 0]).astype(BF)


def coarse_body(
    scale, bins_per,
    ids_ref, prev_ref, low_ref, high_ref, next_ref, first_ref, kernels_ref, mixers_ref, readout_ref, targets_ref,
    gated_ref, second_ref, logit_ref, upper_ref, glow_ref, ghigh_ref,
):
    half = low_ref.shape[0]
    slab = half // 2
    slopes = []
    for h, came in enumerate((prev_ref, next_ref)):
        inner = (
            nn(low_ref[...], kernels_ref[1, 1 - h]) + nn(high_ref[...], kernels_ref[1, 2 - h])
            + came[...].astype(F32)
        )
        slopes.append(gelu_slope(inner))
        gated = gelu(inner).astype(BF)
        gated_ref[h * half : (h + 1) * half] = gated
        out = first_ref[h * half : (h + 1) * half].astype(F32) + nn(gated, mixers_ref[1])
        second_ref[h * slab : (h + 1) * slab] = ((out[:slab] + out[slab:]) * 0.5).astype(BF)
    bins = second_ref.shape[0]
    tracks = readout_ref.shape[1]
    width = min(512, tracks)
    bin_ids = ids_ref[0] * bins_per + lax.broadcasted_iota(jnp.int32, (bins, 1), 0)
    weight = jnp.where(bin_ids * 4 < ids_ref[1], scale, 0.0).astype(F32)
    second = second_ref[...]
    upper = jnp.zeros((bins, second.shape[1]), F32)
    for n in range(tracks // width):
        cols = slice(n * width, (n + 1) * width)
        readout = readout_ref[:, cols]
        logits = nn(second, readout)
        small = jnp.exp(-jnp.abs(logits))
        plus = jnp.maximum(logits, 0.0) + jnp.log1p(small)
        gate = jnp.where(logits >= 0.0, 1.0, small) / (1.0 + small)
        grad = (weight * (plus - targets_ref[:, cols].astype(F32)) * gate).astype(BF)
        logit_ref[:, cols] = grad
        upper = upper + nt(grad, readout)
    upper = (upper * 0.5).astype(BF)
    upper_ref[...] = upper
    back = nt(upper, mixers_ref[1])
    for h, out in enumerate((glow_ref, ghigh_ref)):
        piece = back[h * slab : (h + 1) * slab]
        for s in range(2):
            out[s * slab : (s + 1) * slab] = (piece * slopes[h][s * slab : (s + 1) * slab]).astype(BF)


def readout_body(ids_ref, second_ref, logit_ref, keep_ref, send_ref):
    width = keep_ref.shape[2]
    second = second_ref[...]
    for k in range(4):
        start = pl.multiple_of((ids_ref[0] ^ k) * width, width)
        out = send_ref if k & 1 else keep_ref
        out[k >> 1] = tn(second, logit_ref[:, pl.ds(start, width)]).astype(BF)


def store_blocks(ids_ref, pieces, keep_ref, send_ref):
    width = pieces[0].shape[1] // 4
    for d in range(4):
        block = jnp.concatenate([p[:, d * width : (d + 1) * width] for p in pieces], axis=1)
        far = (ids_ref[0] >> 1) ^ (d >> 1)

        @pl.when((ids_ref[0] & 1) == (d & 1))
        def _(block=block, far=far):
            keep_ref[far] = block

        @pl.when((ids_ref[0] & 1) != (d & 1))
        def _(block=block, far=far):
            send_ref[far] = block


def mixer_piece(slab, gated, up, spread_ref, split_ref):
    mixed = 0.0
    for j in range(2):
        left = nn(gated, spread_ref[j]).astype(BF)
        right = nn(up, split_ref[j]).astype(BF)
        rows = []
        for s in range(up.shape[0] // slab):
            rows += [right[s * slab : (s + 1) * slab]] * 2
        mixed = mixed + tn(left, jnp.concatenate(rows, axis=0))
    return mixed.astype(BF)


def weight_body(
    slab, ids_ref, after_ref, low_ref, high_ref, gprev_ref, glow_ref, ghigh_ref, gnext_ref, gated_ref, up_ref,
    spread_ref, split_ref, keep_ref, send_ref,
):
    grads = (gprev_ref, glow_ref, ghigh_ref, gnext_ref)
    pieces = []
    for t in range(3):
        pieces.append((tn(low_ref[...], grads[2 - t][...]) + tn(high_ref[...], grads[3 - t][...])).astype(BF))
    pieces.append(mixer_piece(slab, gated_ref[...], up_ref[...], spread_ref, split_ref))
    store_blocks(ids_ref, pieces, keep_ref, send_ref)


def fine_back_body(
    scale,
    after_ref, gprev_ref, glow_ref, ghigh_ref, gnext_ref, upper_ref, first_ref, kernels_ref, mixers_ref, inner_ref,
    trunk_ref, lower_ref, ilow_ref, ihigh_ref, lanes_ref,
):
    half = glow_ref.shape[0]
    slab = half // 2
    grads = (gprev_ref, glow_ref, ghigh_ref, gnext_ref)
    upper = upper_ref[...].astype(F32)
    for h, out in enumerate((ilow_ref, ihigh_ref)):
        back = (
            nt(grads[h + 2][...], kernels_ref[1, 0])
            + nt(grads[h + 1][...], kernels_ref[1, 1])
            + nt(grads[h][...], kernels_ref[1, 2])
        )
        slope = gelu_slope(first_ref[h * half : (h + 1) * half].astype(F32))
        base = upper[h * slab : (h + 1) * slab]
        total = jnp.concatenate([base, base], axis=0) + back * slope
        for t in range(lanes_ref.shape[0]):
            cols = slice(t * 128, (t + 1) * 128)
            for s in range(2):
                lanes_ref[t, pl.ds(s, slab, stride=2), :] = total[s * slab : (s + 1) * slab, cols] * scale
            trunk_ref[h * half : (h + 1) * half, cols] = lanes_ref[t]
        lower = (total * 0.5).astype(BF)
        lower_ref[h * half : (h + 1) * half] = lower
        inner = nt(lower, mixers_ref[0])
        spread_inner = jnp.concatenate([inner[:slab], inner[:slab], inner[slab:], inner[slab:]], axis=0)
        slope = gelu_slope(inner_ref[2 * h * half : 2 * (h + 1) * half])
        out[...] = (spread_inner * slope).astype(BF)


def output_body(parts_ref, kernels_ref, mixers_ref):
    total = parts_ref[0].astype(F32)
    for g in range(1, parts_ref.shape[0]):
        total = total + parts_ref[g].astype(F32)
    cut, per = kernels_ref.shape[3], mixers_ref.shape[1]
    for n in range(2):
        start = 4 * n * cut
        for t in range(3):
            kernels_ref[n, t] = total[:, start + t * cut : start + (t + 1) * cut]
        tail = total[:, start + 3 * cut : start + 4 * cut]
        mixers_ref[n] = jnp.concatenate([tail[:per], tail[per:]], axis=1)


def swap(value, axis, bit):
    size = lax.axis_size(axis)
    return lax.ppermute(value, axis, [(i, i ^ bit) for i in range(size)])


def halo(low, high):
    size = lax.axis_size("seq")
    up = [(i, i + 1) for i in range(size - 1)]
    return (
        lax.ppermute(high, "seq", up),
        lax.ppermute(low, "seq", [(j, i) for i, j in up]),
    )


def core_sum(keep, send):
    came = swap(send, "dp", 1)
    away = (keep[1].astype(F32) + came[1].astype(F32)).astype(BF)
    here = keep[0].astype(F32) + came[0].astype(F32)
    return here, away


def seq_parts(total):
    groups = lax.axis_size("seq")
    rows, columns = total.shape
    return lax.all_to_all(
        total.reshape(groups, rows // groups, columns), "seq", split_axis=0, concat_axis=0, tiled=True
    )


def side_rows(value, side):
    groups = lax.axis_size("seq")
    *blocks, rows, columns = value.shape
    value = value.reshape(*blocks, groups // 2, 2, rows // groups, columns)
    return lax.dynamic_index_in_dim(value, side, axis=len(blocks) + 1, keepdims=False).astype(F32)


def left_body(ids_ref, keep_ref, came_ref, x_ref, other_ref, own_ref):
    side = ids_ref[1] & 1

    def total(at):
        return keep_ref[0, :, at].astype(F32) + came_ref[0, :, at].astype(F32) + x_ref[:, at].astype(F32)

    other_ref[...] = total(1 - side).astype(BF)
    own_ref[...] = total(side)


def right_body(ids_ref, keep_ref, came_ref, side_ref, away_ref, here_ref):
    side = ids_ref[1] & 1

    def total(at):
        return keep_ref[at, :, side].astype(F32) + came_ref[at, :, side].astype(F32) + side_ref[at].astype(F32)

    away_ref[...] = total(1).astype(BF)
    here_ref[...] = total(0)


def both_body(left_ref, left_came_ref, right_ref, right_came_ref, both_ref):
    columns = left_ref.shape[2]
    both_ref[:, :, :columns] = (left_ref[...] + left_came_ref[...].astype(F32)).astype(BF)
    both_ref[:, :, columns:] = (right_ref[...] + right_came_ref[...].astype(F32)).astype(BF)


def crossed_sums(place, left_keep, left_send, right_keep, right_send, first, first_came):
    groups = lax.axis_size("seq")
    side = lax.axis_index("seq") % 2
    blocks, rows, columns = left_keep.shape
    pairs = (groups // 2, 2, rows // groups, columns)
    half = (groups // 2, rows // groups, columns)
    right_came = swap(right_send, "dp", 1)
    left_came = swap(left_send, "dp", 1)
    left_away = (left_keep[1].astype(F32) + left_came[1].astype(F32)).astype(BF)
    left_away, first_came = lax.optimization_barrier((left_away, first_came))
    x_came = swap(left_away, "dp", 2)
    other = side_rows(right_keep, 1 - side) + side_rows(right_came, 1 - side)
    side_came = swap(other.astype(BF), "seq", 1)

    def split(value):
        return value.reshape(blocks, *pairs)

    other, left = call(
        left_body, (place, split(left_keep), split(left_came), x_came.reshape(pairs)),
        [(half, BF), (half, F32)], 20, smem=1,
    )
    left_came = swap(other, "seq", 1)
    away, right = call(
        right_body, (place, split(right_keep), split(right_came), side_came), [(half, BF), (half, F32)], 20, smem=1
    )
    right_came = swap(away, "dp", 2)
    both, = call(
        both_body, (left, left_came, right, right_came), [((groups // 2, rows // groups, 2 * columns), BF)], 20
    )
    first = seq_parts((first + first_came.astype(F32)).astype(BF))
    both, first = lax.optimization_barrier((both, first))
    lines = [list(range(start, groups, 2)) for start in range(2)]
    parts = lax.all_to_all(both, "seq", split_axis=0, concat_axis=0, axis_index_groups=lines, tiled=True)
    return parts, first.astype(F32).sum(axis=0)


def shards(embeddings, layout, lengths, targets, projection, kernels, mixers, readout):
    groups = lax.axis_size("seq")
    windows = lax.axis_size("dp")
    me = lax.axis_index("dp")
    device = lax.axis_index("seq")
    rows = embeddings[0, 0]
    row_count = rows.shape[0]
    depth, channels = projection.shape
    width = kernels.shape[3]
    tracks = readout.shape[1]
    half, quarter, eighth = row_count // 2, row_count // 4, row_count // 8
    length = lengths[0]

    side = device % 2
    share = depth // 2
    piece = share // 2
    columns = channels // 2
    block = row_count // groups
    from_core = swap(projection, "dp", 1)
    mine = lax.dynamic_slice_in_dim(projection, side * share, share, axis=0)
    far = [
        [swap(mine[i * piece : (i + 1) * piece, n * columns : (n + 1) * columns], "dp", 2) for i in range(2)]
        for n in range(2)
    ]
    near, away = (me ^ 2) * depth, (me ^ 3) * depth
    later = []
    for i in range(2):
        at, side_at = side * share + i * piece, (1 - side) * share + i * piece
        later += [near + at, away + at, near + side_at, away + side_at]
    total, *blocks = product(rows, [projection, from_core], [me * depth, (me ^ 1) * depth], later, piece)
    weights = []
    for n in range(2):
        for i in range(2):
            held = far[n][i]
            if n == 0 and i == 0:
                held, total = lax.optimization_barrier((held, total))
            crossed = swap(held, "seq", 1)
            weights.append([held, swap(held, "dp", 1), crossed, swap(crossed, "dp", 1)])

    def send(sums):
        return lax.all_to_all(
            sums.reshape(groups, block, columns), "seq", split_axis=0, concat_axis=0, tiled=True
        ).reshape(row_count, columns)

    left = send(absorb(total, 0, blocks, weights[0] + weights[1], True, 20))
    right = absorb(total, columns, blocks[:6], weights[2] + weights[3][:2], False, 20)
    right = send(absorb(right, 0, blocks[6:], weights[3][2:], True, 60))

    column = lax.dynamic_index_in_dim(layout[0], device, axis=1, keepdims=True)
    position = column * block + jnp.arange(block, dtype=jnp.int32)[None, :]
    slot = (position // half) * half + (position % 4) * eighth + (position % half) // 4
    target = jnp.where(device * row_count + position < length, slot, -1).reshape(1, row_count)

    hidden, low, high, down, up = call(
        place_body, (target, left, right, kernels),
        [((row_count, channels), BF), ((half, channels), BF), ((half, channels), BF),
         ((half, width), BF), ((half, width), BF)],
        24,
    )
    fprev, fnext = halo(down, up)
    local, = call(local_body, (low, high, kernels), [((row_count, width), F32)], 24)
    inner, gated, first, alow, ahigh, adown, aup = call(
        fine_body, (fprev, fnext, local, hidden, kernels, mixers),
        [((row_count, width), F32), ((row_count, width), BF), ((half, channels), BF),
         ((quarter, channels), BF), ((quarter, channels), BF), ((quarter, width), BF), ((quarter, width), BF)],
        24,
    )
    aprev, anext = halo(adown, aup)
    bins = quarter
    loss = 2.0 / math.sqrt(windows * groups * bins)
    ids = jnp.stack([device, length]).astype(jnp.int32)
    place = jnp.stack([me, device]).astype(jnp.int32)

    def coarse(*refs):
        coarse_body(loss, bins, *refs)

    cgated, second, logit_grad, upper, glow, ghigh = call(
        coarse, (ids, aprev, alow, ahigh, anext, first, kernels, mixers, readout, targets[0]),
        [((half, width), BF), ((bins, channels), BF), ((bins, tracks), BF), ((bins, channels), BF),
         ((quarter, width), BF), ((quarter, width), BF)],
        32, smem=1,
    )
    gprev, gnext = halo(glow, ghigh)
    track_keep, track_send = call(
        readout_body, (place, second, logit_grad), [((2, channels, tracks // 4), BF)] * 2,
        24, smem=1,
    )
    track_here, track_away = core_sum(track_keep, track_send)
    track_away, gprev, gnext = lax.optimization_barrier((track_away, gprev, gnext))

    per = width // groups
    fold = np.zeros((2, width, channels), ml_dtypes.bfloat16)
    split = np.zeros((2, channels, width), ml_dtypes.bfloat16)
    for j in range(2):
        for a in range(width):
            fold[j, a, (a // per) * 2 * per + j * per + a % per] = 1
        piece_width = width // 4
        for b in range(width):
            split[j, (b // piece_width) * 2 * piece_width + j * piece_width + b % piece_width, b] = 1
    fold, split = jnp.asarray(fold), jnp.asarray(split)
    pair = [((2, channels, width), BF)] * 2

    def fine_back(*refs):
        fine_back_body(math.sqrt(windows * groups * bins) * 0.5, *refs)

    def weights(*refs):
        weight_body(eighth, *refs)

    track_x = swap(track_away, "dp", 2)
    trunk, lower, ilow, ihigh = call(
        fine_back, (track_away, gprev, glow, ghigh, gnext, upper, first, kernels, mixers, inner),
        [((half, channels), F32), ((half, channels), BF), ((half, width), BF), ((half, width), BF)],
        32, after=1,
        scratch=[pltpu.VMEM((channels // 128, quarter, 128), F32)],
    )
    iprev, inext = halo(ilow, ihigh)
    coarse_keep, coarse_send = call(
        weights, (place, ilow, alow, ahigh, gprev, glow, ghigh, gnext, cgated, upper, fold, split), pair,
        32, smem=1, after=1,
    )
    iprev, inext, coarse_send = lax.optimization_barrier((iprev, inext, coarse_send))
    fine_keep, fine_send = call(
        weights, (place, ilow, low, high, iprev, ilow, ihigh, inext, gated, lower, fold, split), pair,
        32, smem=1, after=1,
    )
    fine_send, track_x = lax.optimization_barrier((fine_send, track_x))
    both, readout_total = crossed_sums(
        place, fine_keep, fine_send, coarse_keep, coarse_send, track_here, track_x
    )
    cut = width // windows
    kernel_total, mixer_total = call(
        output_body, (both,),
        [((2, 3, channels // groups, cut), F32), ((2, per, 2 * cut), F32)], 16,
    )
    return (kernel_total, mixer_total, readout_total, trunk[None])


def solution(mesh):
    placed = (
        P("dp", "seq", None, None),
        P("dp", None, None),
        P("dp"),
        P("dp", "seq", None),
        P("dp", None),
        P(),
        P(),
        P(),
    )
    return jax.shard_map(
        shards,
        mesh=mesh,
        in_specs=placed,
        out_specs=(
            P(None, None, "seq", "dp"),
            P(None, "seq", "dp"),
            P("seq", "dp"),
            P("dp", "seq", None),
        ),
        check_vma=False,
    )
```

```python
import math

import jax
import jax.numpy as jnp
import ml_dtypes
import numpy as np
from jax import lax
from jax.experimental import pallas as pl
from jax.experimental.pallas import tpu as pltpu
from jax.sharding import PartitionSpec as P

SPREAD_FINE = 256
SPREAD_COARSE = 128
BF = jnp.bfloat16
F32 = jnp.float32

CHEAP = pl.CostEstimate(flops=1024, bytes_accessed=1024, transcendentals=0)
VMEM = pl.BlockSpec(memory_space=pltpu.VMEM)
SMEM = pl.BlockSpec(memory_space=pltpu.SMEM)
HBM = pl.BlockSpec(memory_space=pltpu.HBM)
ANY = pl.BlockSpec(memory_space=pl.ANY)


def params(mib):
    return pltpu.CompilerParams(vmem_limit_bytes=mib * 1024 * 1024)


def gelu(v):
    return 0.5 * v * (1.0 + lax.erf(v * (1.0 / math.sqrt(2.0))))


def gelu_slope(v):
    cumulative = 0.5 * (1.0 + lax.erf(v * (1.0 / math.sqrt(2.0))))
    density = jnp.exp(-0.5 * v * v) * (1.0 / math.sqrt(2.0 * math.pi))
    return cumulative + v * density


def nn(a, b):
    return jnp.dot(a, b, preferred_element_type=F32)


def nt(a, b):
    return lax.dot_general(a, b, (((1,), (1,)), ((), ())), preferred_element_type=F32)


def tn(a, b):
    return lax.dot_general(a, b, (((0,), (0,)), ((), ())), preferred_element_type=F32)


def call(body, inputs, outs, mib, smem=0, scratch=(), after=0):
    outs = [jax.ShapeDtypeStruct(s, d) for s, d in outs]
    return pl.pallas_call(
        body,
        out_shape=outs,
        in_specs=[SMEM] * smem + [ANY] * after + [VMEM] * (len(inputs) - smem - after),
        out_specs=[VMEM] * len(outs),
        scratch_shapes=list(scratch),
        compiler_params=params(mib),
        cost_estimate=CHEAP,
    )(*inputs)


def product(rows, weights, starts, later, block):
    count, spare = len(weights), len(later)
    row_count = rows.shape[0]
    depth, columns = weights[0].shape
    blocks = [(k, at) for k in range(count) for at in range(0, depth, block)]

    def body(starts_ref, rows_ref, *refs):
        weight_refs, out_ref, later_refs = refs[:count], refs[count], refs[count + 1 : count + 1 + spare]
        held_ref, piece_ref, sems, later_sems = refs[count + 1 + spare :]
        copies = []
        for n, (k, at) in enumerate(blocks):
            start = pl.multiple_of(starts_ref[k] + at, block)
            copies.append((
                pltpu.make_async_copy(
                    rows_ref.at[:, pl.ds(start, block)], held_ref.at[:, pl.ds(n * block, block)], sems.at[0, n]
                ),
                pltpu.make_async_copy(
                    weight_refs[k].at[pl.ds(at, block)], piece_ref.at[pl.ds(n * block, block)], sems.at[1, n]
                ),
            ))
            for copy in copies[-1]:
                copy.start()
        rest = []
        for n in range(spare):
            start = pl.multiple_of(starts_ref[count + n], block)
            rest.append(
                pltpu.make_async_copy(rows_ref.at[:, pl.ds(start, block)], later_refs[n], later_sems.at[n])
            )
            rest[-1].start()
        half = row_count // 2
        for h in range(2):
            part = slice(h * half, (h + 1) * half)
            sums = 0.0
            for k in range(count):
                if h == 0:
                    for n in range(len(blocks)):
                        if blocks[n][0] == k:
                            for copy in copies[n]:
                                copy.wait()
                span = slice(k * depth, (k + 1) * depth)
                sums = sums + nn(held_ref[part, span], piece_ref[span])
            out_ref[part] = sums
        for copy in rest:
            copy.wait()

    out = [jax.ShapeDtypeStruct((row_count, columns), F32)]
    out += [jax.ShapeDtypeStruct((row_count, block), BF)] * spare
    return pl.pallas_call(
        body,
        out_shape=out,
        in_specs=[SMEM] + [HBM] * (count + 1),
        out_specs=[VMEM] * (1 + spare),
        scratch_shapes=[
            pltpu.VMEM((row_count, count * depth), BF),
            pltpu.VMEM((count * depth, columns), BF),
            pltpu.SemaphoreType.DMA((2, len(blocks))),
            pltpu.SemaphoreType.DMA((spare,)),
        ],
        compiler_params=params(49),
        cost_estimate=CHEAP,
    )(jnp.stack(starts + later).astype(jnp.int32), rows, *weights)


def absorb(total, column, blocks, weights, mib):
    count = len(weights)
    row_count = total.shape[0]
    columns = weights[0].shape[1]

    def body(old_ref, *refs):
        out_ref = refs[2 * count]
        half = row_count // 2
        for h in range(2):
            part = slice(h * half, (h + 1) * half)
            sums = old_ref[part, column : column + columns]
            for k in range(count):
                sums = sums + nn(refs[k][part], refs[count + k][...])
            out_ref[part] = sums.astype(BF)

    return call(
        body, (total, *blocks, *weights), [((row_count, columns), BF)], mib
    )[0]


def place_body(target_ref, left_ref, right_ref, kernels_ref, hidden_ref, low_ref, high_ref, down_ref, up_ref):
    half = low_ref.shape[0]
    row_count, columns = left_ref.shape
    for h, out in enumerate((low_ref, high_ref)):
        order = lax.broadcasted_iota(jnp.int32, (half, row_count), 0) + h * half
        pick = jnp.where(order == target_ref[...], 1.0, 0.0).astype(BF)
        for n, rows_ref in enumerate((left_ref, right_ref)):
            placed = nn(pick, rows_ref[...])
            cols = slice(n * columns, (n + 1) * columns)
            hidden_ref[h * half : (h + 1) * half, cols] = placed.astype(BF)
            out[:, cols] = gelu(placed).astype(BF)
    down_ref[...] = nn(low_ref[...], kernels_ref[0, 2]).astype(BF)
    up_ref[...] = nn(high_ref[...], kernels_ref[0, 0]).astype(BF)


def local_body(low_ref, high_ref, kernels_ref, inner_ref):
    half = low_ref.shape[0]
    low, high = low_ref[...], high_ref[...]
    inner_ref[:half] = nn(low, kernels_ref[0, 1]) + nn(high, kernels_ref[0, 2])
    inner_ref[half:] = nn(low, kernels_ref[0, 0]) + nn(high, kernels_ref[0, 1])


def fine_body(
    prev_ref, next_ref, local_ref, hidden_ref, kernels_ref, mixers_ref,
    inner_ref, gated_ref, first_ref, alow_ref, ahigh_ref, down_ref, up_ref,
):
    half = prev_ref.shape[0]
    slab = half // 4
    for h, (came, active) in enumerate(((prev_ref, alow_ref), (next_ref, ahigh_ref))):
        inner = local_ref[h * half : (h + 1) * half] + came[...].astype(F32)
        inner_ref[h * half : (h + 1) * half] = inner
        gated = gelu(inner).astype(BF)
        gated_ref[h * half : (h + 1) * half] = gated
        out = hidden_ref[h * half : (h + 1) * half].astype(F32) + nn(gated, mixers_ref[0])
        for s in range(2):
            a = out[2 * s * slab : (2 * s + 1) * slab]
            b = out[(2 * s + 1) * slab : (2 * s + 2) * slab]
            pooled = ((a + b) * 0.5).astype(BF)
            start = h * half // 2 + s * slab
            first_ref[start : start + slab] = pooled
            active[s * slab : (s + 1) * slab] = gelu(pooled.astype(F32)).astype(BF)
    down_ref[...] = nn(alow_ref[...], kernels_ref[1, 2]).astype(BF)
    up_ref[...] = nn(ahigh_ref[...], kernels_ref[1, 0]).astype(BF)


def coarse_body(
    scale, bins_per,
    ids_ref, prev_ref, low_ref, high_ref, next_ref, first_ref, kernels_ref, mixers_ref, readout_ref, targets_ref,
    gated_ref, second_ref, logit_ref, upper_ref, glow_ref, ghigh_ref,
):
    half = low_ref.shape[0]
    slab = half // 2
    slopes = []
    for h, came in enumerate((prev_ref, next_ref)):
        inner = (
            nn(low_ref[...], kernels_ref[1, 1 - h]) + nn(high_ref[...], kernels_ref[1, 2 - h])
            + came[...].astype(F32)
        )
        slopes.append(gelu_slope(inner))
        gated = gelu(inner).astype(BF)
        gated_ref[h * half : (h + 1) * half] = gated
        out = first_ref[h * half : (h + 1) * half].astype(F32) + nn(gated, mixers_ref[1])
        second_ref[h * slab : (h + 1) * slab] = ((out[:slab] + out[slab:]) * 0.5).astype(BF)
    bins = second_ref.shape[0]
    tracks = readout_ref.shape[1]
    width = min(512, tracks)
    bin_ids = ids_ref[0] * bins_per + lax.broadcasted_iota(jnp.int32, (bins, 1), 0)
    weight = jnp.where(bin_ids * 4 < ids_ref[1], scale, 0.0).astype(F32)
    second = second_ref[...]
    upper = jnp.zeros((bins, second.shape[1]), F32)
    for n in range(tracks // width):
        cols = slice(n * width, (n + 1) * width)
        readout = readout_ref[:, cols]
        logits = nn(second, readout)
        small = jnp.exp(-jnp.abs(logits))
        plus = jnp.maximum(logits, 0.0) + jnp.log1p(small)
        gate = jnp.where(logits >= 0.0, 1.0, small) / (1.0 + small)
        grad = (weight * (plus - targets_ref[:, cols].astype(F32)) * gate).astype(BF)
        logit_ref[:, cols] = grad
        upper = upper + nt(grad, readout)
    upper = (upper * 0.5).astype(BF)
    upper_ref[...] = upper
    back = nt(upper, mixers_ref[1])
    for h, out in enumerate((glow_ref, ghigh_ref)):
        piece = back[h * slab : (h + 1) * slab]
        for s in range(2):
            out[s * slab : (s + 1) * slab] = (piece * slopes[h][s * slab : (s + 1) * slab]).astype(BF)


def readout_body(ids_ref, second_ref, logit_ref, keep_ref, send_ref):
    width = keep_ref.shape[2]
    second = second_ref[...]
    for k in range(4):
        start = pl.multiple_of((ids_ref[0] ^ k) * width, width)
        out = send_ref if k & 1 else keep_ref
        out[k >> 1] = tn(second, logit_ref[:, pl.ds(start, width)]).astype(BF)


def store_blocks(ids_ref, pieces, keep_ref, send_ref):
    width = pieces[0].shape[1] // 4
    for d in range(4):
        block = jnp.concatenate([p[:, d * width : (d + 1) * width] for p in pieces], axis=1)
        far = (ids_ref[0] >> 1) ^ (d >> 1)

        @pl.when((ids_ref[0] & 1) == (d & 1))
        def _(block=block, far=far):
            keep_ref[far] = block

        @pl.when((ids_ref[0] & 1) != (d & 1))
        def _(block=block, far=far):
            send_ref[far] = block


def mixer_piece(slab, gated, up, spread_ref, split_ref):
    mixed = 0.0
    for j in range(2):
        left = nn(gated, spread_ref[j]).astype(BF)
        right = nn(up, split_ref[j]).astype(BF)
        rows = []
        for s in range(up.shape[0] // slab):
            rows += [right[s * slab : (s + 1) * slab]] * 2
        mixed = mixed + tn(left, jnp.concatenate(rows, axis=0))
    return mixed.astype(BF)


def weight_body(
    slab, ids_ref, after_ref, low_ref, high_ref, gprev_ref, glow_ref, ghigh_ref, gnext_ref, gated_ref, up_ref,
    spread_ref, split_ref, keep_ref, send_ref,
):
    grads = (gprev_ref, glow_ref, ghigh_ref, gnext_ref)
    pieces = []
    for t in range(3):
        pieces.append((tn(low_ref[...], grads[2 - t][...]) + tn(high_ref[...], grads[3 - t][...])).astype(BF))
    pieces.append(mixer_piece(slab, gated_ref[...], up_ref[...], spread_ref, split_ref))
    store_blocks(ids_ref, pieces, keep_ref, send_ref)


def fine_back_body(
    scale,
    after_ref, gprev_ref, glow_ref, ghigh_ref, gnext_ref, upper_ref, first_ref, kernels_ref, mixers_ref, inner_ref,
    trunk_ref, lower_ref, ilow_ref, ihigh_ref, lanes_ref,
):
    half = glow_ref.shape[0]
    slab = half // 2
    grads = (gprev_ref, glow_ref, ghigh_ref, gnext_ref)
    upper = upper_ref[...].astype(F32)
    for h, out in enumerate((ilow_ref, ihigh_ref)):
        back = (
            nt(grads[h + 2][...], kernels_ref[1, 0])
            + nt(grads[h + 1][...], kernels_ref[1, 1])
            + nt(grads[h][...], kernels_ref[1, 2])
        )
        slope = gelu_slope(first_ref[h * half : (h + 1) * half].astype(F32))
        base = upper[h * slab : (h + 1) * slab]
        total = jnp.concatenate([base, base], axis=0) + back * slope
        for t in range(lanes_ref.shape[0]):
            cols = slice(t * 128, (t + 1) * 128)
            for s in range(2):
                lanes_ref[t, pl.ds(s, slab, stride=2), :] = total[s * slab : (s + 1) * slab, cols] * scale
            trunk_ref[h * half : (h + 1) * half, cols] = lanes_ref[t]
        lower = (total * 0.5).astype(BF)
        lower_ref[h * half : (h + 1) * half] = lower
        inner = nt(lower, mixers_ref[0])
        spread_inner = jnp.concatenate([inner[:slab], inner[:slab], inner[slab:], inner[slab:]], axis=0)
        slope = gelu_slope(inner_ref[2 * h * half : 2 * (h + 1) * half])
        out[...] = (spread_inner * slope).astype(BF)


def output_body(parts_ref, kernels_ref, mixers_ref):
    total = parts_ref[0].astype(F32)
    for g in range(1, parts_ref.shape[0]):
        total = total + parts_ref[g].astype(F32)
    cut, per = kernels_ref.shape[3], mixers_ref.shape[1]
    for n in range(2):
        start = 4 * n * cut
        for t in range(3):
            kernels_ref[n, t] = total[:, start + t * cut : start + (t + 1) * cut]
        tail = total[:, start + 3 * cut : start + 4 * cut]
        mixers_ref[n] = jnp.concatenate([tail[:per], tail[per:]], axis=1)


def swap(value, axis, bit):
    size = lax.axis_size(axis)
    return lax.ppermute(value, axis, [(i, i ^ bit) for i in range(size)])


def halo(low, high):
    size = lax.axis_size("seq")
    up = [(i, i + 1) for i in range(size - 1)]
    return (
        lax.ppermute(high, "seq", up),
        lax.ppermute(low, "seq", [(j, i) for i, j in up]),
    )


def core_sum(keep, send):
    came = swap(send, "dp", 1)
    away = (keep[1].astype(F32) + came[1].astype(F32)).astype(BF)
    here = keep[0].astype(F32) + came[0].astype(F32)
    return here, away


def seq_parts(total):
    groups = lax.axis_size("seq")
    rows, columns = total.shape
    return lax.all_to_all(
        total.reshape(groups, rows // groups, columns), "seq", split_axis=0, concat_axis=0, tiled=True
    )


def side_rows(value, side):
    groups = lax.axis_size("seq")
    *blocks, rows, columns = value.shape
    value = value.reshape(*blocks, groups // 2, 2, rows // groups, columns)
    return lax.dynamic_index_in_dim(value, side, axis=len(blocks) + 1, keepdims=False).astype(F32)


def crossed_sums(left_keep, left_send, right_keep, right_send, first, first_came):
    groups = lax.axis_size("seq")
    side = lax.axis_index("seq") % 2
    right_came = swap(right_send, "dp", 1)
    left_came = swap(left_send, "dp", 1)
    left_away = (left_keep[1].astype(F32) + left_came[1].astype(F32)).astype(BF)
    left_away, first_came = lax.optimization_barrier((left_away, first_came))
    x_came = swap(left_away, "dp", 2)
    other = side_rows(right_keep, 1 - side) + side_rows(right_came, 1 - side)
    side_came = swap(other.astype(BF), "seq", 1)

    def left_half(at):
        return side_rows(left_keep[0], at) + side_rows(left_came[0], at) + side_rows(x_came, at)

    def right_half(at):
        return side_rows(right_keep[at], side) + side_rows(right_came[at], side) + side_came[at].astype(F32)

    left = swap(left_half(1 - side).astype(BF), "seq", 1)
    right = swap(right_half(1).astype(BF), "dp", 2)
    left = left_half(side) + left.astype(F32)
    right = right_half(0) + right.astype(F32)
    both = jnp.concatenate([left, right], axis=2).astype(BF)
    first = seq_parts((first + first_came.astype(F32)).astype(BF))
    both, first = lax.optimization_barrier((both, first))
    lines = [list(range(start, groups, 2)) for start in range(2)]
    parts = lax.all_to_all(both, "seq", split_axis=0, concat_axis=0, axis_index_groups=lines, tiled=True)
    return parts, first.astype(F32).sum(axis=0)


def shards(embeddings, layout, lengths, targets, projection, kernels, mixers, readout):
    groups = lax.axis_size("seq")
    windows = lax.axis_size("dp")
    me = lax.axis_index("dp")
    device = lax.axis_index("seq")
    rows = embeddings[0, 0]
    row_count = rows.shape[0]
    depth, channels = projection.shape
    width = kernels.shape[3]
    tracks = readout.shape[1]
    half, quarter, eighth = row_count // 2, row_count // 4, row_count // 8
    length = lengths[0]

    side = device % 2
    share = depth // 2
    piece = share // 2
    columns = channels // 2
    block = row_count // groups
    from_core = swap(projection, "dp", 1)
    mine = lax.dynamic_slice_in_dim(projection, side * share, share, axis=0)
    far = [
        [swap(mine[i * piece : (i + 1) * piece, n * columns : (n + 1) * columns], "dp", 2) for i in range(2)]
        for n in range(2)
    ]
    near, away = (me ^ 2) * depth, (me ^ 3) * depth
    later = []
    for i in range(2):
        at, side_at = side * share + i * piece, (1 - side) * share + i * piece
        later += [near + at, away + at, near + side_at, away + side_at]
    total, *blocks = product(rows, [projection, from_core], [me * depth, (me ^ 1) * depth], later, piece)
    weights = []
    for n in range(2):
        for i in range(2):
            held = far[n][i]
            if n == 0 and i == 0:
                held, total = lax.optimization_barrier((held, total))
            crossed = swap(held, "seq", 1)
            weights.append([held, swap(held, "dp", 1), crossed, swap(crossed, "dp", 1)])

    def send(sums):
        return lax.all_to_all(
            sums.reshape(groups, block, columns), "seq", split_axis=0, concat_axis=0, tiled=True
        ).reshape(row_count, columns)

    left = send(absorb(total, 0, blocks, weights[0] + weights[1], 20))
    left, last = lax.optimization_barrier((left, weights[3][2]))
    right = send(absorb(total, columns, blocks, weights[2] + weights[3][:2] + [last, weights[3][3]], 60))

    column = lax.dynamic_index_in_dim(layout[0], device, axis=1, keepdims=True)
    position = column * block + jnp.arange(block, dtype=jnp.int32)[None, :]
    slot = (position // half) * half + (position % 4) * eighth + (position % half) // 4
    target = jnp.where(device * row_count + position < length, slot, -1).reshape(1, row_count)

    hidden, low, high, down, up = call(
        place_body, (target, left, right, kernels),
        [((row_count, channels), BF), ((half, channels), BF), ((half, channels), BF),
         ((half, width), BF), ((half, width), BF)],
        24,
    )
    fprev, fnext = halo(down, up)
    local, = call(local_body, (low, high, kernels), [((row_count, width), F32)], 24)
    inner, gated, first, alow, ahigh, adown, aup = call(
        fine_body, (fprev, fnext, local, hidden, kernels, mixers),
        [((row_count, width), F32), ((row_count, width), BF), ((half, channels), BF),
         ((quarter, channels), BF), ((quarter, channels), BF), ((quarter, width), BF), ((quarter, width), BF)],
        24,
    )
    aprev, anext = halo(adown, aup)
    bins = quarter
    loss = 2.0 / math.sqrt(windows * groups * bins)
    ids = jnp.stack([device, length]).astype(jnp.int32)
    place = jnp.stack([me, device]).astype(jnp.int32)

    def coarse(*refs):
        coarse_body(loss, bins, *refs)

    cgated, second, logit_grad, upper, glow, ghigh = call(
        coarse, (ids, aprev, alow, ahigh, anext, first, kernels, mixers, readout, targets[0]),
        [((half, width), BF), ((bins, channels), BF), ((bins, tracks), BF), ((bins, channels), BF),
         ((quarter, width), BF), ((quarter, width), BF)],
        32, smem=1,
    )
    gprev, gnext = halo(glow, ghigh)
    track_keep, track_send = call(
        readout_body, (place, second, logit_grad), [((2, channels, tracks // 4), BF)] * 2,
        24, smem=1,
    )
    track_here, track_away = core_sum(track_keep, track_send)
    track_away, gprev, gnext = lax.optimization_barrier((track_away, gprev, gnext))

    per = width // groups
    fold = np.zeros((2, width, channels), ml_dtypes.bfloat16)
    split = np.zeros((2, channels, width), ml_dtypes.bfloat16)
    for j in range(2):
        for a in range(width):
            fold[j, a, (a // per) * 2 * per + j * per + a % per] = 1
        piece_width = width // 4
        for b in range(width):
            split[j, (b // piece_width) * 2 * piece_width + j * piece_width + b % piece_width, b] = 1
    fold, split = jnp.asarray(fold), jnp.asarray(split)
    pair = [((2, channels, width), BF)] * 2

    def fine_back(*refs):
        fine_back_body(math.sqrt(windows * groups * bins) * 0.5, *refs)

    def weights(*refs):
        weight_body(eighth, *refs)

    track_x = swap(track_away, "dp", 2)
    trunk, lower, ilow, ihigh = call(
        fine_back, (track_away, gprev, glow, ghigh, gnext, upper, first, kernels, mixers, inner),
        [((half, channels), F32), ((half, channels), BF), ((half, width), BF), ((half, width), BF)],
        32, after=1,
        scratch=[pltpu.VMEM((channels // 128, quarter, 128), F32)],
    )
    iprev, inext = halo(ilow, ihigh)
    coarse_keep, coarse_send = call(
        weights, (place, ilow, alow, ahigh, gprev, glow, ghigh, gnext, cgated, upper, fold, split), pair,
        32, smem=1, after=1,
    )
    iprev, inext, coarse_send = lax.optimization_barrier((iprev, inext, coarse_send))
    fine_keep, fine_send = call(
        weights, (place, ilow, low, high, iprev, ilow, ihigh, inext, gated, lower, fold, split), pair,
        32, smem=1, after=1,
    )
    fine_send, track_x = lax.optimization_barrier((fine_send, track_x))
    both, readout_total = crossed_sums(fine_keep, fine_send, coarse_keep, coarse_send, track_here, track_x)
    cut = width // windows
    kernel_total, mixer_total = call(
        output_body, (both,),
        [((2, 3, channels // groups, cut), F32), ((2, per, 2 * cut), F32)], 16,
    )
    return (kernel_total, mixer_total, readout_total, trunk[None])


def solution(mesh):
    placed = (
        P("dp", "seq", None, None),
        P("dp", None, None),
        P("dp"),
        P("dp", "seq", None),
        P("dp", None),
        P(),
        P(),
        P(),
    )
    return jax.shard_map(
        shards,
        mesh=mesh,
        in_specs=placed,
        out_specs=(
            P(None, None, "seq", "dp"),
            P(None, "seq", "dp"),
            P("seq", "dp"),
            P("dp", "seq", None),
        ),
        check_vma=False,
    )
```

```python
import math

import jax
import jax.numpy as jnp
import ml_dtypes
import numpy as np
from jax import lax
from jax.experimental import pallas as pl
from jax.experimental.pallas import tpu as pltpu
from jax.sharding import PartitionSpec as P

SPREAD_FINE = 256
SPREAD_COARSE = 128
BF = jnp.bfloat16
F32 = jnp.float32

CHEAP = pl.CostEstimate(flops=1024, bytes_accessed=1024, transcendentals=0)
VMEM = pl.BlockSpec(memory_space=pltpu.VMEM)
SMEM = pl.BlockSpec(memory_space=pltpu.SMEM)
HBM = pl.BlockSpec(memory_space=pltpu.HBM)
ANY = pl.BlockSpec(memory_space=pl.ANY)


def params(mib):
    return pltpu.CompilerParams(vmem_limit_bytes=mib * 1024 * 1024)


def gelu(v):
    return 0.5 * v * (1.0 + lax.erf(v * (1.0 / math.sqrt(2.0))))


def gelu_slope(v):
    cumulative = 0.5 * (1.0 + lax.erf(v * (1.0 / math.sqrt(2.0))))
    density = jnp.exp(-0.5 * v * v) * (1.0 / math.sqrt(2.0 * math.pi))
    return cumulative + v * density


def nn(a, b):
    return jnp.dot(a, b, preferred_element_type=F32)


def nt(a, b):
    return lax.dot_general(a, b, (((1,), (1,)), ((), ())), preferred_element_type=F32)


def tn(a, b):
    return lax.dot_general(a, b, (((0,), (0,)), ((), ())), preferred_element_type=F32)


def call(body, inputs, outs, mib, smem=0, scratch=(), after=0):
    outs = [jax.ShapeDtypeStruct(s, d) for s, d in outs]
    return pl.pallas_call(
        body,
        out_shape=outs,
        in_specs=[SMEM] * smem + [ANY] * after + [VMEM] * (len(inputs) - smem - after),
        out_specs=[VMEM] * len(outs),
        scratch_shapes=list(scratch),
        compiler_params=params(mib),
        cost_estimate=CHEAP,
    )(*inputs)


def product(rows, weights, starts, later, block):
    count, spare = len(weights), len(later)
    row_count = rows.shape[0]
    depth, columns = weights[0].shape
    blocks = [(k, at) for k in range(count) for at in range(0, depth, block)]

    def body(starts_ref, rows_ref, *refs):
        weight_refs, out_ref, later_refs = refs[:count], refs[count], refs[count + 1 : count + 1 + spare]
        held_ref, piece_ref, sems, later_sems = refs[count + 1 + spare :]
        copies = []
        for n, (k, at) in enumerate(blocks):
            start = pl.multiple_of(starts_ref[k] + at, block)
            copies.append((
                pltpu.make_async_copy(
                    rows_ref.at[:, pl.ds(start, block)], held_ref.at[:, pl.ds(n * block, block)], sems.at[0, n]
                ),
                pltpu.make_async_copy(
                    weight_refs[k].at[pl.ds(at, block)], piece_ref.at[pl.ds(n * block, block)], sems.at[1, n]
                ),
            ))
            for copy in copies[-1]:
                copy.start()
        rest = []
        for n in range(spare):
            start = pl.multiple_of(starts_ref[count + n], block)
            rest.append(
                pltpu.make_async_copy(rows_ref.at[:, pl.ds(start, block)], later_refs[n], later_sems.at[n])
            )
            rest[-1].start()
        half = row_count // 2
        for h in range(2):
            part = slice(h * half, (h + 1) * half)
            sums = 0.0
            for k in range(count):
                if h == 0:
                    for n in range(len(blocks)):
                        if blocks[n][0] == k:
                            for copy in copies[n]:
                                copy.wait()
                span = slice(k * depth, (k + 1) * depth)
                sums = sums + nn(held_ref[part, span], piece_ref[span])
            out_ref[part] = sums
        for copy in rest:
            copy.wait()

    out = [jax.ShapeDtypeStruct((row_count, columns), F32)]
    out += [jax.ShapeDtypeStruct((row_count, block), BF)] * spare
    return pl.pallas_call(
        body,
        out_shape=out,
        in_specs=[SMEM] + [HBM] * (count + 1),
        out_specs=[VMEM] * (1 + spare),
        scratch_shapes=[
            pltpu.VMEM((row_count, count * depth), BF),
            pltpu.VMEM((count * depth, columns), BF),
            pltpu.SemaphoreType.DMA((2, len(blocks))),
            pltpu.SemaphoreType.DMA((spare,)),
        ],
        compiler_params=params(49),
        cost_estimate=CHEAP,
    )(jnp.stack(starts + later).astype(jnp.int32), rows, *weights)


def absorb(total, column, blocks, weights, mib):
    count = len(weights)
    row_count = total.shape[0]
    columns = weights[0].shape[1]

    def body(old_ref, *refs):
        out_ref = refs[2 * count]
        half = row_count // 2
        for h in range(2):
            part = slice(h * half, (h + 1) * half)
            sums = old_ref[part, column : column + columns]
            for k in range(count):
                sums = sums + nn(refs[k][part], refs[count + k][...])
            out_ref[part] = sums.astype(BF)

    return call(
        body, (total, *blocks, *weights), [((row_count, columns), BF)], mib
    )[0]


def place_body(target_ref, left_ref, right_ref, kernels_ref, hidden_ref, low_ref, high_ref, down_ref, up_ref):
    half = low_ref.shape[0]
    row_count, columns = left_ref.shape
    for h, out in enumerate((low_ref, high_ref)):
        order = lax.broadcasted_iota(jnp.int32, (half, row_count), 0) + h * half
        pick = jnp.where(order == target_ref[...], 1.0, 0.0).astype(BF)
        for n, rows_ref in enumerate((left_ref, right_ref)):
            placed = nn(pick, rows_ref[...])
            cols = slice(n * columns, (n + 1) * columns)
            hidden_ref[h * half : (h + 1) * half, cols] = placed.astype(BF)
            out[:, cols] = gelu(placed).astype(BF)
    down_ref[...] = nn(low_ref[...], kernels_ref[0, 2]).astype(BF)
    up_ref[...] = nn(high_ref[...], kernels_ref[0, 0]).astype(BF)


def local_body(low_ref, high_ref, kernels_ref, inner_ref):
    half = low_ref.shape[0]
    low, high = low_ref[...], high_ref[...]
    inner_ref[:half] = nn(low, kernels_ref[0, 1]) + nn(high, kernels_ref[0, 2])
    inner_ref[half:] = nn(low, kernels_ref[0, 0]) + nn(high, kernels_ref[0, 1])


def fine_body(
    prev_ref, next_ref, local_ref, hidden_ref, kernels_ref, mixers_ref,
    inner_ref, gated_ref, first_ref, alow_ref, ahigh_ref, down_ref, up_ref,
):
    half = prev_ref.shape[0]
    slab = half // 4
    for h, (came, active) in enumerate(((prev_ref, alow_ref), (next_ref, ahigh_ref))):
        inner = local_ref[h * half : (h + 1) * half] + came[...].astype(F32)
        inner_ref[h * half : (h + 1) * half] = inner
        gated = gelu(inner).astype(BF)
        gated_ref[h * half : (h + 1) * half] = gated
        out = hidden_ref[h * half : (h + 1) * half].astype(F32) + nn(gated, mixers_ref[0])
        for s in range(2):
            a = out[2 * s * slab : (2 * s + 1) * slab]
            b = out[(2 * s + 1) * slab : (2 * s + 2) * slab]
            pooled = ((a + b) * 0.5).astype(BF)
            start = h * half // 2 + s * slab
            first_ref[start : start + slab] = pooled
            active[s * slab : (s + 1) * slab] = gelu(pooled.astype(F32)).astype(BF)
    down_ref[...] = nn(alow_ref[...], kernels_ref[1, 2]).astype(BF)
    up_ref[...] = nn(ahigh_ref[...], kernels_ref[1, 0]).astype(BF)


def coarse_body(
    scale, bins_per,
    ids_ref, prev_ref, low_ref, high_ref, next_ref, first_ref, kernels_ref, mixers_ref, readout_ref, targets_ref,
    gated_ref, second_ref, logit_ref, upper_ref, glow_ref, ghigh_ref,
):
    half = low_ref.shape[0]
    slab = half // 2
    slopes = []
    for h, came in enumerate((prev_ref, next_ref)):
        inner = (
            nn(low_ref[...], kernels_ref[1, 1 - h]) + nn(high_ref[...], kernels_ref[1, 2 - h])
            + came[...].astype(F32)
        )
        slopes.append(gelu_slope(inner))
        gated = gelu(inner).astype(BF)
        gated_ref[h * half : (h + 1) * half] = gated
        out = first_ref[h * half : (h + 1) * half].astype(F32) + nn(gated, mixers_ref[1])
        second_ref[h * slab : (h + 1) * slab] = ((out[:slab] + out[slab:]) * 0.5).astype(BF)
    bins = second_ref.shape[0]
    tracks = readout_ref.shape[1]
    width = min(512, tracks)
    bin_ids = ids_ref[0] * bins_per + lax.broadcasted_iota(jnp.int32, (bins, 1), 0)
    weight = jnp.where(bin_ids * 4 < ids_ref[1], scale, 0.0).astype(F32)
    second = second_ref[...]
    upper = jnp.zeros((bins, second.shape[1]), F32)
    for n in range(tracks // width):
        cols = slice(n * width, (n + 1) * width)
        readout = readout_ref[:, cols]
        logits = nn(second, readout)
        small = jnp.exp(-jnp.abs(logits))
        plus = jnp.maximum(logits, 0.0) + jnp.log1p(small)
        gate = jnp.where(logits >= 0.0, 1.0, small) / (1.0 + small)
        grad = (weight * (plus - targets_ref[:, cols].astype(F32)) * gate).astype(BF)
        logit_ref[:, cols] = grad
        upper = upper + nt(grad, readout)
    upper = (upper * 0.5).astype(BF)
    upper_ref[...] = upper
    back = nt(upper, mixers_ref[1])
    for h, out in enumerate((glow_ref, ghigh_ref)):
        piece = back[h * slab : (h + 1) * slab]
        for s in range(2):
            out[s * slab : (s + 1) * slab] = (piece * slopes[h][s * slab : (s + 1) * slab]).astype(BF)


def readout_body(ids_ref, second_ref, logit_ref, keep_ref, send_ref):
    width = keep_ref.shape[2]
    second = second_ref[...]
    for k in range(4):
        start = pl.multiple_of((ids_ref[0] ^ k) * width, width)
        out = send_ref if k & 1 else keep_ref
        out[k >> 1] = tn(second, logit_ref[:, pl.ds(start, width)]).astype(BF)


def store_blocks(ids_ref, pieces, keep_ref, send_ref):
    width = pieces[0].shape[1] // 4
    for d in range(4):
        block = jnp.concatenate([p[:, d * width : (d + 1) * width] for p in pieces], axis=1)
        far = (ids_ref[0] >> 1) ^ (d >> 1)

        @pl.when((ids_ref[0] & 1) == (d & 1))
        def _(block=block, far=far):
            keep_ref[far] = block

        @pl.when((ids_ref[0] & 1) != (d & 1))
        def _(block=block, far=far):
            send_ref[far] = block


def mixer_piece(slab, gated, up, spread_ref, split_ref):
    mixed = 0.0
    for j in range(2):
        left = nn(gated, spread_ref[j]).astype(BF)
        right = nn(up, split_ref[j]).astype(BF)
        rows = []
        for s in range(up.shape[0] // slab):
            rows += [right[s * slab : (s + 1) * slab]] * 2
        mixed = mixed + tn(left, jnp.concatenate(rows, axis=0))
    return mixed.astype(BF)


def weight_body(
    slab, ids_ref, after_ref, low_ref, high_ref, gprev_ref, glow_ref, ghigh_ref, gnext_ref, gated_ref, up_ref,
    spread_ref, split_ref, keep_ref, send_ref,
):
    grads = (gprev_ref, glow_ref, ghigh_ref, gnext_ref)
    pieces = []
    for t in range(3):
        pieces.append((tn(low_ref[...], grads[2 - t][...]) + tn(high_ref[...], grads[3 - t][...])).astype(BF))
    pieces.append(mixer_piece(slab, gated_ref[...], up_ref[...], spread_ref, split_ref))
    store_blocks(ids_ref, pieces, keep_ref, send_ref)


def fine_back_body(
    scale,
    after_ref, gprev_ref, glow_ref, ghigh_ref, gnext_ref, upper_ref, first_ref, kernels_ref, mixers_ref, inner_ref,
    trunk_ref, lower_ref, ilow_ref, ihigh_ref, lanes_ref,
):
    half = glow_ref.shape[0]
    slab = half // 2
    grads = (gprev_ref, glow_ref, ghigh_ref, gnext_ref)
    upper = upper_ref[...].astype(F32)
    for h, out in enumerate((ilow_ref, ihigh_ref)):
        back = (
            nt(grads[h + 2][...], kernels_ref[1, 0])
            + nt(grads[h + 1][...], kernels_ref[1, 1])
            + nt(grads[h][...], kernels_ref[1, 2])
        )
        slope = gelu_slope(first_ref[h * half : (h + 1) * half].astype(F32))
        base = upper[h * slab : (h + 1) * slab]
        total = jnp.concatenate([base, base], axis=0) + back * slope
        for t in range(lanes_ref.shape[0]):
            cols = slice(t * 128, (t + 1) * 128)
            for s in range(2):
                lanes_ref[t, pl.ds(s, slab, stride=2), :] = total[s * slab : (s + 1) * slab, cols] * scale
            trunk_ref[h * half : (h + 1) * half, cols] = lanes_ref[t]
        lower = (total * 0.5).astype(BF)
        lower_ref[h * half : (h + 1) * half] = lower
        inner = nt(lower, mixers_ref[0])
        spread_inner = jnp.concatenate([inner[:slab], inner[:slab], inner[slab:], inner[slab:]], axis=0)
        slope = gelu_slope(inner_ref[2 * h * half : 2 * (h + 1) * half])
        out[...] = (spread_inner * slope).astype(BF)


def output_body(parts_ref, kernels_ref, mixers_ref):
    total = parts_ref[0].astype(F32)
    for g in range(1, parts_ref.shape[0]):
        total = total + parts_ref[g].astype(F32)
    cut, per = kernels_ref.shape[3], mixers_ref.shape[1]
    for n in range(2):
        start = 4 * n * cut
        for t in range(3):
            kernels_ref[n, t] = total[:, start + t * cut : start + (t + 1) * cut]
        tail = total[:, start + 3 * cut : start + 4 * cut]
        mixers_ref[n] = jnp.concatenate([tail[:per], tail[per:]], axis=1)


def swap(value, axis, bit):
    size = lax.axis_size(axis)
    return lax.ppermute(value, axis, [(i, i ^ bit) for i in range(size)])


def halo(low, high):
    size = lax.axis_size("seq")
    up = [(i, i + 1) for i in range(size - 1)]
    return (
        lax.ppermute(high, "seq", up),
        lax.ppermute(low, "seq", [(j, i) for i, j in up]),
    )


def core_sum(keep, send):
    came = swap(send, "dp", 1)
    away = (keep[1].astype(F32) + came[1].astype(F32)).astype(BF)
    here = keep[0].astype(F32) + came[0].astype(F32)
    return here, away


def seq_parts(total):
    groups = lax.axis_size("seq")
    rows, columns = total.shape
    return lax.all_to_all(
        total.reshape(groups, rows // groups, columns), "seq", split_axis=0, concat_axis=0, tiled=True
    )


def side_rows(value, side):
    groups = lax.axis_size("seq")
    *blocks, rows, columns = value.shape
    value = value.reshape(*blocks, groups // 2, 2, rows // groups, columns)
    return lax.dynamic_index_in_dim(value, side, axis=len(blocks) + 1, keepdims=False).astype(F32)


def crossed_sums(left_keep, left_send, right_keep, right_send, first, first_came):
    groups = lax.axis_size("seq")
    side = lax.axis_index("seq") % 2
    right_came = swap(right_send, "dp", 1)
    left_came = swap(left_send, "dp", 1)
    left_away = (left_keep[1].astype(F32) + left_came[1].astype(F32)).astype(BF)
    left_away, first_came = lax.optimization_barrier((left_away, first_came))
    x_came = swap(left_away, "dp", 2)
    other = side_rows(right_keep, 1 - side) + side_rows(right_came, 1 - side)
    side_came = swap(other.astype(BF), "seq", 1)

    def left_half(at):
        return side_rows(left_keep[0], at) + side_rows(left_came[0], at) + side_rows(x_came, at)

    def right_half(at):
        return side_rows(right_keep[at], side) + side_rows(right_came[at], side) + side_came[at].astype(F32)

    left = swap(left_half(1 - side).astype(BF), "seq", 1)
    right = swap(right_half(1).astype(BF), "dp", 2)
    left = left_half(side) + left.astype(F32)
    right = right_half(0) + right.astype(F32)
    both = jnp.concatenate([left, right], axis=2).astype(BF)
    first = seq_parts((first + first_came.astype(F32)).astype(BF))
    both, first = lax.optimization_barrier((both, first))
    lines = [list(range(start, groups, 2)) for start in range(2)]
    parts = lax.all_to_all(both, "seq", split_axis=0, concat_axis=0, axis_index_groups=lines, tiled=True)
    return parts, first.astype(F32).sum(axis=0)


def shards(embeddings, layout, lengths, targets, projection, kernels, mixers, readout):
    groups = lax.axis_size("seq")
    windows = lax.axis_size("dp")
    me = lax.axis_index("dp")
    device = lax.axis_index("seq")
    rows = embeddings[0, 0]
    row_count = rows.shape[0]
    depth, channels = projection.shape
    width = kernels.shape[3]
    tracks = readout.shape[1]
    half, quarter, eighth = row_count // 2, row_count // 4, row_count // 8
    length = lengths[0]

    side = device % 2
    share = depth // 2
    piece = share // 2
    columns = channels // 2
    block = row_count // groups
    from_core = swap(projection, "dp", 1)
    mine = lax.dynamic_slice_in_dim(projection, side * share, share, axis=0)
    far = [
        [swap(mine[i * piece : (i + 1) * piece, n * columns : (n + 1) * columns], "dp", 2) for i in range(2)]
        for n in range(2)
    ]
    extra = lax.dynamic_slice(projection, ((1 - side) * share + piece, columns), (piece, columns))
    extra = swap(extra, "dp", 2)
    near, away = (me ^ 2) * depth, (me ^ 3) * depth
    later = []
    for i in range(2):
        at, side_at = side * share + i * piece, (1 - side) * share + i * piece
        later += [near + at, away + at, near + side_at, away + side_at]
    total, *blocks = product(rows, [projection, from_core], [me * depth, (me ^ 1) * depth], later, piece)
    weights = []
    for n in range(2):
        for i in range(2):
            held = far[n][i]
            if n == 0 and i == 0:
                held, total = lax.optimization_barrier((held, total))
            crossed = extra if n == 1 and i == 1 else swap(held, "seq", 1)
            weights.append([held, swap(held, "dp", 1), crossed, swap(crossed, "dp", 1)])

    def send(sums):
        return lax.all_to_all(
            sums.reshape(groups, block, columns), "seq", split_axis=0, concat_axis=0, tiled=True
        ).reshape(row_count, columns)

    left = absorb(total, 0, blocks, weights[0] + weights[1], 20)
    left, weights[3][3] = lax.optimization_barrier((left, weights[3][3]))
    left = send(left)
    right = absorb(total, columns, blocks, weights[2] + weights[3], 60)
    left, right = lax.optimization_barrier((left, right))
    right = send(right)

    column = lax.dynamic_index_in_dim(layout[0], device, axis=1, keepdims=True)
    position = column * block + jnp.arange(block, dtype=jnp.int32)[None, :]
    slot = (position // half) * half + (position % 4) * eighth + (position % half) // 4
    target = jnp.where(device * row_count + position < length, slot, -1).reshape(1, row_count)

    hidden, low, high, down, up = call(
        place_body, (target, left, right, kernels),
        [((row_count, channels), BF), ((half, channels), BF), ((half, channels), BF),
         ((half, width), BF), ((half, width), BF)],
        24,
    )
    fprev, fnext = halo(down, up)
    local, = call(local_body, (low, high, kernels), [((row_count, width), F32)], 24)
    inner, gated, first, alow, ahigh, adown, aup = call(
        fine_body, (fprev, fnext, local, hidden, kernels, mixers),
        [((row_count, width), F32), ((row_count, width), BF), ((half, channels), BF),
         ((quarter, channels), BF), ((quarter, channels), BF), ((quarter, width), BF), ((quarter, width), BF)],
        24,
    )
    aprev, anext = halo(adown, aup)
    bins = quarter
    loss = 2.0 / math.sqrt(windows * groups * bins)
    ids = jnp.stack([device, length]).astype(jnp.int32)
    place = jnp.stack([me, device]).astype(jnp.int32)

    def coarse(*refs):
        coarse_body(loss, bins, *refs)

    cgated, second, logit_grad, upper, glow, ghigh = call(
        coarse, (ids, aprev, alow, ahigh, anext, first, kernels, mixers, readout, targets[0]),
        [((half, width), BF), ((bins, channels), BF), ((bins, tracks), BF), ((bins, channels), BF),
         ((quarter, width), BF), ((quarter, width), BF)],
        32, smem=1,
    )
    gprev, gnext = halo(glow, ghigh)
    track_keep, track_send = call(
        readout_body, (place, second, logit_grad), [((2, channels, tracks // 4), BF)] * 2,
        24, smem=1,
    )
    track_here, track_away = core_sum(track_keep, track_send)
    track_away, gprev, gnext = lax.optimization_barrier((track_away, gprev, gnext))

    per = width // groups
    fold = np.zeros((2, width, channels), ml_dtypes.bfloat16)
    split = np.zeros((2, channels, width), ml_dtypes.bfloat16)
    for j in range(2):
        for a in range(width):
            fold[j, a, (a // per) * 2 * per + j * per + a % per] = 1
        piece_width = width // 4
        for b in range(width):
            split[j, (b // piece_width) * 2 * piece_width + j * piece_width + b % piece_width, b] = 1
    fold, split = jnp.asarray(fold), jnp.asarray(split)
    pair = [((2, channels, width), BF)] * 2

    def fine_back(*refs):
        fine_back_body(math.sqrt(windows * groups * bins) * 0.5, *refs)

    def weights(*refs):
        weight_body(eighth, *refs)

    track_x = swap(track_away, "dp", 2)
    trunk, lower, ilow, ihigh = call(
        fine_back, (track_away, gprev, glow, ghigh, gnext, upper, first, kernels, mixers, inner),
        [((half, channels), F32), ((half, channels), BF), ((half, width), BF), ((half, width), BF)],
        32, after=1,
        scratch=[pltpu.VMEM((channels // 128, quarter, 128), F32)],
    )
    iprev, inext = halo(ilow, ihigh)
    coarse_keep, coarse_send = call(
        weights, (place, ilow, alow, ahigh, gprev, glow, ghigh, gnext, cgated, upper, fold, split), pair,
        32, smem=1, after=1,
    )
    iprev, inext, coarse_send = lax.optimization_barrier((iprev, inext, coarse_send))
    fine_keep, fine_send = call(
        weights, (place, ilow, low, high, iprev, ilow, ihigh, inext, gated, lower, fold, split), pair,
        32, smem=1, after=1,
    )
    fine_send, track_x = lax.optimization_barrier((fine_send, track_x))
    both, readout_total = crossed_sums(fine_keep, fine_send, coarse_keep, coarse_send, track_here, track_x)
    cut = width // windows
    kernel_total, mixer_total = call(
        output_body, (both,),
        [((2, 3, channels // groups, cut), F32), ((2, per, 2 * cut), F32)], 16,
    )
    return (kernel_total, mixer_total, readout_total, trunk[None])


def solution(mesh):
    placed = (
        P("dp", "seq", None, None),
        P("dp", None, None),
        P("dp"),
        P("dp", "seq", None),
        P("dp", None),
        P(),
        P(),
        P(),
    )
    return jax.shard_map(
        shards,
        mesh=mesh,
        in_specs=placed,
        out_specs=(
            P(None, None, "seq", "dp"),
            P(None, "seq", "dp"),
            P("seq", "dp"),
            P("dp", "seq", None),
        ),
        check_vma=False,
    )
```

```python
import math

import jax
import jax.numpy as jnp
import ml_dtypes
import numpy as np
from jax import lax
from jax.experimental import pallas as pl
from jax.experimental.pallas import tpu as pltpu
from jax.sharding import PartitionSpec as P

SPREAD_FINE = 256
SPREAD_COARSE = 128
BF = jnp.bfloat16
F32 = jnp.float32

CHEAP = pl.CostEstimate(flops=1024, bytes_accessed=1024, transcendentals=0)
VMEM = pl.BlockSpec(memory_space=pltpu.VMEM)
SMEM = pl.BlockSpec(memory_space=pltpu.SMEM)
HBM = pl.BlockSpec(memory_space=pltpu.HBM)
ANY = pl.BlockSpec(memory_space=pl.ANY)


def params(mib):
    return pltpu.CompilerParams(vmem_limit_bytes=mib * 1024 * 1024)


def gelu(v):
    return 0.5 * v * (1.0 + lax.erf(v * (1.0 / math.sqrt(2.0))))


def gelu_slope(v):
    cumulative = 0.5 * (1.0 + lax.erf(v * (1.0 / math.sqrt(2.0))))
    density = jnp.exp(-0.5 * v * v) * (1.0 / math.sqrt(2.0 * math.pi))
    return cumulative + v * density


def nn(a, b):
    return jnp.dot(a, b, preferred_element_type=F32)


def nt(a, b):
    return lax.dot_general(a, b, (((1,), (1,)), ((), ())), preferred_element_type=F32)


def tn(a, b):
    return lax.dot_general(a, b, (((0,), (0,)), ((), ())), preferred_element_type=F32)


def call(body, inputs, outs, mib, smem=0, scratch=(), after=0):
    outs = [jax.ShapeDtypeStruct(s, d) for s, d in outs]
    return pl.pallas_call(
        body,
        out_shape=outs,
        in_specs=[SMEM] * smem + [ANY] * after + [VMEM] * (len(inputs) - smem - after),
        out_specs=[VMEM] * len(outs),
        scratch_shapes=list(scratch),
        compiler_params=params(mib),
        cost_estimate=CHEAP,
    )(*inputs)


def product(rows, weights, starts, later, block):
    count, spare = len(weights), len(later)
    row_count = rows.shape[0]
    depth, columns = weights[0].shape
    blocks = [(k, at) for k in range(count) for at in range(0, depth, block)]

    def body(starts_ref, rows_ref, *refs):
        weight_refs, out_ref, later_refs = refs[:count], refs[count], refs[count + 1 : count + 1 + spare]
        held_ref, piece_ref, sems, later_sems = refs[count + 1 + spare :]
        copies = []
        for n, (k, at) in enumerate(blocks):
            start = pl.multiple_of(starts_ref[k] + at, block)
            copies.append((
                pltpu.make_async_copy(
                    rows_ref.at[:, pl.ds(start, block)], held_ref.at[:, pl.ds(n * block, block)], sems.at[0, n]
                ),
                pltpu.make_async_copy(
                    weight_refs[k].at[pl.ds(at, block)], piece_ref.at[pl.ds(n * block, block)], sems.at[1, n]
                ),
            ))
            for copy in copies[-1]:
                copy.start()
        rest = []
        for n in range(spare):
            start = pl.multiple_of(starts_ref[count + n], block)
            rest.append(
                pltpu.make_async_copy(rows_ref.at[:, pl.ds(start, block)], later_refs[n], later_sems.at[n])
            )
            rest[-1].start()
        half = row_count // 2
        for h in range(2):
            part = slice(h * half, (h + 1) * half)
            sums = 0.0
            for k in range(count):
                if h == 0:
                    for n in range(len(blocks)):
                        if blocks[n][0] == k:
                            for copy in copies[n]:
                                copy.wait()
                span = slice(k * depth, (k + 1) * depth)
                sums = sums + nn(held_ref[part, span], piece_ref[span])
            out_ref[part] = sums
        for copy in rest:
            copy.wait()

    out = [jax.ShapeDtypeStruct((row_count, columns), F32)]
    out += [jax.ShapeDtypeStruct((row_count, block), BF)] * spare
    return pl.pallas_call(
        body,
        out_shape=out,
        in_specs=[SMEM] + [HBM] * (count + 1),
        out_specs=[VMEM] * (1 + spare),
        scratch_shapes=[
            pltpu.VMEM((row_count, count * depth), BF),
            pltpu.VMEM((count * depth, columns), BF),
            pltpu.SemaphoreType.DMA((2, len(blocks))),
            pltpu.SemaphoreType.DMA((spare,)),
        ],
        compiler_params=params(49),
        cost_estimate=CHEAP,
    )(jnp.stack(starts + later).astype(jnp.int32), rows, *weights)


def absorb(total, column, blocks, weights, mib):
    count = len(weights)
    row_count = total.shape[0]
    columns = weights[0].shape[1]

    def body(old_ref, *refs):
        out_ref = refs[2 * count]
        half = row_count // 2
        for h in range(2):
            part = slice(h * half, (h + 1) * half)
            sums = old_ref[part, column : column + columns]
            for k in range(count):
                sums = sums + nn(refs[k][part], refs[count + k][...])
            out_ref[part] = sums.astype(BF)

    return call(
        body, (total, *blocks, *weights), [((row_count, columns), BF)], mib
    )[0]


def place_body(target_ref, left_ref, right_ref, kernels_ref, hidden_ref, low_ref, high_ref, down_ref, up_ref):
    half = low_ref.shape[0]
    row_count, columns = left_ref.shape
    for h, out in enumerate((low_ref, high_ref)):
        order = lax.broadcasted_iota(jnp.int32, (half, row_count), 0) + h * half
        pick = jnp.where(order == target_ref[...], 1.0, 0.0).astype(BF)
        for n, rows_ref in enumerate((left_ref, right_ref)):
            placed = nn(pick, rows_ref[...])
            cols = slice(n * columns, (n + 1) * columns)
            hidden_ref[h * half : (h + 1) * half, cols] = placed.astype(BF)
            out[:, cols] = gelu(placed).astype(BF)
    down_ref[...] = nn(low_ref[...], kernels_ref[0, 2]).astype(BF)
    up_ref[...] = nn(high_ref[...], kernels_ref[0, 0]).astype(BF)


def local_body(low_ref, high_ref, kernels_ref, inner_ref):
    half = low_ref.shape[0]
    low, high = low_ref[...], high_ref[...]
    inner_ref[:half] = nn(low, kernels_ref[0, 1]) + nn(high, kernels_ref[0, 2])
    inner_ref[half:] = nn(low, kernels_ref[0, 0]) + nn(high, kernels_ref[0, 1])


def fine_body(
    prev_ref, next_ref, local_ref, hidden_ref, kernels_ref, mixers_ref,
    inner_ref, gated_ref, first_ref, alow_ref, ahigh_ref, down_ref, up_ref,
):
    half = prev_ref.shape[0]
    slab = half // 4
    for h, (came, active) in enumerate(((prev_ref, alow_ref), (next_ref, ahigh_ref))):
        inner = local_ref[h * half : (h + 1) * half] + came[...].astype(F32)
        inner_ref[h * half : (h + 1) * half] = inner
        gated = gelu(inner).astype(BF)
        gated_ref[h * half : (h + 1) * half] = gated
        out = hidden_ref[h * half : (h + 1) * half].astype(F32) + nn(gated, mixers_ref[0])
        for s in range(2):
            a = out[2 * s * slab : (2 * s + 1) * slab]
            b = out[(2 * s + 1) * slab : (2 * s + 2) * slab]
            pooled = ((a + b) * 0.5).astype(BF)
            start = h * half // 2 + s * slab
            first_ref[start : start + slab] = pooled
            active[s * slab : (s + 1) * slab] = gelu(pooled.astype(F32)).astype(BF)
    down_ref[...] = nn(alow_ref[...], kernels_ref[1, 2]).astype(BF)
    up_ref[...] = nn(ahigh_ref[...], kernels_ref[1, 0]).astype(BF)


def coarse_body(
    scale, bins_per,
    ids_ref, prev_ref, low_ref, high_ref, next_ref, first_ref, kernels_ref, mixers_ref, readout_ref, targets_ref,
    gated_ref, second_ref, logit_ref, upper_ref, glow_ref, ghigh_ref,
):
    half = low_ref.shape[0]
    slab = half // 2
    slopes = []
    for h, came in enumerate((prev_ref, next_ref)):
        inner = (
            nn(low_ref[...], kernels_ref[1, 1 - h]) + nn(high_ref[...], kernels_ref[1, 2 - h])
            + came[...].astype(F32)
        )
        slopes.append(gelu_slope(inner))
        gated = gelu(inner).astype(BF)
        gated_ref[h * half : (h + 1) * half] = gated
        out = first_ref[h * half : (h + 1) * half].astype(F32) + nn(gated, mixers_ref[1])
        second_ref[h * slab : (h + 1) * slab] = ((out[:slab] + out[slab:]) * 0.5).astype(BF)
    bins = second_ref.shape[0]
    tracks = readout_ref.shape[1]
    width = min(512, tracks)
    bin_ids = ids_ref[0] * bins_per + lax.broadcasted_iota(jnp.int32, (bins, 1), 0)
    weight = jnp.where(bin_ids * 4 < ids_ref[1], scale, 0.0).astype(F32)
    second = second_ref[...]
    upper = jnp.zeros((bins, second.shape[1]), F32)
    for n in range(tracks // width):
        cols = slice(n * width, (n + 1) * width)
        readout = readout_ref[:, cols]
        logits = nn(second, readout)
        small = jnp.exp(-jnp.abs(logits))
        plus = jnp.maximum(logits, 0.0) + jnp.log1p(small)
        gate = jnp.where(logits >= 0.0, 1.0, small) / (1.0 + small)
        grad = (weight * (plus - targets_ref[:, cols].astype(F32)) * gate).astype(BF)
        logit_ref[:, cols] = grad
        upper = upper + nt(grad, readout)
    upper = (upper * 0.5).astype(BF)
    upper_ref[...] = upper
    back = nt(upper, mixers_ref[1])
    for h, out in enumerate((glow_ref, ghigh_ref)):
        piece = back[h * slab : (h + 1) * slab]
        for s in range(2):
            out[s * slab : (s + 1) * slab] = (piece * slopes[h][s * slab : (s + 1) * slab]).astype(BF)


def readout_body(ids_ref, second_ref, logit_ref, keep_ref, send_ref):
    width = keep_ref.shape[2]
    second = second_ref[...]
    for k in range(4):
        start = pl.multiple_of((ids_ref[0] ^ k) * width, width)
        out = send_ref if k & 1 else keep_ref
        out[k >> 1] = tn(second, logit_ref[:, pl.ds(start, width)]).astype(BF)


def store_blocks(ids_ref, pieces, keep_refs, send_ref):
    width = pieces[0].shape[1] // 4
    for d in range(4):
        block = jnp.concatenate([p[:, d * width : (d + 1) * width] for p in pieces], axis=1)
        far = (ids_ref[0] >> 1) ^ (d >> 1)

        for k in range(2):

            @pl.when(((ids_ref[0] & 1) == (d & 1)) & (far == k))
            def _(block=block, k=k):
                keep_refs[k][...] = block

        @pl.when((ids_ref[0] & 1) != (d & 1))
        def _(block=block, far=far):
            send_ref[far] = block


def mixer_piece(slab, gated, up, spread_ref, split_ref):
    mixed = 0.0
    for j in range(2):
        left = nn(gated, spread_ref[j]).astype(BF)
        right = nn(up, split_ref[j]).astype(BF)
        rows = []
        for s in range(up.shape[0] // slab):
            rows += [right[s * slab : (s + 1) * slab]] * 2
        mixed = mixed + tn(left, jnp.concatenate(rows, axis=0))
    return mixed.astype(BF)


def weight_body(
    slab, ids_ref, after_ref, low_ref, high_ref, gprev_ref, glow_ref, ghigh_ref, gnext_ref, gated_ref, up_ref,
    spread_ref, split_ref, *out_refs,
):
    grads = (gprev_ref, glow_ref, ghigh_ref, gnext_ref)
    pieces = []
    for t in range(3):
        pieces.append((tn(low_ref[...], grads[2 - t][...]) + tn(high_ref[...], grads[3 - t][...])).astype(BF))
    pieces.append(mixer_piece(slab, gated_ref[...], up_ref[...], spread_ref, split_ref))
    *keep_refs, send_ref = out_refs
    if len(keep_refs) == 1:
        keep_refs = [keep_refs[0].at[k] for k in range(2)]
    store_blocks(ids_ref, pieces, keep_refs, send_ref)


def fine_back_body(
    scale,
    after_ref, gprev_ref, glow_ref, ghigh_ref, gnext_ref, upper_ref, first_ref, kernels_ref, mixers_ref, inner_ref,
    trunk_ref, lower_ref, ilow_ref, ihigh_ref, lanes_ref,
):
    half = glow_ref.shape[0]
    slab = half // 2
    grads = (gprev_ref, glow_ref, ghigh_ref, gnext_ref)
    upper = upper_ref[...].astype(F32)
    for h, out in enumerate((ilow_ref, ihigh_ref)):
        back = (
            nt(grads[h + 2][...], kernels_ref[1, 0])
            + nt(grads[h + 1][...], kernels_ref[1, 1])
            + nt(grads[h][...], kernels_ref[1, 2])
        )
        slope = gelu_slope(first_ref[h * half : (h + 1) * half].astype(F32))
        base = upper[h * slab : (h + 1) * slab]
        total = jnp.concatenate([base, base], axis=0) + back * slope
        for t in range(lanes_ref.shape[0]):
            cols = slice(t * 128, (t + 1) * 128)
            for s in range(2):
                lanes_ref[t, pl.ds(s, slab, stride=2), :] = total[s * slab : (s + 1) * slab, cols] * scale
            trunk_ref[h * half : (h + 1) * half, cols] = lanes_ref[t]
        lower = (total * 0.5).astype(BF)
        lower_ref[h * half : (h + 1) * half] = lower
        inner = nt(lower, mixers_ref[0])
        spread_inner = jnp.concatenate([inner[:slab], inner[:slab], inner[slab:], inner[slab:]], axis=0)
        slope = gelu_slope(inner_ref[2 * h * half : 2 * (h + 1) * half])
        out[...] = (spread_inner * slope).astype(BF)


def output_body(parts_ref, kernels_ref, mixers_ref):
    total = parts_ref[0].astype(F32)
    for g in range(1, parts_ref.shape[0]):
        total = total + parts_ref[g].astype(F32)
    cut, per = kernels_ref.shape[3], mixers_ref.shape[1]
    for n in range(2):
        start = 4 * n * cut
        for t in range(3):
            kernels_ref[n, t] = total[:, start + t * cut : start + (t + 1) * cut]
        tail = total[:, start + 3 * cut : start + 4 * cut]
        mixers_ref[n] = jnp.concatenate([tail[:per], tail[per:]], axis=1)


def swap(value, axis, bit):
    size = lax.axis_size(axis)
    return lax.ppermute(value, axis, [(i, i ^ bit) for i in range(size)])


def halo(low, high):
    size = lax.axis_size("seq")
    up = [(i, i + 1) for i in range(size - 1)]
    return (
        lax.ppermute(high, "seq", up),
        lax.ppermute(low, "seq", [(j, i) for i, j in up]),
    )


def core_sum(keep, send):
    came = swap(send, "dp", 1)
    away = (keep[1].astype(F32) + came[1].astype(F32)).astype(BF)
    here = keep[0].astype(F32) + came[0].astype(F32)
    return here, away


def seq_parts(total):
    groups = lax.axis_size("seq")
    rows, columns = total.shape
    return lax.all_to_all(
        total.reshape(groups, rows // groups, columns), "seq", split_axis=0, concat_axis=0, tiled=True
    )


def side_rows(value, side):
    groups = lax.axis_size("seq")
    *blocks, rows, columns = value.shape
    value = value.reshape(*blocks, groups // 2, 2, rows // groups, columns)
    return lax.dynamic_index_in_dim(value, side, axis=len(blocks) + 1, keepdims=False).astype(F32)


def both_body(left_ref, left_came_ref, right_ref, right_came_ref, both_ref):
    columns = left_ref.shape[2]
    both_ref[:, :, :columns] = (left_ref[...] + left_came_ref[...].astype(F32)).astype(BF)
    both_ref[:, :, columns:] = (right_ref[...] + right_came_ref[...].astype(F32)).astype(BF)


def crossed_sums(left_keep, left_send, right_keep, right_send, first, first_came):
    groups = lax.axis_size("seq")
    side = lax.axis_index("seq") % 2
    right_came = swap(right_send, "dp", 1)
    left_came = swap(left_send, "dp", 1)
    left_away = (left_keep[1].astype(F32) + left_came[1].astype(F32)).astype(BF)
    left_away, first_came = lax.optimization_barrier((left_away, first_came))
    x_came = swap(left_away, "dp", 2)
    other = side_rows(right_keep, 1 - side) + side_rows(right_came, 1 - side)
    side_came = swap(other.astype(BF), "seq", 1)

    def left_half(at):
        return side_rows(left_keep[0], at) + side_rows(left_came[0], at) + side_rows(x_came, at)

    own = side_rows(right_keep, side) + side_rows(right_came, side) + side_came.astype(F32)
    left = swap(left_half(1 - side).astype(BF), "seq", 1)
    right = swap(own[1].astype(BF), "dp", 2)
    both, = call(
        both_body, (left_half(side), left, own[0], right), [((*left.shape[:2], 2 * left.shape[2]), BF)], 20
    )
    first = seq_parts((first + first_came.astype(F32)).astype(BF))
    both, first = lax.optimization_barrier((both, first))
    lines = [list(range(start, groups, 2)) for start in range(2)]
    parts = lax.all_to_all(both, "seq", split_axis=0, concat_axis=0, axis_index_groups=lines, tiled=True)
    return parts, first.astype(F32).sum(axis=0)


def shards(embeddings, layout, lengths, targets, projection, kernels, mixers, readout):
    groups = lax.axis_size("seq")
    windows = lax.axis_size("dp")
    me = lax.axis_index("dp")
    device = lax.axis_index("seq")
    rows = embeddings[0, 0]
    row_count = rows.shape[0]
    depth, channels = projection.shape
    width = kernels.shape[3]
    tracks = readout.shape[1]
    half, quarter, eighth = row_count // 2, row_count // 4, row_count // 8
    length = lengths[0]

    side = device % 2
    share = depth // 2
    piece = share // 2
    columns = channels // 2
    block = row_count // groups
    from_core = swap(projection, "dp", 1)
    mine = lax.dynamic_slice_in_dim(projection, side * share, share, axis=0)
    far = [
        [swap(mine[i * piece : (i + 1) * piece, n * columns : (n + 1) * columns], "dp", 2) for i in range(2)]
        for n in range(2)
    ]
    extra = lax.dynamic_slice(projection, ((1 - side) * share + piece, columns), (piece, columns))
    extra = swap(extra, "dp", 2)
    near, away = (me ^ 2) * depth, (me ^ 3) * depth
    later = []
    for i in range(2):
        at, side_at = side * share + i * piece, (1 - side) * share + i * piece
        later += [near + at, away + at, near + side_at, away + side_at]
    total, *blocks = product(rows, [projection, from_core], [me * depth, (me ^ 1) * depth], later, piece)
    weights = []
    for n in range(2):
        for i in range(2):
            held = far[n][i]
            if n == 0 and i == 0:
                held, total = lax.optimization_barrier((held, total))
            crossed = extra if n == 1 and i == 1 else swap(held, "seq", 1)
            weights.append([held, swap(held, "dp", 1), crossed, swap(crossed, "dp", 1)])

    def send(sums):
        return lax.all_to_all(
            sums.reshape(groups, block, columns), "seq", split_axis=0, concat_axis=0, tiled=True
        ).reshape(row_count, columns)

    left = absorb(total, 0, blocks, weights[0] + weights[1], 20)
    left, weights[3][3] = lax.optimization_barrier((left, weights[3][3]))
    left = send(left)
    right = absorb(total, columns, blocks, weights[2] + weights[3], 60)
    left, right = lax.optimization_barrier((left, right))
    right = send(right)

    column = lax.dynamic_index_in_dim(layout[0], device, axis=1, keepdims=True)
    position = column * block + jnp.arange(block, dtype=jnp.int32)[None, :]
    slot = (position // half) * half + (position % 4) * eighth + (position % half) // 4
    target = jnp.where(device * row_count + position < length, slot, -1).reshape(1, row_count)

    hidden, low, high, down, up = call(
        place_body, (target, left, right, kernels),
        [((row_count, channels), BF), ((half, channels), BF), ((half, channels), BF),
         ((half, width), BF), ((half, width), BF)],
        24,
    )
    fprev, fnext = halo(down, up)
    local, = call(local_body, (low, high, kernels), [((row_count, width), F32)], 24)
    inner, gated, first, alow, ahigh, adown, aup = call(
        fine_body, (fprev, fnext, local, hidden, kernels, mixers),
        [((row_count, width), F32), ((row_count, width), BF), ((half, channels), BF),
         ((quarter, channels), BF), ((quarter, channels), BF), ((quarter, width), BF), ((quarter, width), BF)],
        24,
    )
    aprev, anext = halo(adown, aup)
    bins = quarter
    loss = 2.0 / math.sqrt(windows * groups * bins)
    ids = jnp.stack([device, length]).astype(jnp.int32)
    place = jnp.stack([me, device]).astype(jnp.int32)

    def coarse(*refs):
        coarse_body(loss, bins, *refs)

    cgated, second, logit_grad, upper, glow, ghigh = call(
        coarse, (ids, aprev, alow, ahigh, anext, first, kernels, mixers, readout, targets[0]),
        [((half, width), BF), ((bins, channels), BF), ((bins, tracks), BF), ((bins, channels), BF),
         ((quarter, width), BF), ((quarter, width), BF)],
        32, smem=1,
    )
    gprev, gnext = halo(glow, ghigh)
    track_keep, track_send = call(
        readout_body, (place, second, logit_grad), [((2, channels, tracks // 4), BF)] * 2,
        24, smem=1,
    )
    track_here, track_away = core_sum(track_keep, track_send)
    track_away, gprev, gnext = lax.optimization_barrier((track_away, gprev, gnext))

    per = width // groups
    fold = np.zeros((2, width, channels), ml_dtypes.bfloat16)
    split = np.zeros((2, channels, width), ml_dtypes.bfloat16)
    for j in range(2):
        for a in range(width):
            fold[j, a, (a // per) * 2 * per + j * per + a % per] = 1
        piece_width = width // 4
        for b in range(width):
            split[j, (b // piece_width) * 2 * piece_width + j * piece_width + b % piece_width, b] = 1
    fold, split = jnp.asarray(fold), jnp.asarray(split)
    pair = [((2, channels, width), BF)] * 2
    parts = [((channels, width), BF)] * 2 + pair[:1]

    def fine_back(*refs):
        fine_back_body(math.sqrt(windows * groups * bins) * 0.5, *refs)

    def weights(*refs):
        weight_body(eighth, *refs)

    track_x = swap(track_away, "dp", 2)
    trunk, lower, ilow, ihigh = call(
        fine_back, (track_away, gprev, glow, ghigh, gnext, upper, first, kernels, mixers, inner),
        [((half, channels), F32), ((half, channels), BF), ((half, width), BF), ((half, width), BF)],
        32, after=1,
        scratch=[pltpu.VMEM((channels // 128, quarter, 128), F32)],
    )
    iprev, inext = halo(ilow, ihigh)
    coarse_keep, coarse_send = call(
        weights, (place, ilow, alow, ahigh, gprev, glow, ghigh, gnext, cgated, upper, fold, split), pair,
        32, smem=1, after=1,
    )
    iprev, inext, coarse_send = lax.optimization_barrier((iprev, inext, coarse_send))
    *fine_keep, fine_send = call(
        weights, (place, ilow, low, high, iprev, ilow, ihigh, inext, gated, lower, fold, split), parts,
        32, smem=1, after=1,
    )
    fine_send, track_x = lax.optimization_barrier((fine_send, track_x))
    both, readout_total = crossed_sums(fine_keep, fine_send, coarse_keep, coarse_send, track_here, track_x)
    cut = width // windows
    kernel_total, mixer_total = call(
        output_body, (both,),
        [((2, 3, channels // groups, cut), F32), ((2, per, 2 * cut), F32)], 16,
    )
    return (kernel_total, mixer_total, readout_total, trunk[None])


def solution(mesh):
    placed = (
        P("dp", "seq", None, None),
        P("dp", None, None),
        P("dp"),
        P("dp", "seq", None),
        P("dp", None),
        P(),
        P(),
        P(),
    )
    return jax.shard_map(
        shards,
        mesh=mesh,
        in_specs=placed,
        out_specs=(
            P(None, None, "seq", "dp"),
            P(None, "seq", "dp"),
            P("seq", "dp"),
            P("dp", "seq", None),
        ),
        check_vma=False,
    )
```

```python
import math

import jax
import jax.numpy as jnp
import ml_dtypes
import numpy as np
from jax import lax
from jax.experimental import pallas as pl
from jax.experimental.pallas import tpu as pltpu
from jax.sharding import PartitionSpec as P

SPREAD_FINE = 256
SPREAD_COARSE = 128
BF = jnp.bfloat16
F32 = jnp.float32

CHEAP = pl.CostEstimate(flops=1024, bytes_accessed=1024, transcendentals=0)
VMEM = pl.BlockSpec(memory_space=pltpu.VMEM)
SMEM = pl.BlockSpec(memory_space=pltpu.SMEM)
HBM = pl.BlockSpec(memory_space=pltpu.HBM)
ANY = pl.BlockSpec(memory_space=pl.ANY)


def params(mib):
    return pltpu.CompilerParams(vmem_limit_bytes=mib * 1024 * 1024)


def gelu(v):
    return 0.5 * v * (1.0 + lax.erf(v * (1.0 / math.sqrt(2.0))))


def gelu_slope(v):
    cumulative = 0.5 * (1.0 + lax.erf(v * (1.0 / math.sqrt(2.0))))
    density = jnp.exp(-0.5 * v * v) * (1.0 / math.sqrt(2.0 * math.pi))
    return cumulative + v * density


def nn(a, b):
    return jnp.dot(a, b, preferred_element_type=F32)


def nt(a, b):
    return lax.dot_general(a, b, (((1,), (1,)), ((), ())), preferred_element_type=F32)


def tn(a, b):
    return lax.dot_general(a, b, (((0,), (0,)), ((), ())), preferred_element_type=F32)


def call(body, inputs, outs, mib, smem=0, scratch=(), after=0):
    outs = [jax.ShapeDtypeStruct(s, d) for s, d in outs]
    return pl.pallas_call(
        body,
        out_shape=outs,
        in_specs=[SMEM] * smem + [ANY] * after + [VMEM] * (len(inputs) - smem - after),
        out_specs=[VMEM] * len(outs),
        scratch_shapes=list(scratch),
        compiler_params=params(mib),
        cost_estimate=CHEAP,
    )(*inputs)


def product(rows, weights, starts, later, block):
    count, spare = len(weights), len(later)
    row_count = rows.shape[0]
    depth, columns = weights[0].shape
    blocks = [(k, at) for k in range(count) for at in range(0, depth, block)]

    def body(starts_ref, rows_ref, *refs):
        weight_refs, out_refs, later_refs = refs[:count], refs[count : count + 2], refs[count + 2 : count + 2 + spare]
        held_ref, piece_ref, sems, later_sems = refs[count + 2 + spare :]
        copies = []
        for n, (k, at) in enumerate(blocks):
            start = pl.multiple_of(starts_ref[k] + at, block)
            copies.append((
                pltpu.make_async_copy(
                    rows_ref.at[:, pl.ds(start, block)], held_ref.at[:, pl.ds(n * block, block)], sems.at[0, n]
                ),
                pltpu.make_async_copy(
                    weight_refs[k].at[pl.ds(at, block)], piece_ref.at[pl.ds(n * block, block)], sems.at[1, n]
                ),
            ))
            for copy in copies[-1]:
                copy.start()
        rest = []
        for n in range(spare):
            start = pl.multiple_of(starts_ref[count + n], block)
            rest.append(
                pltpu.make_async_copy(rows_ref.at[:, pl.ds(start, block)], later_refs[n], later_sems.at[n])
            )
            rest[-1].start()
        half = row_count // 2
        for h in range(2):
            part = slice(h * half, (h + 1) * half)
            sums = 0.0
            for k in range(count):
                if h == 0:
                    for n in range(len(blocks)):
                        if blocks[n][0] == k:
                            for copy in copies[n]:
                                copy.wait()
                span = slice(k * depth, (k + 1) * depth)
                sums = sums + nn(held_ref[part, span], piece_ref[span])
            for n, out_ref in enumerate(out_refs):
                out_ref[part] = sums[:, n * columns // 2 : (n + 1) * columns // 2]
        for copy in rest:
            copy.wait()

    out = [jax.ShapeDtypeStruct((row_count, columns // 2), F32)] * 2
    out += [jax.ShapeDtypeStruct((row_count, block), BF)] * spare
    return pl.pallas_call(
        body,
        out_shape=out,
        in_specs=[SMEM] + [HBM] * (count + 1),
        out_specs=[VMEM] * (2 + spare),
        scratch_shapes=[
            pltpu.VMEM((row_count, count * depth), BF),
            pltpu.VMEM((count * depth, columns), BF),
            pltpu.SemaphoreType.DMA((2, len(blocks))),
            pltpu.SemaphoreType.DMA((spare,)),
        ],
        compiler_params=params(49),
        cost_estimate=CHEAP,
    )(jnp.stack(starts + later).astype(jnp.int32), rows, *weights)


def absorb(total, blocks, weights, mib):
    count = len(weights)
    row_count = total.shape[0]
    columns = weights[0].shape[1]

    def body(old_ref, *refs):
        out_ref = refs[2 * count]
        half = row_count // 2
        for h in range(2):
            part = slice(h * half, (h + 1) * half)
            sums = old_ref[part]
            for k in range(count):
                sums = sums + nn(refs[k][part], refs[count + k][...])
            out_ref[part] = sums.astype(BF)

    return call(
        body, (total, *blocks, *weights), [((row_count, columns), BF)], mib
    )[0]


def place_body(target_ref, left_ref, right_ref, kernels_ref, hidden_ref, low_ref, high_ref, down_ref, up_ref):
    half = low_ref.shape[0]
    row_count, columns = left_ref.shape
    for h, out in enumerate((low_ref, high_ref)):
        order = lax.broadcasted_iota(jnp.int32, (half, row_count), 0) + h * half
        pick = jnp.where(order == target_ref[...], 1.0, 0.0).astype(BF)
        for n, rows_ref in enumerate((left_ref, right_ref)):
            placed = nn(pick, rows_ref[...])
            cols = slice(n * columns, (n + 1) * columns)
            hidden_ref[h * half : (h + 1) * half, cols] = placed.astype(BF)
            out[:, cols] = gelu(placed).astype(BF)
    down_ref[...] = nn(low_ref[...], kernels_ref[0, 2]).astype(BF)
    up_ref[...] = nn(high_ref[...], kernels_ref[0, 0]).astype(BF)


def local_body(low_ref, high_ref, kernels_ref, inner_ref):
    half = low_ref.shape[0]
    low, high = low_ref[...], high_ref[...]
    inner_ref[:half] = nn(low, kernels_ref[0, 1]) + nn(high, kernels_ref[0, 2])
    inner_ref[half:] = nn(low, kernels_ref[0, 0]) + nn(high, kernels_ref[0, 1])


def fine_body(
    prev_ref, next_ref, local_ref, hidden_ref, kernels_ref, mixers_ref,
    inner_ref, gated_ref, first_ref, alow_ref, ahigh_ref, down_ref, up_ref,
):
    half = prev_ref.shape[0]
    slab = half // 4
    for h, (came, active) in enumerate(((prev_ref, alow_ref), (next_ref, ahigh_ref))):
        inner = local_ref[h * half : (h + 1) * half] + came[...].astype(F32)
        inner_ref[h * half : (h + 1) * half] = inner
        gated = gelu(inner).astype(BF)
        gated_ref[h * half : (h + 1) * half] = gated
        out = hidden_ref[h * half : (h + 1) * half].astype(F32) + nn(gated, mixers_ref[0])
        for s in range(2):
            a = out[2 * s * slab : (2 * s + 1) * slab]
            b = out[(2 * s + 1) * slab : (2 * s + 2) * slab]
            pooled = ((a + b) * 0.5).astype(BF)
            start = h * half // 2 + s * slab
            first_ref[start : start + slab] = pooled
            active[s * slab : (s + 1) * slab] = gelu(pooled.astype(F32)).astype(BF)
    down_ref[...] = nn(alow_ref[...], kernels_ref[1, 2]).astype(BF)
    up_ref[...] = nn(ahigh_ref[...], kernels_ref[1, 0]).astype(BF)


def coarse_body(
    scale, bins_per,
    ids_ref, prev_ref, low_ref, high_ref, next_ref, first_ref, kernels_ref, mixers_ref, readout_ref, targets_ref,
    gated_ref, second_ref, logit_ref, upper_ref, glow_ref, ghigh_ref,
):
    half = low_ref.shape[0]
    slab = half // 2
    slopes = []
    for h, came in enumerate((prev_ref, next_ref)):
        inner = (
            nn(low_ref[...], kernels_ref[1, 1 - h]) + nn(high_ref[...], kernels_ref[1, 2 - h])
            + came[...].astype(F32)
        )
        slopes.append(gelu_slope(inner))
        gated = gelu(inner).astype(BF)
        gated_ref[h * half : (h + 1) * half] = gated
        out = first_ref[h * half : (h + 1) * half].astype(F32) + nn(gated, mixers_ref[1])
        second_ref[h * slab : (h + 1) * slab] = ((out[:slab] + out[slab:]) * 0.5).astype(BF)
    bins = second_ref.shape[0]
    tracks = readout_ref.shape[1]
    width = min(512, tracks)
    bin_ids = ids_ref[0] * bins_per + lax.broadcasted_iota(jnp.int32, (bins, 1), 0)
    weight = jnp.where(bin_ids * 4 < ids_ref[1], scale, 0.0).astype(F32)
    second = second_ref[...]
    upper = jnp.zeros((bins, second.shape[1]), F32)
    for n in range(tracks // width):
        cols = slice(n * width, (n + 1) * width)
        readout = readout_ref[:, cols]
        logits = nn(second, readout)
        small = jnp.exp(-jnp.abs(logits))
        plus = jnp.maximum(logits, 0.0) + jnp.log1p(small)
        gate = jnp.where(logits >= 0.0, 1.0, small) / (1.0 + small)
        grad = (weight * (plus - targets_ref[:, cols].astype(F32)) * gate).astype(BF)
        logit_ref[:, cols] = grad
        upper = upper + nt(grad, readout)
    upper = (upper * 0.5).astype(BF)
    upper_ref[...] = upper
    back = nt(upper, mixers_ref[1])
    for h, out in enumerate((glow_ref, ghigh_ref)):
        piece = back[h * slab : (h + 1) * slab]
        for s in range(2):
            out[s * slab : (s + 1) * slab] = (piece * slopes[h][s * slab : (s + 1) * slab]).astype(BF)


def readout_body(ids_ref, second_ref, logit_ref, keep_ref, send_ref):
    width = keep_ref.shape[2]
    second = second_ref[...]
    for k in range(4):
        start = pl.multiple_of((ids_ref[0] ^ k) * width, width)
        out = send_ref if k & 1 else keep_ref
        out[k >> 1] = tn(second, logit_ref[:, pl.ds(start, width)]).astype(BF)


def store_blocks(ids_ref, pieces, keep_refs, send_ref):
    width = pieces[0].shape[1] // 4
    for d in range(4):
        block = jnp.concatenate([p[:, d * width : (d + 1) * width] for p in pieces], axis=1)
        far = (ids_ref[0] >> 1) ^ (d >> 1)

        for k in range(2):

            @pl.when(((ids_ref[0] & 1) == (d & 1)) & (far == k))
            def _(block=block, k=k):
                keep_refs[k][...] = block

        @pl.when((ids_ref[0] & 1) != (d & 1))
        def _(block=block, far=far):
            send_ref[far] = block


def mixer_piece(slab, gated, up, spread_ref, split_ref):
    mixed = 0.0
    for j in range(2):
        left = nn(gated, spread_ref[j]).astype(BF)
        right = nn(up, split_ref[j]).astype(BF)
        rows = []
        for s in range(up.shape[0] // slab):
            rows += [right[s * slab : (s + 1) * slab]] * 2
        mixed = mixed + tn(left, jnp.concatenate(rows, axis=0))
    return mixed.astype(BF)


def weight_body(
    slab, ids_ref, after_ref, low_ref, high_ref, gprev_ref, glow_ref, ghigh_ref, gnext_ref, gated_ref, up_ref,
    spread_ref, split_ref, *out_refs,
):
    grads = (gprev_ref, glow_ref, ghigh_ref, gnext_ref)
    pieces = []
    for t in range(3):
        pieces.append((tn(low_ref[...], grads[2 - t][...]) + tn(high_ref[...], grads[3 - t][...])).astype(BF))
    pieces.append(mixer_piece(slab, gated_ref[...], up_ref[...], spread_ref, split_ref))
    *keep_refs, send_ref = out_refs
    if len(keep_refs) == 1:
        keep_refs = [keep_refs[0].at[k] for k in range(2)]
    store_blocks(ids_ref, pieces, keep_refs, send_ref)


def fine_back_body(
    scale,
    after_ref, gprev_ref, glow_ref, ghigh_ref, gnext_ref, upper_ref, first_ref, kernels_ref, mixers_ref, inner_ref,
    trunk_ref, lower_ref, ilow_ref, ihigh_ref, lanes_ref,
):
    half = glow_ref.shape[0]
    slab = half // 2
    grads = (gprev_ref, glow_ref, ghigh_ref, gnext_ref)
    upper = upper_ref[...].astype(F32)
    for h, out in enumerate((ilow_ref, ihigh_ref)):
        back = (
            nt(grads[h + 2][...], kernels_ref[1, 0])
            + nt(grads[h + 1][...], kernels_ref[1, 1])
            + nt(grads[h][...], kernels_ref[1, 2])
        )
        slope = gelu_slope(first_ref[h * half : (h + 1) * half].astype(F32))
        base = upper[h * slab : (h + 1) * slab]
        total = jnp.concatenate([base, base], axis=0) + back * slope
        for t in range(lanes_ref.shape[0]):
            cols = slice(t * 128, (t + 1) * 128)
            for s in range(2):
                lanes_ref[t, pl.ds(s, slab, stride=2), :] = total[s * slab : (s + 1) * slab, cols] * scale
            trunk_ref[h * half : (h + 1) * half, cols] = lanes_ref[t]
        lower = (total * 0.5).astype(BF)
        lower_ref[h * half : (h + 1) * half] = lower
        inner = nt(lower, mixers_ref[0])
        spread_inner = jnp.concatenate([inner[:slab], inner[:slab], inner[slab:], inner[slab:]], axis=0)
        slope = gelu_slope(inner_ref[2 * h * half : 2 * (h + 1) * half])
        out[...] = (spread_inner * slope).astype(BF)


def output_body(parts_ref, kernels_ref, mixers_ref):
    total = parts_ref[0].astype(F32)
    for g in range(1, parts_ref.shape[0]):
        total = total + parts_ref[g].astype(F32)
    cut, per = kernels_ref.shape[3], mixers_ref.shape[1]
    for n in range(2):
        start = 4 * n * cut
        for t in range(3):
            kernels_ref[n, t] = total[:, start + t * cut : start + (t + 1) * cut]
        tail = total[:, start + 3 * cut : start + 4 * cut]
        mixers_ref[n] = jnp.concatenate([tail[:per], tail[per:]], axis=1)


def swap(value, axis, bit):
    size = lax.axis_size(axis)
    return lax.ppermute(value, axis, [(i, i ^ bit) for i in range(size)])


def halo(low, high):
    size = lax.axis_size("seq")
    up = [(i, i + 1) for i in range(size - 1)]
    return (
        lax.ppermute(high, "seq", up),
        lax.ppermute(low, "seq", [(j, i) for i, j in up]),
    )


def core_sum(keep, send):
    came = swap(send, "dp", 1)
    away = (keep[1].astype(F32) + came[1].astype(F32)).astype(BF)
    here = keep[0].astype(F32) + came[0].astype(F32)
    return here, away


def seq_parts(total):
    groups = lax.axis_size("seq")
    rows, columns = total.shape
    return lax.all_to_all(
        total.reshape(groups, rows // groups, columns), "seq", split_axis=0, concat_axis=0, tiled=True
    )


def side_rows(value, side):
    groups = lax.axis_size("seq")
    *blocks, rows, columns = value.shape
    value = value.reshape(*blocks, groups // 2, 2, rows // groups, columns)
    return lax.dynamic_index_in_dim(value, side, axis=len(blocks) + 1, keepdims=False).astype(F32)


def both_body(left_ref, left_came_ref, right_ref, right_came_ref, both_ref):
    columns = left_ref.shape[2]
    both_ref[:, :, :columns] = (left_ref[...] + left_came_ref[...].astype(F32)).astype(BF)
    both_ref[:, :, columns:] = (right_ref[...] + right_came_ref[...].astype(F32)).astype(BF)


def crossed_sums(left_keep, left_send, right_keep, right_send, first, first_came):
    groups = lax.axis_size("seq")
    side = lax.axis_index("seq") % 2
    right_came = swap(right_send, "dp", 1)
    left_came = swap(left_send, "dp", 1)
    left_away = (left_keep[1].astype(F32) + left_came[1].astype(F32)).astype(BF)
    left_away, first_came = lax.optimization_barrier((left_away, first_came))
    x_came = swap(left_away, "dp", 2)
    other = side_rows(right_keep, 1 - side) + side_rows(right_came, 1 - side)
    side_came = swap(other.astype(BF), "seq", 1)

    def left_half(at):
        return side_rows(left_keep[0], at) + side_rows(left_came[0], at) + side_rows(x_came, at)

    own = side_rows(right_keep, side) + side_rows(right_came, side) + side_came.astype(F32)
    left = swap(left_half(1 - side).astype(BF), "seq", 1)
    right = swap(own[1].astype(BF), "dp", 2)
    both, = call(
        both_body, (left_half(side), left, own[0], right), [((*left.shape[:2], 2 * left.shape[2]), BF)], 20
    )
    first = seq_parts((first + first_came.astype(F32)).astype(BF))
    both, first = lax.optimization_barrier((both, first))
    lines = [list(range(start, groups, 2)) for start in range(2)]
    parts = lax.all_to_all(both, "seq", split_axis=0, concat_axis=0, axis_index_groups=lines, tiled=True)
    return parts, first.astype(F32).sum(axis=0)


def shards(embeddings, layout, lengths, targets, projection, kernels, mixers, readout):
    groups = lax.axis_size("seq")
    windows = lax.axis_size("dp")
    me = lax.axis_index("dp")
    device = lax.axis_index("seq")
    rows = embeddings[0, 0]
    row_count = rows.shape[0]
    depth, channels = projection.shape
    width = kernels.shape[3]
    tracks = readout.shape[1]
    half, quarter, eighth = row_count // 2, row_count // 4, row_count // 8
    length = lengths[0]

    side = device % 2
    share = depth // 2
    piece = share // 2
    columns = channels // 2
    block = row_count // groups
    from_core = swap(projection, "dp", 1)
    mine = lax.dynamic_slice_in_dim(projection, side * share, share, axis=0)
    far = [
        [swap(mine[i * piece : (i + 1) * piece, n * columns : (n + 1) * columns], "dp", 2) for i in range(2)]
        for n in range(2)
    ]
    extra = lax.dynamic_slice(projection, ((1 - side) * share + piece, columns), (piece, columns))
    extra = swap(extra, "dp", 2)
    near, away = (me ^ 2) * depth, (me ^ 3) * depth
    later = []
    for i in range(2):
        at, side_at = side * share + i * piece, (1 - side) * share + i * piece
        later += [near + at, away + at, near + side_at, away + side_at]
    total, total_right, *blocks = product(rows, [projection, from_core], [me * depth, (me ^ 1) * depth], later, piece)
    weights = []
    for n in range(2):
        for i in range(2):
            held = far[n][i]
            if n == 0 and i == 0:
                held, total = lax.optimization_barrier((held, total))
            crossed = extra if n == 1 and i == 1 else swap(held, "seq", 1)
            weights.append([held, swap(held, "dp", 1), crossed, swap(crossed, "dp", 1)])

    def send(sums):
        return lax.all_to_all(
            sums.reshape(groups, block, columns), "seq", split_axis=0, concat_axis=0, tiled=True
        ).reshape(row_count, columns)

    left = absorb(total, blocks, weights[0] + weights[1], 20)
    left, weights[3][3] = lax.optimization_barrier((left, weights[3][3]))
    left = send(left)
    right = absorb(total_right, blocks, weights[2] + weights[3], 60)
    left, right = lax.optimization_barrier((left, right))
    right = send(right)

    column = lax.dynamic_index_in_dim(layout[0], device, axis=1, keepdims=True)
    position = column * block + jnp.arange(block, dtype=jnp.int32)[None, :]
    slot = (position // half) * half + (position % 4) * eighth + (position % half) // 4
    target = jnp.where(device * row_count + position < length, slot, -1).reshape(1, row_count)

    hidden, low, high, down, up = call(
        place_body, (target, left, right, kernels),
        [((row_count, channels), BF), ((half, channels), BF), ((half, channels), BF),
         ((half, width), BF), ((half, width), BF)],
        24,
    )
    fprev, fnext = halo(down, up)
    local, = call(local_body, (low, high, kernels), [((row_count, width), F32)], 24)
    inner, gated, first, alow, ahigh, adown, aup = call(
        fine_body, (fprev, fnext, local, hidden, kernels, mixers),
        [((row_count, width), F32), ((row_count, width), BF), ((half, channels), BF),
         ((quarter, channels), BF), ((quarter, channels), BF), ((quarter, width), BF), ((quarter, width), BF)],
        24,
    )
    aprev, anext = halo(adown, aup)
    bins = quarter
    loss = 2.0 / math.sqrt(windows * groups * bins)
    ids = jnp.stack([device, length]).astype(jnp.int32)
    place = jnp.stack([me, device]).astype(jnp.int32)

    def coarse(*refs):
        coarse_body(loss, bins, *refs)

    cgated, second, logit_grad, upper, glow, ghigh = call(
        coarse, (ids, aprev, alow, ahigh, anext, first, kernels, mixers, readout, targets[0]),
        [((half, width), BF), ((bins, channels), BF), ((bins, tracks), BF), ((bins, channels), BF),
         ((quarter, width), BF), ((quarter, width), BF)],
        32, smem=1,
    )
    gprev, gnext = halo(glow, ghigh)
    track_keep, track_send = call(
        readout_body, (place, second, logit_grad), [((2, channels, tracks // 4), BF)] * 2,
        24, smem=1,
    )
    track_here, track_away = core_sum(track_keep, track_send)
    track_away, gprev, gnext = lax.optimization_barrier((track_away, gprev, gnext))

    per = width // groups
    fold = np.zeros((2, width, channels), ml_dtypes.bfloat16)
    split = np.zeros((2, channels, width), ml_dtypes.bfloat16)
    for j in range(2):
        for a in range(width):
            fold[j, a, (a // per) * 2 * per + j * per + a % per] = 1
        piece_width = width // 4
        for b in range(width):
            split[j, (b // piece_width) * 2 * piece_width + j * piece_width + b % piece_width, b] = 1
    fold, split = jnp.asarray(fold), jnp.asarray(split)
    pair = [((2, channels, width), BF)] * 2
    parts = [((channels, width), BF)] * 2 + pair[:1]

    def fine_back(*refs):
        fine_back_body(math.sqrt(windows * groups * bins) * 0.5, *refs)

    def weights(*refs):
        weight_body(eighth, *refs)

    track_x = swap(track_away, "dp", 2)
    trunk, lower, ilow, ihigh = call(
        fine_back, (track_away, gprev, glow, ghigh, gnext, upper, first, kernels, mixers, inner),
        [((half, channels), F32), ((half, channels), BF), ((half, width), BF), ((half, width), BF)],
        32, after=1,
        scratch=[pltpu.VMEM((channels // 128, quarter, 128), F32)],
    )
    iprev, inext = halo(ilow, ihigh)
    coarse_keep, coarse_send = call(
        weights, (place, ilow, alow, ahigh, gprev, glow, ghigh, gnext, cgated, upper, fold, split), pair,
        32, smem=1, after=1,
    )
    iprev, inext, coarse_send = lax.optimization_barrier((iprev, inext, coarse_send))
    *fine_keep, fine_send = call(
        weights, (place, ilow, low, high, iprev, ilow, ihigh, inext, gated, lower, fold, split), parts,
        32, smem=1, after=1,
    )
    fine_send, track_x = lax.optimization_barrier((fine_send, track_x))
    both, readout_total = crossed_sums(fine_keep, fine_send, coarse_keep, coarse_send, track_here, track_x)
    cut = width // windows
    kernel_total, mixer_total = call(
        output_body, (both,),
        [((2, 3, channels // groups, cut), F32), ((2, per, 2 * cut), F32)], 16,
    )
    return (kernel_total, mixer_total, readout_total, trunk[None])


def solution(mesh):
    placed = (
        P("dp", "seq", None, None),
        P("dp", None, None),
        P("dp"),
        P("dp", "seq", None),
        P("dp", None),
        P(),
        P(),
        P(),
    )
    return jax.shard_map(
        shards,
        mesh=mesh,
        in_specs=placed,
        out_specs=(
            P(None, None, "seq", "dp"),
            P(None, "seq", "dp"),
            P("seq", "dp"),
            P("dp", "seq", None),
        ),
        check_vma=False,
    )
```
